32 devices in a mesh: feed: 16 (over z, y, x), tm: 2 (over core).
Axes of the slice: x: 2, y: 2, z: 4, core: 2. Of those that a mesh axis runs over, the one named last changes fastest.
Arguments:
- samples: bfloat16 [2048, 12288], P('feed', 'tm'), may hold values from -6 to 6
- filter_taps: float32 [4, 1024], replicated, may hold values from -3 to 3
- feed_cylinder: int32 [2048], replicated, may hold values from 0 to 3
- feed_delay: int32 [2048], replicated, may hold values from 0 to 4095
- pointing: int32 [512, 4], replicated, may hold values from 0 to 4095
- chirp_rate: float32 [512], P('feed'), may hold values from 1 to 40
Outputs:
- series: float32 [512, 12, 1024], P('feed', 'tm')
The draws below stay inside these ranges and needn't reach their ends.
All inputs are finite; a program needn't handle non-finite values.
Results may differ from the reference program's by a relative error of at most 0.0046.
Values may be sent and summed in bfloat16 or wider, within the bound.
No kernel may reach another device: no remote copies, remote signals or barrier semaphores. Data moves between devices by JAX's collectives and lax.ppermute only.
A program may use at most 64 MiB of HBM per device.

```python
import math
import jax
import jax.numpy as jnp
from jax import lax

FEEDS = 2048
NCHAN = 512
BEAMS = 512
TAPS = 4
CYL = 4
PHASES = 4096
FRAMES = 12


def place_ends(entries, rng, smallest, high):
    longest = entries.shape.index(max(entries.shape))
    spots = []
    for shift in (0, 1):
        where = [jax.random.randint(jax.random.fold_in(rng, axis), (), 0, length) for axis, length in enumerate(entries.shape)]
        where[longest] = (where[longest] + shift) % entries.shape[longest]
        spots.append(tuple(where))
    return entries.at[spots[0]].set(smallest).at[spots[1]].set(high)


def steps_of(own_key, shape, pieces, smallest, top_value):
    gain, own = 1.0, jax.random.fold_in(own_key, 6)
    for dim, blocks in pieces:
        heights = jnp.exp(jax.random.uniform(jax.random.fold_in(own, dim), (blocks,), jnp.float32, smallest / len(pieces), top_value / len(pieces)))
        gain = gain * jnp.repeat(heights, shape[dim] // blocks).reshape([-1 if axis == dim else 1 for axis in range(len(shape))])
    return gain


def noise(own_key, extent, deviation, reach, shards=(), kind=jnp.bfloat16):
    entries = jax.random.normal(own_key, extent, jnp.float32) * deviation
    if len(shards) > 0:
        entries = steps_of(own_key, extent, shards, -0.22, 0.18) * entries
    return jnp.clip(entries, min=-reach, max=reach).astype(kind)


def setup_inputs(seed: int = 0) -> dict:
    splits = jax.random.split(jax.random.key(seed), 7)
    samples = noise(splits[0], (FEEDS, FRAMES * 2 * NCHAN), 1.0, 6.0, ((0, 16), (1, 2)))
    filter_taps = noise(splits[1], (TAPS, 2 * NCHAN), 0.5, 3.0, (), jnp.float32)
    feed_cylinder = place_ends(jax.random.randint(splits[2], (FEEDS,), 0, CYL), jax.random.fold_in(splits[2], 1), 0, CYL - 1).astype(jnp.int32)
    feed_delay = place_ends(jax.random.randint(splits[3], (FEEDS,), 0, PHASES), jax.random.fold_in(splits[3], 1), 0, PHASES - 1).astype(jnp.int32)
    pointing = place_ends(jax.random.randint(splits[4], (BEAMS, CYL), 0, PHASES), jax.random.fold_in(splits[4], 1), 0, PHASES - 1).astype(jnp.int32)
    chirp_rate = jnp.clip(jnp.exp(math.log(40.0) - 3.6888795 * jax.random.uniform(splits[5], (BEAMS,), jnp.float32) ** steps_of(splits[5], (BEAMS,), ((0, 16),), -0.2, 0.2)), 1.0, 40.0)
    return {"samples": samples, "filter_taps": filter_taps, "feed_cylinder": feed_cylinder, "feed_delay": feed_delay, "pointing": pointing, "chirp_rate": chirp_rate}


def reference(samples, filter_taps, feed_cylinder, feed_delay, pointing, chirp_rate):
    length = 2 * NCHAN
    frames = samples.astype(jnp.float32).reshape(FEEDS, FRAMES, length)
    padded = jnp.concatenate([jnp.zeros((FEEDS, TAPS - 1, length), jnp.float32), frames], axis=1)
    filtered = jnp.zeros((FEEDS, FRAMES, length), jnp.float32)
    for tap_index in range(TAPS):
        filtered = filtered + filter_taps[tap_index] * padded[:, tap_index:tap_index + FRAMES, :]
    spectrum = jnp.fft.rfft(filtered, axis=-1)[..., :NCHAN]
    norm_forward = 1.0 / math.sqrt(length)
    spec_real = (jnp.real(spectrum) * norm_forward).astype(jnp.bfloat16)
    spec_imag = (jnp.imag(spectrum) * norm_forward).astype(jnp.bfloat16)
    chan_real = jnp.transpose(spec_real, (2, 1, 0)).reshape(NCHAN // 8, 8, FRAMES, FEEDS)
    chan_imag = jnp.transpose(spec_imag, (2, 1, 0)).reshape(NCHAN // 8, 8, FRAMES, FEEDS)
    steer = jnp.transpose(pointing[:, feed_cylinder])
    channel_ids = jnp.arange(NCHAN, dtype=jnp.int32).reshape(NCHAN // 8, 8)
    beam_scale = 1.0 / math.sqrt(FEEDS)

    def beam_block(inputs):
        local_real, local_imag, ids = inputs
        turns = (ids[:, None] + 1) * feed_delay[None, :] % PHASES
        phase = turns[:, :, None] * steer[None, :, :] % PHASES
        angle = phase.astype(jnp.float32) * (2.0 * math.pi / PHASES)
        w_real = jnp.cos(angle).astype(jnp.bfloat16).astype(jnp.float32)
        w_imag = jnp.sin(angle).astype(jnp.bfloat16).astype(jnp.float32)
        x_real = local_real.astype(jnp.float32)
        x_imag = local_imag.astype(jnp.float32)
        beam_real = jnp.einsum('cfj,cjb->cfb', x_real, w_real) - jnp.einsum('cfj,cjb->cfb', x_imag, w_imag)
        beam_imag = jnp.einsum('cfj,cjb->cfb', x_real, w_imag) + jnp.einsum('cfj,cjb->cfb', x_imag, w_real)
        return ((beam_real * beam_scale).astype(jnp.bfloat16), (beam_imag * beam_scale).astype(jnp.bfloat16))
    beams_real, beams_imag = lax.map(beam_block, (chan_real, chan_imag, channel_ids))
    beams_real = beams_real.reshape(NCHAN, FRAMES, BEAMS).astype(jnp.float32)
    beams_imag = beams_imag.reshape(NCHAN, FRAMES, BEAMS).astype(jnp.float32)
    position = jnp.arange(NCHAN).astype(jnp.float32) / NCHAN
    chirp = (jnp.pi * chirp_rate)[None, :] * (position * position)[:, None]
    chirp_cos = jnp.cos(chirp)[:, None, :]
    chirp_sin = jnp.sin(chirp)[:, None, :]
    chirped_real = beams_real * chirp_cos - beams_imag * chirp_sin
    chirped_imag = beams_real * chirp_sin + beams_imag * chirp_cos
    chirped = jnp.transpose(chirped_real + 1j * chirped_imag, (2, 1, 0))
    synthesized = jnp.fft.ifft(chirped, axis=-1) * math.sqrt(NCHAN)
    return jnp.concatenate([jnp.real(synthesized), jnp.imag(synthesized)], axis=-1).astype(jnp.float32)
```

```python
import functools
import math

import jax
import jax.numpy as jnp
import ml_dtypes
import numpy as np
from jax import lax
from jax.experimental import pallas as pl
from jax.experimental.pallas import tpu as pltpu
from jax.sharding import PartitionSpec as P

FEEDS = 2048
NCHAN = 512
BEAMS = 512
TAPS = 4
CYL = 4
PHASES = 4096


def from_behind(x, axis, by):
    length = lax.axis_size(axis)
    pairs = [(i, i + by) for i in range(length) if 0 <= i + by < length]
    return lax.ppermute(x, axis, pairs)


def forward_basis(length, nchan):
    sample_ids = jnp.arange(length, dtype=jnp.int32)[:, None]
    chan_ids = jnp.arange(nchan, dtype=jnp.int32)[None, :]
    angle = (sample_ids * chan_ids % length).astype(jnp.float32) * (2.0 * math.pi / length)
    scaled = 1.0 / math.sqrt(length)
    return jnp.concatenate([jnp.cos(angle), -jnp.sin(angle)], axis=1) * scaled


def inverse_basis(nchan):
    chan_ids = jnp.arange(nchan, dtype=jnp.int32)[:, None]
    time_ids = jnp.arange(nchan, dtype=jnp.int32)[None, :]
    angle = (chan_ids * time_ids % nchan).astype(jnp.float32) * (2.0 * math.pi / nchan)
    cosine = jnp.cos(angle)
    sine = jnp.sin(angle)
    upper = jnp.concatenate([cosine, sine], axis=1)
    lower = jnp.concatenate([-sine, cosine], axis=1)
    return jnp.concatenate([upper, lower], axis=0) * (1.0 / math.sqrt(nchan))


def spectra_of(frame_block, basis):
    feed_here, batch_frames, length = frame_block.shape
    flat = frame_block.reshape(feed_here * batch_frames, length)
    spectral = jnp.dot(
        flat, basis, precision=lax.Precision.HIGHEST, preferred_element_type=jnp.float32
    )
    spectral = spectral.reshape(feed_here, batch_frames, 2, length // 2)
    return jnp.transpose(spectral, (3, 2, 1, 0)).astype(jnp.bfloat16)


def beamform(turned, steer, feed_delay, first_channel):
    chan_here, _, batch_frames, feeds = turned.shape
    beam_scale = 1.0 / math.sqrt(feeds)

    def one_channel(inputs):
        local, offset = inputs
        channel = first_channel + offset
        turns = (channel + 1) * feed_delay % PHASES
        phase = turns[:, None] * steer % PHASES
        angle = phase.astype(jnp.float32) * (2.0 * math.pi / PHASES)
        w_real = jnp.cos(angle).astype(jnp.bfloat16)
        w_imag = jnp.sin(angle).astype(jnp.bfloat16)
        stacked = local.reshape(2 * batch_frames, feeds)
        with_real = jnp.dot(stacked, w_real, preferred_element_type=jnp.float32)
        with_imag = jnp.dot(stacked, w_imag, preferred_element_type=jnp.float32)
        beam_real = with_real[:batch_frames] - with_imag[batch_frames:]
        beam_imag = with_imag[:batch_frames] + with_real[batch_frames:]
        return (jnp.stack([beam_real, beam_imag]) * beam_scale).astype(jnp.bfloat16)

    offsets = jnp.arange(chan_here, dtype=jnp.int32)
    return lax.map(one_channel, (turned, offsets))


def synthesize(returned, chirp_cos, chirp_sin, basis):
    nchan, _, batch_frames, beams_here = returned.shape
    values = returned.astype(jnp.float32)
    beam_real = values[:, 0]
    beam_imag = values[:, 1]
    chirped_real = beam_real * chirp_cos - beam_imag * chirp_sin
    chirped_imag = beam_real * chirp_sin + beam_imag * chirp_cos
    stacked = jnp.stack([chirped_real, chirped_imag])
    ordered = jnp.transpose(stacked, (3, 2, 0, 1)).reshape(beams_here * batch_frames, 2 * nchan)
    result = jnp.dot(
        ordered, basis, precision=lax.Precision.HIGHEST, preferred_element_type=jnp.float32
    )
    return result.reshape(beams_here, batch_frames, 2 * nchan)


def plain_body(samples, filter_taps, feed_cylinder, feed_delay, pointing, chirp_rate):
    length = 2 * NCHAN
    feed_here = samples.shape[0]
    frames_here = samples.shape[1] // length
    frames = samples.reshape(feed_here, frames_here, length)
    tail = from_behind(frames[:, frames_here - (TAPS - 1) :, :], "tm", 1)
    padded = jnp.concatenate([tail, frames], axis=1).astype(jnp.float32)
    filtered = jnp.zeros((feed_here, frames_here, length), jnp.float32)
    for tap_index in range(TAPS):
        filtered = (
            filtered + filter_taps[tap_index] * padded[:, tap_index : tap_index + frames_here, :]
        )
    basis = forward_basis(length, NCHAN)
    steer = jnp.zeros((FEEDS, BEAMS), jnp.int32)
    for cylinder in range(CYL):
        steer = steer + jnp.where(
            feed_cylinder[:, None] == cylinder, pointing[None, :, cylinder], 0
        )
    chan_here = NCHAN // lax.axis_size("feed")
    first_channel = lax.axis_index("feed") * chan_here
    position = jnp.arange(NCHAN).astype(jnp.float32) / NCHAN
    chirp = (jnp.pi * chirp_rate)[None, :] * (position * position)[:, None]
    chirp_cos = jnp.cos(chirp)[:, None, :]
    chirp_sin = jnp.sin(chirp)[:, None, :]
    back_basis = inverse_basis(NCHAN)
    turned = lax.all_to_all(
        spectra_of(filtered, basis), "feed", split_axis=0, concat_axis=3, tiled=True
    )
    formed = beamform(turned, steer, feed_delay, first_channel)
    returned = lax.all_to_all(formed, "feed", split_axis=3, concat_axis=0, tiled=True)
    series = synthesize(returned, chirp_cos, chirp_sin, back_basis)
    return series


LANES = 128
HALVES = 2
GROUP = ("near", "tm")
VMEM = pltpu.CompilerParams(vmem_limit_bytes=56 * 1024 * 1024)


def split_bf16(table):
    high = table.astype(ml_dtypes.bfloat16)
    low = (table - high.astype(np.float64)).astype(ml_dtypes.bfloat16)
    return np.stack([high, low])


def folded_forward_basis(length):
    half = length // 2
    tables = []
    for parity in range(2):
        channel = 2 * np.arange(half // 2)[:, None] + parity
        angle = (channel * np.arange(half)[None, :] % length) * (2.0 * np.pi / length)
        rows = np.concatenate([np.cos(angle), -np.sin(angle)], axis=0) / math.sqrt(length)
        tables.append(split_bf16(rows))
    return np.stack(tables)


def folded_inverse_basis(nchan, lane_channels):
    kappas = nchan // 2 // lane_channels
    times = np.arange(nchan // 2)[None, :]
    tables = []
    for parity in range(2):
        rows = []
        for sub in range(lane_channels):
            channel = 2 * (lane_channels * np.arange(kappas)[:, None] + sub) + parity
            angle = (channel * times % nchan) * (2.0 * np.pi / nchan)
            rows.append(np.concatenate([np.cos(angle), np.sin(angle)], axis=1))
            rows.append(np.concatenate([-np.sin(angle), np.cos(angle)], axis=1))
        tables.append(split_bf16(np.concatenate(rows, axis=0) / math.sqrt(nchan)))
    return np.stack(tables)


def dot_nt(left, right):
    return lax.dot_general(
        left, right, (((1,), (1,)), ((), ())), preferred_element_type=jnp.float32
    )


def spectra_kernel(frames_here, samples_ref, tail_ref, taps_ref, basis_ref, out_ref, folded, rows):
    feed_here = samples_ref.shape[0]
    length = taps_ref.shape[1]
    half = length // 2

    def frame(index, start):
        lanes = pl.ds((index % frames_here) * length + start, LANES)
        if index < 0:
            lanes = pl.ds((index + TAPS - 1) * length + start, LANES)
            return tail_ref[:, lanes].astype(jnp.float32)
        return samples_ref[:, lanes].astype(jnp.float32)

    def filtered(index, start):
        total = None
        for tap in range(TAPS):
            term = taps_ref[tap : tap + 1, start : start + LANES] * frame(
                index + tap - (TAPS - 1), start
            )
            total = term if total is None else total + term
        return total

    for index in range(frames_here):
        where = pl.ds(index * feed_here, feed_here)
        for start in range(0, half, LANES):
            near = filtered(index, start)
            far = filtered(index, start + half)
            for parity, value in enumerate((near + far, near - far)):
                high = value.astype(jnp.bfloat16)
                folded[parity, 0, where, start : start + LANES] = high
                folded[parity, 1, where, start : start + LANES] = (
                    value - high.astype(jnp.float32)
                ).astype(jnp.bfloat16)

    per_channel = 2 * frames_here
    together = 2
    for parity in range(2):
        for first in range(0, frames_here, together):
            where = pl.ds(first * feed_here, together * feed_here)
            high = folded[parity, 0, where, :]
            low = folded[parity, 1, where, :]
            result = (
                dot_nt(basis_ref[parity, 0], high)
                + dot_nt(basis_ref[parity, 1], high)
                + dot_nt(basis_ref[parity, 0], low)
            )
            count = half // 2
            for part in range(2):
                for ahead in range(together):
                    start = parity * count * per_channel + part * frames_here + first + ahead
                    rows[pl.ds(start, count, stride=per_channel), :] = result[
                        part * count : (part + 1) * count,
                        ahead * feed_here : (ahead + 1) * feed_here,
                    ]
    out_ref[...] = rows[...].astype(jnp.bfloat16)


def spectra_rows(samples, tail, taps, basis):
    feed_here = samples.shape[0]
    length = taps.shape[1]
    frames_here = samples.shape[1] // length
    total_rows = length * frames_here
    return pl.pallas_call(
        functools.partial(spectra_kernel, frames_here),
        out_shape=jax.ShapeDtypeStruct((total_rows, feed_here), jnp.bfloat16),
        scratch_shapes=[
            pltpu.VMEM((2, 2, frames_here * feed_here, length // 2), jnp.bfloat16),
            pltpu.VMEM((total_rows, feed_here), jnp.float32),
        ],
        compiler_params=VMEM,
        name="spectra",
    )(samples, tail, taps, basis)


def sine_turns(turns):
    square = turns * turns
    total = None
    for power in range(11, 0, -2):
        factor = (2.0 * math.pi) ** power / math.factorial(power) * (-1) ** (power // 2)
        total = factor if total is None else total * square + factor
    return total * turns


def unit_vector(turns):
    cosine = sine_turns(0.25 - jnp.abs(turns))
    sine = sine_turns(jnp.maximum(jnp.minimum(turns, 0.5 - turns), -0.5 - turns))
    return cosine, sine


def centred(turns):
    return turns - jnp.floor(turns + 0.5)


def weights_kernel(block_rows, step, first_ref, delay_ref, cylinder_ref, pointing_ref, out_ref):
    channels, rows, width = out_ref.shape
    beams = width // 2
    repeat = beams // LANES
    middle = channels // 2
    first = (first_ref[0] + step * (middle - 1)).astype(jnp.float32)

    def one_block(index, carry):
        where = pl.ds(pl.multiple_of(index * block_rows, block_rows), block_rows)
        delay = jnp.concatenate([delay_ref[where]] * repeat, axis=1)
        cylinder = jnp.concatenate([cylinder_ref[where]] * repeat, axis=1)
        steer = jnp.broadcast_to(pointing_ref[0:1, :], (block_rows, beams))
        for other in range(1, CYL):
            steer = jnp.where(cylinder == other, pointing_ref[other : other + 1, :], steer)
        turns = centred(delay * steer * (1.0 / PHASES))
        low_cos, low_sin = unit_vector(centred(first * turns))
        step_cos, step_sin = unit_vector(centred(float(step) * turns))
        high_cos = low_cos * step_cos - low_sin * step_sin
        high_sin = low_cos * step_sin + low_sin * step_cos
        twice = step_cos + step_cos

        def put(channel, cosine, sine):
            out_ref[channel, where, :beams] = cosine.astype(jnp.bfloat16)
            out_ref[channel, where, beams:] = sine.astype(jnp.bfloat16)

        put(middle - 1, low_cos, low_sin)
        put(middle, high_cos, high_sin)
        up = (low_cos, low_sin, high_cos, high_sin)
        down = (high_cos, high_sin, low_cos, low_sin)
        for away in range(1, middle):
            up = (up[2], up[3], twice * up[2] - up[0], twice * up[3] - up[1])
            down = (down[2], down[3], twice * down[2] - down[0], twice * down[3] - down[1])
            put(middle + away, up[2], up[3])
            put(middle - 1 - away, down[2], down[3])
        return carry

    lax.fori_loop(0, rows // block_rows, one_block, 0)


def make_weights(first, delay, cylinder, pointing, channels, step):
    feeds = delay.shape[0]
    beams = pointing.shape[1]
    rows = 128
    return pl.pallas_call(
        functools.partial(weights_kernel, 32, step),
        grid=(feeds // rows,),
        in_specs=[
            pl.BlockSpec(memory_space=pltpu.SMEM),
            pl.BlockSpec((rows, LANES), lambda i: (i, 0)),
            pl.BlockSpec((rows, LANES), lambda i: (i, 0)),
            pl.BlockSpec(pointing.shape, lambda i: (0, 0)),
        ],
        out_specs=pl.BlockSpec((channels, rows, 2 * beams), lambda i: (0, i, 0)),
        out_shape=jax.ShapeDtypeStruct((channels, feeds, 2 * beams), jnp.bfloat16),
        compiler_params=VMEM,
        cost_estimate=pl.CostEstimate(
            flops=channels * feeds * beams * 8,
            bytes_accessed=channels * feeds * beams * 4,
            transcendentals=0,
        ),
        name="weights",
    )(first, delay, cylinder, pointing)


def beams_kernel(layout, received_ref, weights_ref, out_ref, wide, lined):
    near, cores, channels, frames_here = layout
    together = weights_ref.shape[0]
    beams = weights_ref.shape[2] // 2
    per_source = 2 * frames_here
    per_channel = per_source * cores
    feed_here = received_ref.shape[1]

    @pl.when(pl.program_id(0) == 0)
    def _():
        wide[...] = received_ref[...].astype(jnp.float32)
        for place in range(near):
            for core in range(cores):
                base = (place * cores + core) * channels * per_source
                for part in range(2):
                    for index in range(frames_here):
                        source = base + part * frames_here + index
                        target = (part * cores + core) * frames_here + index
                        lined[place, pl.ds(target, channels, stride=per_channel), :] = wide[
                            pl.ds(source, channels, stride=per_source), :
                        ]

    half = per_channel // 2
    for local in range(together):
        start = pl.multiple_of((pl.program_id(0) * together + local) * per_channel, 8)
        spectra = jnp.concatenate(
            [lined[place, pl.ds(start, per_channel), :] for place in range(near)], axis=1
        ).astype(jnp.bfloat16)
        both = jnp.dot(spectra, weights_ref[local], preferred_element_type=jnp.float32)
        by_real = both[:, :beams]
        by_imag = both[:, beams:]
        turned = jnp.concatenate([-by_imag[half:], by_imag[:half]], axis=0)
        out_ref[local * per_channel : (local + 1) * per_channel, :] = (by_real + turned).astype(
            out_ref.dtype
        )


def partial_beams(received, weights, layout, dtype):
    near, cores, channels, frames_here = layout
    feeds, width = weights.shape[1:]
    per_channel = 2 * cores * frames_here
    together = 4
    return pl.pallas_call(
        functools.partial(beams_kernel, layout),
        grid=(channels // together,),
        in_specs=[
            pl.BlockSpec(received.shape, lambda i: (0, 0)),
            pl.BlockSpec((together, feeds, width), lambda i: (i, 0, 0)),
        ],
        out_specs=pl.BlockSpec((together * per_channel, width // 2), lambda i: (i, 0)),
        out_shape=jax.ShapeDtypeStruct((channels * per_channel, width // 2), dtype),
        scratch_shapes=[
            pltpu.VMEM(received.shape, jnp.float32),
            pltpu.VMEM((near, channels * per_channel, feeds // near), jnp.float32),
        ],
        compiler_params=VMEM,
        cost_estimate=pl.CostEstimate(
            flops=channels * feeds * width * 2 * 128,
            bytes_accessed=weights.size * 2,
            transcendentals=0,
        ),
        name="beams",
    )(received, weights)


def gather_kernel(layout, beams_here, scale, own_ref, other_ref, out_ref, total, rows):
    near, cores, channels, frames_here = layout
    lane_channels = LANES // beams_here
    per_core = 2 * frames_here
    per_channel = per_core * cores
    groups = channels // lane_channels
    total[...] = (own_ref[...] + other_ref[...].astype(jnp.float32)) * scale
    for group in range(groups):
        values = [
            total[pl.ds((group * lane_channels + sub) * per_channel, per_channel), :]
            for sub in range(lane_channels)
        ]
        for place in range(near):
            lanes = slice(place * beams_here, (place + 1) * beams_here)
            tile = jnp.concatenate([value[:, lanes] for value in values], axis=1)
            for core in range(cores):
                start = ((place * cores + core) * groups + group) * per_core
                for part in range(2):
                    source = (part * cores + core) * frames_here
                    rows[pl.ds(start + part * frames_here, frames_here), :] = tile[
                        source : source + frames_here
                    ]
    out_ref[...] = rows[...].astype(jnp.bfloat16)


def gather_beams(own, other, layout, beams_here, scale):
    near, cores, channels, frames_here = layout
    total_rows = near * cores * channels // (LANES // beams_here) * 2 * frames_here
    return pl.pallas_call(
        functools.partial(gather_kernel, layout, beams_here, scale),
        out_shape=jax.ShapeDtypeStruct((total_rows, LANES), jnp.bfloat16),
        scratch_shapes=[
            pltpu.VMEM(own.shape, jnp.float32),
            pltpu.VMEM((total_rows, LANES), jnp.float32),
        ],
        compiler_params=VMEM,
        name="gather",
    )(own, other)


def series_kernel(beams_here, received_ref, cos_ref, sin_ref, basis_ref, out_ref, wide, lined):
    _, frames_here, _ = out_ref.shape
    kappas = cos_ref.shape[0]
    lane_channels = LANES // beams_here
    side = kappas // 2
    slot = 8
    wide[...] = received_ref[...].astype(jnp.float32)
    lined[...] = jnp.zeros_like(lined)
    for index in range(frames_here):
        real = wide[pl.ds(index, kappas, stride=2 * frames_here), :]
        imag = wide[pl.ds(frames_here + index, kappas, stride=2 * frames_here), :]
        chirped_real = real * cos_ref[...] - imag * sin_ref[...]
        chirped_imag = real * sin_ref[...] + imag * cos_ref[...]
        for parity in range(2):
            where = slice(parity * side, (parity + 1) * side)
            both = jnp.concatenate([chirped_real[where], chirped_imag[where]], axis=0)
            turned = both.T
            for sub in range(lane_channels):
                lined[parity, sub, pl.ds(index, beams_here, stride=slot), :] = turned[sub * beams_here : (sub + 1) * beams_here]
    sides = []
    for parity in range(2):
        value = jnp.concatenate([lined[parity, sub] for sub in range(lane_channels)], axis=1)
        high = value.astype(jnp.bfloat16)
        low = (value - high.astype(jnp.float32)).astype(jnp.bfloat16)
        sides.append(
            jnp.dot(high, basis_ref[parity, 0], preferred_element_type=jnp.float32)
            + jnp.dot(low, basis_ref[parity, 0], preferred_element_type=jnp.float32)
            + jnp.dot(high, basis_ref[parity, 1], preferred_element_type=jnp.float32)
        )
    times = sides[0].shape[1] // 2
    for part in range(2):
        even = sides[0][:, part * times : (part + 1) * times]
        odd = sides[1][:, part * times : (part + 1) * times]
        for which, value in enumerate((even + odd, even - odd)):
            start = (2 * part + which) * times
            out_ref[:, :, start : start + times] = value.reshape(beams_here, slot, times)[
                :, :frames_here, :
            ]


def make_series(received, chirp_cos, chirp_sin, basis, beams_here, frames_here):
    slot = 8
    lane_channels = LANES // beams_here
    return pl.pallas_call(
        functools.partial(series_kernel, beams_here),
        out_shape=jax.ShapeDtypeStruct(
            (beams_here, frames_here, 2 * basis.shape[3]), jnp.float32
        ),
        scratch_shapes=[
            pltpu.VMEM(received.shape, jnp.float32),
            pltpu.VMEM((2, lane_channels, beams_here * slot, LANES), jnp.float32),
        ],
        compiler_params=VMEM,
        name="series",
    )(received, chirp_cos, chirp_sin, basis)


def halves_body(samples, filter_taps, feed_cylinder, feed_delay, pointing, chirp_rate):
    length = filter_taps.shape[1]
    nchan = length // 2
    feed_here = samples.shape[0]
    frames_here = samples.shape[1] // length
    feeds = feed_delay.shape[0]
    beams = pointing.shape[0]
    beams_here = chirp_rate.shape[0]
    near = lax.axis_size("near")
    cores = lax.axis_size("tm")
    group = near * cores
    channels = nchan // group
    half_feeds = feeds // HALVES
    half_beams = beams // HALVES
    layout = (near, cores, channels, frames_here)
    half_index = lax.axis_index("half")
    place = lax.axis_index(GROUP)

    tail = from_behind(samples[:, (frames_here - (TAPS - 1)) * length :], "tm", 1)
    forward = jnp.asarray(folded_forward_basis(length))
    spectra = spectra_rows(samples, tail, filter_taps, forward)
    spectra = spectra.reshape(group, channels * 2 * frames_here, feed_here)
    received = lax.all_to_all(spectra, GROUP, 0, 0, tiled=True)
    received = received.reshape(-1, feed_here)

    in_parity = group // 2
    first = 2 * (place % in_parity) * channels + place // in_parity + 1
    first = jnp.reshape(first, (1,)).astype(jnp.int32)
    delay = lax.dynamic_slice_in_dim(feed_delay, half_index * half_feeds, half_feeds)
    delay = jnp.broadcast_to(delay.astype(jnp.float32)[:, None], (half_feeds, LANES))
    cylinder = lax.dynamic_slice_in_dim(feed_cylinder, half_index * half_feeds, half_feeds)
    cylinder = jnp.broadcast_to(cylinder[:, None], (half_feeds, LANES))
    aim = jnp.transpose(pointing).astype(jnp.float32)
    own_aim = lax.dynamic_slice_in_dim(aim, half_index * half_beams, half_beams, 1)
    other_aim = lax.dynamic_slice_in_dim(aim, (1 - half_index) * half_beams, half_beams, 1)

    other_weights = make_weights(first, delay, cylinder, other_aim, channels, 2)
    to_send = partial_beams(received, other_weights, layout, jnp.bfloat16)
    swap = [(i, HALVES - 1 - i) for i in range(HALVES)]
    arrived = lax.ppermute(to_send, "half", swap)
    own_aim, _ = lax.optimization_barrier((own_aim, to_send))
    own_weights = make_weights(first, delay, cylinder, own_aim, channels, 2)
    own = partial_beams(received, own_weights, layout, jnp.float32)
    gathered = gather_beams(own, arrived, layout, beams_here, 1.0 / math.sqrt(feeds))
    lane_channels = LANES // beams_here
    gathered = gathered.reshape(group, -1, LANES)
    returned = lax.all_to_all(gathered, GROUP, 0, 0, tiled=True).reshape(-1, LANES)

    kappa = jnp.arange(nchan // lane_channels, dtype=jnp.int32)[:, None]
    sub = jnp.arange(LANES, dtype=jnp.int32)[None, :] // beams_here
    side = nchan // lane_channels // 2
    channel = 2 * (lane_channels * (kappa % side) + sub) + kappa // side
    position = channel.astype(jnp.float32) / nchan
    rate = jnp.tile(jnp.pi * chirp_rate, lane_channels)[None, :]
    chirp = rate * (position * position)
    inverse = jnp.asarray(folded_inverse_basis(nchan, lane_channels))
    return make_series(
        returned, jnp.cos(chirp), jnp.sin(chirp), inverse, beams_here, frames_here
    )


def solution(mesh):
    feed_size = mesh.shape["feed"]
    wide_enough = FEEDS // feed_size % LANES == 0 and BEAMS // feed_size * 4 == LANES
    if not wide_enough:
        return jax.shard_map(
            plain_body,
            mesh=mesh,
            in_specs=(P("feed", "tm"), P(), P(), P(), P(), P("feed")),
            out_specs=P("feed", "tm", None),
            check_vma=False,
        )
    devices = mesh.devices.reshape(HALVES, feed_size // HALVES, mesh.shape["tm"])
    halved = jax.sharding.Mesh(devices, ("half", "near", "tm"))
    feed = ("half", "near")
    return jax.shard_map(
        halves_body,
        mesh=halved,
        in_specs=(P(feed, "tm"), P(), P(), P(), P(), P(feed)),
        out_specs=P(feed, "tm", None),
        check_vma=False,
    )
```

```python
import functools
import math

import jax
import jax.numpy as jnp
import ml_dtypes
import numpy as np
from jax import lax
from jax.experimental import pallas as pl
from jax.experimental.pallas import tpu as pltpu
from jax.sharding import PartitionSpec as P

FEEDS = 2048
NCHAN = 512
BEAMS = 512
TAPS = 4
CYL = 4
PHASES = 4096


def from_behind(x, axis, by):
    length = lax.axis_size(axis)
    pairs = [(i, i + by) for i in range(length) if 0 <= i + by < length]
    return lax.ppermute(x, axis, pairs)


def forward_basis(length, nchan):
    sample_ids = jnp.arange(length, dtype=jnp.int32)[:, None]
    chan_ids = jnp.arange(nchan, dtype=jnp.int32)[None, :]
    angle = (sample_ids * chan_ids % length).astype(jnp.float32) * (2.0 * math.pi / length)
    scaled = 1.0 / math.sqrt(length)
    return jnp.concatenate([jnp.cos(angle), -jnp.sin(angle)], axis=1) * scaled


def inverse_basis(nchan):
    chan_ids = jnp.arange(nchan, dtype=jnp.int32)[:, None]
    time_ids = jnp.arange(nchan, dtype=jnp.int32)[None, :]
    angle = (chan_ids * time_ids % nchan).astype(jnp.float32) * (2.0 * math.pi / nchan)
    cosine = jnp.cos(angle)
    sine = jnp.sin(angle)
    upper = jnp.concatenate([cosine, sine], axis=1)
    lower = jnp.concatenate([-sine, cosine], axis=1)
    return jnp.concatenate([upper, lower], axis=0) * (1.0 / math.sqrt(nchan))


def spectra_of(frame_block, basis):
    feed_here, batch_frames, length = frame_block.shape
    flat = frame_block.reshape(feed_here * batch_frames, length)
    spectral = jnp.dot(
        flat, basis, precision=lax.Precision.HIGHEST, preferred_element_type=jnp.float32
    )
    spectral = spectral.reshape(feed_here, batch_frames, 2, length // 2)
    return jnp.transpose(spectral, (3, 2, 1, 0)).astype(jnp.bfloat16)


def beamform(turned, steer, feed_delay, first_channel):
    chan_here, _, batch_frames, feeds = turned.shape
    beam_scale = 1.0 / math.sqrt(feeds)

    def one_channel(inputs):
        local, offset = inputs
        channel = first_channel + offset
        turns = (channel + 1) * feed_delay % PHASES
        phase = turns[:, None] * steer % PHASES
        angle = phase.astype(jnp.float32) * (2.0 * math.pi / PHASES)
        w_real = jnp.cos(angle).astype(jnp.bfloat16)
        w_imag = jnp.sin(angle).astype(jnp.bfloat16)
        stacked = local.reshape(2 * batch_frames, feeds)
        with_real = jnp.dot(stacked, w_real, preferred_element_type=jnp.float32)
        with_imag = jnp.dot(stacked, w_imag, preferred_element_type=jnp.float32)
        beam_real = with_real[:batch_frames] - with_imag[batch_frames:]
        beam_imag = with_imag[:batch_frames] + with_real[batch_frames:]
        return (jnp.stack([beam_real, beam_imag]) * beam_scale).astype(jnp.bfloat16)

    offsets = jnp.arange(chan_here, dtype=jnp.int32)
    return lax.map(one_channel, (turned, offsets))


def synthesize(returned, chirp_cos, chirp_sin, basis):
    nchan, _, batch_frames, beams_here = returned.shape
    values = returned.astype(jnp.float32)
    beam_real = values[:, 0]
    beam_imag = values[:, 1]
    chirped_real = beam_real * chirp_cos - beam_imag * chirp_sin
    chirped_imag = beam_real * chirp_sin + beam_imag * chirp_cos
    stacked = jnp.stack([chirped_real, chirped_imag])
    ordered = jnp.transpose(stacked, (3, 2, 0, 1)).reshape(beams_here * batch_frames, 2 * nchan)
    result = jnp.dot(
        ordered, basis, precision=lax.Precision.HIGHEST, preferred_element_type=jnp.float32
    )
    return result.reshape(beams_here, batch_frames, 2 * nchan)


def plain_body(samples, filter_taps, feed_cylinder, feed_delay, pointing, chirp_rate):
    length = 2 * NCHAN
    feed_here = samples.shape[0]
    frames_here = samples.shape[1] // length
    frames = samples.reshape(feed_here, frames_here, length)
    tail = from_behind(frames[:, frames_here - (TAPS - 1) :, :], "tm", 1)
    padded = jnp.concatenate([tail, frames], axis=1).astype(jnp.float32)
    filtered = jnp.zeros((feed_here, frames_here, length), jnp.float32)
    for tap_index in range(TAPS):
        filtered = (
            filtered + filter_taps[tap_index] * padded[:, tap_index : tap_index + frames_here, :]
        )
    basis = forward_basis(length, NCHAN)
    steer = jnp.zeros((FEEDS, BEAMS), jnp.int32)
    for cylinder in range(CYL):
        steer = steer + jnp.where(
            feed_cylinder[:, None] == cylinder, pointing[None, :, cylinder], 0
        )
    chan_here = NCHAN // lax.axis_size("feed")
    first_channel = lax.axis_index("feed") * chan_here
    position = jnp.arange(NCHAN).astype(jnp.float32) / NCHAN
    chirp = (jnp.pi * chirp_rate)[None, :] * (position * position)[:, None]
    chirp_cos = jnp.cos(chirp)[:, None, :]
    chirp_sin = jnp.sin(chirp)[:, None, :]
    back_basis = inverse_basis(NCHAN)
    turned = lax.all_to_all(
        spectra_of(filtered, basis), "feed", split_axis=0, concat_axis=3, tiled=True
    )
    formed = beamform(turned, steer, feed_delay, first_channel)
    returned = lax.all_to_all(formed, "feed", split_axis=3, concat_axis=0, tiled=True)
    series = synthesize(returned, chirp_cos, chirp_sin, back_basis)
    return series


LANES = 128
HALVES = 2
GROUP = ("near", "tm")
VMEM = pltpu.CompilerParams(vmem_limit_bytes=56 * 1024 * 1024)


def split_bf16(table):
    high = table.astype(ml_dtypes.bfloat16)
    low = (table - high.astype(np.float64)).astype(ml_dtypes.bfloat16)
    return np.stack([high, low])


def folded_forward_basis(length):
    half = length // 2
    tables = []
    for parity in range(2):
        channel = 2 * np.arange(half // 2)[:, None] + parity
        angle = (channel * np.arange(half)[None, :] % length) * (2.0 * np.pi / length)
        rows = np.concatenate([np.cos(angle), -np.sin(angle)], axis=0) / math.sqrt(length)
        tables.append(split_bf16(rows))
    return np.stack(tables)


def folded_inverse_basis(nchan, lane_channels):
    kappas = nchan // 2 // lane_channels
    times = np.arange(nchan // 2)[None, :]
    tables = []
    for parity in range(2):
        rows = []
        for sub in range(lane_channels):
            channel = 2 * (lane_channels * np.arange(kappas)[:, None] + sub) + parity
            angle = (channel * times % nchan) * (2.0 * np.pi / nchan)
            rows.append(np.concatenate([np.cos(angle), np.sin(angle)], axis=1))
            rows.append(np.concatenate([-np.sin(angle), np.cos(angle)], axis=1))
        tables.append(split_bf16(np.concatenate(rows, axis=0) / math.sqrt(nchan)))
    return np.stack(tables)


def dot_nt(left, right):
    return lax.dot_general(
        left, right, (((1,), (1,)), ((), ())), preferred_element_type=jnp.float32
    )


def spectra_kernel(frames_here, samples_ref, tail_ref, taps_ref, basis_ref, out_ref, folded, rows):
    feed_here = samples_ref.shape[0]
    length = taps_ref.shape[1]
    half = length // 2

    def frame(index, start):
        lanes = pl.ds((index % frames_here) * length + start, LANES)
        if index < 0:
            lanes = pl.ds((index + TAPS - 1) * length + start, LANES)
            return tail_ref[:, lanes].astype(jnp.float32)
        return samples_ref[:, lanes].astype(jnp.float32)

    def filtered(index, start):
        total = None
        for tap in range(TAPS):
            term = taps_ref[tap : tap + 1, start : start + LANES] * frame(
                index + tap - (TAPS - 1), start
            )
            total = term if total is None else total + term
        return total

    for index in range(frames_here):
        where = pl.ds(index * feed_here, feed_here)
        for start in range(0, half, LANES):
            near = filtered(index, start)
            far = filtered(index, start + half)
            for parity, value in enumerate((near + far, near - far)):
                high = value.astype(jnp.bfloat16)
                folded[parity, 0, where, start : start + LANES] = high
                folded[parity, 1, where, start : start + LANES] = (
                    value - high.astype(jnp.float32)
                ).astype(jnp.bfloat16)

    per_channel = 2 * frames_here
    together = 2
    for parity in range(2):
        for first in range(0, frames_here, together):
            where = pl.ds(first * feed_here, together * feed_here)
            high = folded[parity, 0, where, :]
            low = folded[parity, 1, where, :]
            result = (
                dot_nt(basis_ref[parity, 0], high)
                + dot_nt(basis_ref[parity, 1], high)
                + dot_nt(basis_ref[parity, 0], low)
            )
            count = half // 2
            for part in range(2):
                for ahead in range(together):
                    start = parity * count * per_channel + part * frames_here + first + ahead
                    rows[pl.ds(start, count, stride=per_channel), :] = result[
                        part * count : (part + 1) * count,
                        ahead * feed_here : (ahead + 1) * feed_here,
                    ]
    out_ref[...] = rows[...].astype(jnp.bfloat16)


def spectra_rows(samples, tail, taps, basis):
    feed_here = samples.shape[0]
    length = taps.shape[1]
    frames_here = samples.shape[1] // length
    total_rows = length * frames_here
    return pl.pallas_call(
        functools.partial(spectra_kernel, frames_here),
        out_shape=jax.ShapeDtypeStruct((total_rows, feed_here), jnp.bfloat16),
        scratch_shapes=[
            pltpu.VMEM((2, 2, frames_here * feed_here, length // 2), jnp.bfloat16),
            pltpu.VMEM((total_rows, feed_here), jnp.float32),
        ],
        compiler_params=VMEM,
        name="spectra",
    )(samples, tail, taps, basis)


def sine_turns(turns):
    square = turns * turns
    total = None
    for power in range(11, 0, -2):
        factor = (2.0 * math.pi) ** power / math.factorial(power) * (-1) ** (power // 2)
        total = factor if total is None else total * square + factor
    return total * turns


def unit_vector(turns):
    cosine = sine_turns(0.25 - jnp.abs(turns))
    sine = sine_turns(jnp.maximum(jnp.minimum(turns, 0.5 - turns), -0.5 - turns))
    return cosine, sine


def centred(turns):
    return turns - jnp.floor(turns + 0.5)


def chain_start(first, channels, step):
    return (first + step * (channels // 2 - 1)).astype(jnp.float32)


def chain_of_weights(first, step, delay, cylinder, pointing_ref, out_ref, where):
    channels, _, width = out_ref.shape
    beams = width // 2
    repeat = beams // LANES
    middle = channels // 2
    delay = jnp.concatenate([delay] * repeat, axis=1)
    cylinder = jnp.concatenate([cylinder] * repeat, axis=1)
    steer = jnp.broadcast_to(pointing_ref[0:1, :], delay.shape)
    for other in range(1, CYL):
        steer = jnp.where(cylinder == other, pointing_ref[other : other + 1, :], steer)
    turns = centred(delay * steer * (1.0 / PHASES))
    low_cos, low_sin = unit_vector(centred(first * turns))
    step_cos, step_sin = unit_vector(centred(float(step) * turns))
    high_cos = low_cos * step_cos - low_sin * step_sin
    high_sin = low_cos * step_sin + low_sin * step_cos
    twice = step_cos + step_cos

    def put(channel, cosine, sine):
        out_ref[channel, where, :beams] = cosine.astype(jnp.bfloat16)
        out_ref[channel, where, beams:] = sine.astype(jnp.bfloat16)

    put(middle - 1, low_cos, low_sin)
    put(middle, high_cos, high_sin)
    up = (low_cos, low_sin, high_cos, high_sin)
    down = (high_cos, high_sin, low_cos, low_sin)
    for away in range(1, middle):
        up = (up[2], up[3], twice * up[2] - up[0], twice * up[3] - up[1])
        down = (down[2], down[3], twice * down[2] - down[0], twice * down[3] - down[1])
        put(middle + away, up[2], up[3])
        put(middle - 1 - away, down[2], down[3])


def weights_kernel(block_rows, step, first_ref, delay_ref, cylinder_ref, pointing_ref, out_ref):
    channels, rows, _ = out_ref.shape
    first = chain_start(first_ref[0], channels, step)

    def one_block(index, carry):
        where = pl.ds(pl.multiple_of(index * block_rows, block_rows), block_rows)
        chain_of_weights(
            first, step, delay_ref[where], cylinder_ref[where], pointing_ref, out_ref, where
        )
        return carry

    lax.fori_loop(0, rows // block_rows, one_block, 0)


def make_weights(first, delay, cylinder, pointing, channels, step):
    feeds = delay.shape[0]
    beams = pointing.shape[1]
    rows = 128
    return pl.pallas_call(
        functools.partial(weights_kernel, 32, step),
        grid=(feeds // rows,),
        in_specs=[
            pl.BlockSpec(memory_space=pltpu.SMEM),
            pl.BlockSpec((rows, LANES), lambda i: (i, 0)),
            pl.BlockSpec((rows, LANES), lambda i: (i, 0)),
            pl.BlockSpec(pointing.shape, lambda i: (0, 0)),
        ],
        out_specs=pl.BlockSpec((channels, rows, 2 * beams), lambda i: (0, i, 0)),
        out_shape=jax.ShapeDtypeStruct((channels, feeds, 2 * beams), jnp.bfloat16),
        compiler_params=VMEM,
        cost_estimate=pl.CostEstimate(
            flops=channels * feeds * beams * 8,
            bytes_accessed=channels * feeds * beams * 4,
            transcendentals=0,
        ),
        name="weights",
    )(first, delay, cylinder, pointing)


def padded_rows(rows):
    return -(-rows // 16) * 16


def turn_products(both):
    beams = both.shape[1] // 2
    half = both.shape[0] // 2
    by_imag = both[:, beams:]
    return both[:, :beams] + jnp.concatenate([-by_imag[half:], by_imag[:half]], axis=0)


def beams_kernel(layout, received_ref, weights_ref, out_ref, lined_ref, wide, lined):
    near, cores, channels, frames_here = layout
    together = weights_ref.shape[0]
    per_source = 2 * frames_here
    per_channel = per_source * cores
    feed_here = received_ref.shape[1]
    spare = lined_ref.shape[1] - per_channel

    @pl.when(pl.program_id(0) == 0)
    def _():
        wide[...] = received_ref[...].astype(jnp.float32)
        for place in range(near):
            for core in range(cores):
                base = (place * cores + core) * channels * per_source
                for part in range(2):
                    for index in range(frames_here):
                        source = base + part * frames_here + index
                        target = (part * cores + core) * frames_here + index
                        lined[place, pl.ds(target, channels, stride=per_channel), :] = wide[
                            pl.ds(source, channels, stride=per_source), :
                        ]

    for local in range(together):
        start = pl.multiple_of((pl.program_id(0) * together + local) * per_channel, 8)
        spectra = [
            jnp.concatenate(
                [
                    lined[place, pl.ds(start, per_channel), :],
                    jnp.zeros((spare, feed_here), jnp.float32),
                ],
                axis=0,
            )
            for place in range(near)
        ]
        spectra = jnp.concatenate(spectra, axis=1).astype(jnp.bfloat16)
        lined_ref[local] = spectra
        both = jnp.dot(spectra, weights_ref[local], preferred_element_type=jnp.float32)
        out_ref[local * per_channel : (local + 1) * per_channel, :] = turn_products(
            both[:per_channel]
        ).astype(out_ref.dtype)


def partial_beams(received, weights, layout, dtype):
    near, cores, channels, frames_here = layout
    feeds, width = weights.shape[1:]
    per_channel = 2 * cores * frames_here
    padded = padded_rows(per_channel)
    together = 8
    return pl.pallas_call(
        functools.partial(beams_kernel, layout),
        grid=(channels // together,),
        in_specs=[
            pl.BlockSpec(received.shape, lambda i: (0, 0)),
            pl.BlockSpec((together, feeds, width), lambda i: (i, 0, 0)),
        ],
        out_specs=[
            pl.BlockSpec((together * per_channel, width // 2), lambda i: (i, 0)),
            pl.BlockSpec((together, padded, feeds), lambda i: (i, 0, 0)),
        ],
        out_shape=[
            jax.ShapeDtypeStruct((channels * per_channel, width // 2), dtype),
            jax.ShapeDtypeStruct((channels, padded, feeds), jnp.bfloat16),
        ],
        scratch_shapes=[
            pltpu.VMEM(received.shape, jnp.float32),
            pltpu.VMEM((near, channels * per_channel, feeds // near), jnp.float32),
        ],
        compiler_params=VMEM,
        cost_estimate=pl.CostEstimate(
            flops=channels * feeds * width * 2 * 128,
            bytes_accessed=weights.size * 2,
            transcendentals=0,
        ),
        name="beams",
    )(received, weights)


def own_beams_kernel(
    per_channel, step, first_ref, lined_ref, delay_ref, cylinder_ref, pointing_ref, out_ref, total, weights
):
    channels, _, feeds = lined_ref.shape
    _, rows, width = weights.shape
    block_rows = 32
    together = 4
    first = chain_start(first_ref[0], channels, step)
    for start in range(0, feeds, rows):

        def one_block(index, carry):
            target = pl.ds(pl.multiple_of(index * block_rows, block_rows), block_rows)
            source = pl.ds(pl.multiple_of(start + index * block_rows, block_rows), block_rows)
            chain_of_weights(
                first, step, delay_ref[source], cylinder_ref[source], pointing_ref, weights, target
            )
            return carry

        lax.fori_loop(0, rows // block_rows, one_block, 0)

        def some_channels(index, carry):
            ids = [index * together + local for local in range(together)]
            places = [pl.ds(pl.multiple_of(i * per_channel, 8), per_channel) for i in ids]
            olds = [total[place, :] if start else None for place in places]
            news = [
                jnp.dot(
                    lined_ref[i, :, start : start + rows],
                    weights[i],
                    preferred_element_type=jnp.float32,
                )[:per_channel]
                for i in ids
            ]
            for place, old, new in zip(places, olds, news):
                value = new if old is None else old + new
                if start + rows < feeds:
                    total[place, :] = value
                else:
                    out_ref[place, :] = turn_products(value)
            return carry

        lax.fori_loop(0, channels // together, some_channels, 0)


def own_beams(first, lined, delay, cylinder, pointing, per_channel, step):
    channels, _, feeds = lined.shape
    beams = pointing.shape[1]
    rows = 256
    in_vmem = pl.BlockSpec(memory_space=pltpu.VMEM)
    return pl.pallas_call(
        functools.partial(own_beams_kernel, per_channel, step),
        in_specs=[pl.BlockSpec(memory_space=pltpu.SMEM)] + [in_vmem] * 4,
        out_specs=in_vmem,
        out_shape=jax.ShapeDtypeStruct((channels * per_channel, beams), jnp.float32),
        scratch_shapes=[
            pltpu.VMEM((channels * per_channel, 2 * beams), jnp.float32),
            pltpu.VMEM((channels, rows, 2 * beams), jnp.bfloat16),
        ],
        compiler_params=VMEM,
        cost_estimate=pl.CostEstimate(
            flops=channels * feeds * beams * 4 * 128,
            bytes_accessed=channels * feeds * beams * 4,
            transcendentals=0,
        ),
        name="own_beams",
    )(first, lined, delay, cylinder, pointing)


def gather_kernel(layout, beams_here, scale, own_ref, other_ref, out_ref, total, rows):
    near, cores, channels, frames_here = layout
    lane_channels = LANES // beams_here
    per_core = 2 * frames_here
    per_channel = per_core * cores
    groups = channels // lane_channels
    total[...] = (own_ref[...] + other_ref[...].astype(jnp.float32)) * scale
    for group in range(groups):
        values = [
            total[pl.ds((group * lane_channels + sub) * per_channel, per_channel), :]
            for sub in range(lane_channels)
        ]
        for place in range(near):
            lanes = slice(place * beams_here, (place + 1) * beams_here)
            tile = jnp.concatenate([value[:, lanes] for value in values], axis=1)
            for core in range(cores):
                start = ((place * cores + core) * groups + group) * per_core
                for part in range(2):
                    source = (part * cores + core) * frames_here
                    rows[pl.ds(start + part * frames_here, frames_here), :] = tile[
                        source : source + frames_here
                    ]
    out_ref[...] = rows[...].astype(jnp.bfloat16)


def gather_beams(own, other, layout, beams_here, scale):
    near, cores, channels, frames_here = layout
    total_rows = near * cores * channels // (LANES // beams_here) * 2 * frames_here
    return pl.pallas_call(
        functools.partial(gather_kernel, layout, beams_here, scale),
        out_shape=jax.ShapeDtypeStruct((total_rows, LANES), jnp.bfloat16),
        scratch_shapes=[
            pltpu.VMEM(own.shape, jnp.float32),
            pltpu.VMEM((total_rows, LANES), jnp.float32),
        ],
        compiler_params=VMEM,
        name="gather",
    )(own, other)


def series_kernel(beams_here, received_ref, cos_ref, sin_ref, basis_ref, out_ref, wide, lined):
    frames_here = out_ref.shape[0]
    kappas = cos_ref.shape[0]
    lane_channels = LANES // beams_here
    side = kappas // 2
    wide[...] = received_ref[...].astype(jnp.float32)
    for index in range(frames_here):
        real = wide[pl.ds(index, kappas, stride=2 * frames_here), :]
        imag = wide[pl.ds(frames_here + index, kappas, stride=2 * frames_here), :]
        chirped_real = real * cos_ref[...] - imag * sin_ref[...]
        chirped_imag = real * sin_ref[...] + imag * cos_ref[...]
        target = slice(index * beams_here, (index + 1) * beams_here)
        for parity in range(2):
            where = slice(parity * side, (parity + 1) * side)
            both = jnp.concatenate([chirped_real[where], chirped_imag[where]], axis=0)
            turned = both.T
            high = turned.astype(jnp.bfloat16)
            low = (turned - high.astype(jnp.float32)).astype(jnp.bfloat16)
            for sub in range(lane_channels):
                source = slice(sub * beams_here, (sub + 1) * beams_here)
                lanes = slice(sub * 2 * side, (sub + 1) * 2 * side)
                lined[parity, 0, target, lanes] = high[source]
                lined[parity, 1, target, lanes] = low[source]
    sides = []
    for parity in range(2):
        high = lined[parity, 0]
        low = lined[parity, 1]
        sides.append(
            jnp.dot(high, basis_ref[parity, 0], preferred_element_type=jnp.float32)
            + jnp.dot(low, basis_ref[parity, 0], preferred_element_type=jnp.float32)
            + jnp.dot(high, basis_ref[parity, 1], preferred_element_type=jnp.float32)
        )
    times = sides[0].shape[1] // 2
    for part in range(2):
        even = sides[0][:, part * times : (part + 1) * times]
        odd = sides[1][:, part * times : (part + 1) * times]
        for which, value in enumerate((even + odd, even - odd)):
            start = (2 * part + which) * times
            out_ref[:, :, start : start + times] = value.reshape(frames_here, beams_here, times)


def make_series(received, chirp_cos, chirp_sin, basis, beams_here, frames_here):
    series = pl.pallas_call(
        functools.partial(series_kernel, beams_here),
        out_shape=jax.ShapeDtypeStruct(
            (frames_here, beams_here, 2 * basis.shape[3]), jnp.float32
        ),
        scratch_shapes=[
            pltpu.VMEM(received.shape, jnp.float32),
            pltpu.VMEM((2, 2, frames_here * beams_here, basis.shape[2]), jnp.bfloat16),
        ],
        compiler_params=VMEM,
        name="series",
    )(received, chirp_cos, chirp_sin, basis)
    return jnp.transpose(series, (1, 0, 2))


def halves_body(samples, filter_taps, feed_cylinder, feed_delay, pointing, chirp_rate):
    length = filter_taps.shape[1]
    nchan = length // 2
    feed_here = samples.shape[0]
    frames_here = samples.shape[1] // length
    feeds = feed_delay.shape[0]
    beams = pointing.shape[0]
    beams_here = chirp_rate.shape[0]
    near = lax.axis_size("near")
    cores = lax.axis_size("tm")
    group = near * cores
    channels = nchan // group
    half_feeds = feeds // HALVES
    half_beams = beams // HALVES
    layout = (near, cores, channels, frames_here)
    half_index = lax.axis_index("half")
    place = lax.axis_index(GROUP)

    tail = from_behind(samples[:, (frames_here - (TAPS - 1)) * length :], "tm", 1)
    forward = jnp.asarray(folded_forward_basis(length))
    spectra = spectra_rows(samples, tail, filter_taps, forward)
    spectra = spectra.reshape(group, channels * 2 * frames_here, feed_here)
    received = lax.all_to_all(spectra, GROUP, 0, 0, tiled=True)
    received = received.reshape(-1, feed_here)

    in_parity = group // 2
    first = 2 * (place % in_parity) * channels + place // in_parity + 1
    first = jnp.reshape(first, (1,)).astype(jnp.int32)
    delay = lax.dynamic_slice_in_dim(feed_delay, half_index * half_feeds, half_feeds)
    delay = jnp.broadcast_to(delay.astype(jnp.float32)[:, None], (half_feeds, LANES))
    cylinder = lax.dynamic_slice_in_dim(feed_cylinder, half_index * half_feeds, half_feeds)
    cylinder = jnp.broadcast_to(cylinder[:, None], (half_feeds, LANES))
    aim = jnp.transpose(pointing).astype(jnp.float32)
    own_aim = lax.dynamic_slice_in_dim(aim, half_index * half_beams, half_beams, 1)
    other_aim = lax.dynamic_slice_in_dim(aim, (1 - half_index) * half_beams, half_beams, 1)

    other_weights = make_weights(first, delay, cylinder, other_aim, channels, 2)
    to_send, lined = partial_beams(received, other_weights, layout, jnp.bfloat16)
    swap = [(i, HALVES - 1 - i) for i in range(HALVES)]
    arrived = lax.ppermute(to_send, "half", swap)
    own = own_beams(first, lined, delay, cylinder, own_aim, 2 * cores * frames_here, 2)
    gathered = gather_beams(own, arrived, layout, beams_here, 1.0 / math.sqrt(feeds))
    lane_channels = LANES // beams_here
    gathered = gathered.reshape(group, -1, LANES)
    returned = lax.all_to_all(gathered, GROUP, 0, 0, tiled=True).reshape(-1, LANES)

    kappa = jnp.arange(nchan // lane_channels, dtype=jnp.int32)[:, None]
    sub = jnp.arange(LANES, dtype=jnp.int32)[None, :] // beams_here
    side = nchan // lane_channels // 2
    channel = 2 * (lane_channels * (kappa % side) + sub) + kappa // side
    position = channel.astype(jnp.float32) / nchan
    rate = jnp.tile(jnp.pi * chirp_rate, lane_channels)[None, :]
    chirp = rate * (position * position)
    inverse = jnp.asarray(folded_inverse_basis(nchan, lane_channels))
    return make_series(
        returned, jnp.cos(chirp), jnp.sin(chirp), inverse, beams_here, frames_here
    )


def solution(mesh):
    feed_size = mesh.shape["feed"]
    wide_enough = FEEDS // feed_size % LANES == 0 and BEAMS // feed_size * 4 == LANES
    if not wide_enough:
        return jax.shard_map(
            plain_body,
            mesh=mesh,
            in_specs=(P("feed", "tm"), P(), P(), P(), P(), P("feed")),
            out_specs=P("feed", "tm", None),
            check_vma=False,
        )
    devices = mesh.devices.reshape(HALVES, feed_size // HALVES, mesh.shape["tm"])
    halved = jax.sharding.Mesh(devices, ("half", "near", "tm"))
    feed = ("half", "near")
    return jax.shard_map(
        halves_body,
        mesh=halved,
        in_specs=(P(feed, "tm"), P(), P(), P(), P(), P(feed)),
        out_specs=P(feed, "tm", None),
        check_vma=False,
    )
```

```python
import functools
import math

import jax
import jax.numpy as jnp
import ml_dtypes
import numpy as np
from jax import lax
from jax.experimental import pallas as pl
from jax.experimental.pallas import tpu as pltpu
from jax.sharding import PartitionSpec as P

FEEDS = 2048
NCHAN = 512
BEAMS = 512
TAPS = 4
CYL = 4
PHASES = 4096


def from_behind(x, axis, by):
    length = lax.axis_size(axis)
    pairs = [(i, i + by) for i in range(length) if 0 <= i + by < length]
    return lax.ppermute(x, axis, pairs)


def forward_basis(length, nchan):
    sample_ids = jnp.arange(length, dtype=jnp.int32)[:, None]
    chan_ids = jnp.arange(nchan, dtype=jnp.int32)[None, :]
    angle = (sample_ids * chan_ids % length).astype(jnp.float32) * (2.0 * math.pi / length)
    scaled = 1.0 / math.sqrt(length)
    return jnp.concatenate([jnp.cos(angle), -jnp.sin(angle)], axis=1) * scaled


def inverse_basis(nchan):
    chan_ids = jnp.arange(nchan, dtype=jnp.int32)[:, None]
    time_ids = jnp.arange(nchan, dtype=jnp.int32)[None, :]
    angle = (chan_ids * time_ids % nchan).astype(jnp.float32) * (2.0 * math.pi / nchan)
    cosine = jnp.cos(angle)
    sine = jnp.sin(angle)
    upper = jnp.concatenate([cosine, sine], axis=1)
    lower = jnp.concatenate([-sine, cosine], axis=1)
    return jnp.concatenate([upper, lower], axis=0) * (1.0 / math.sqrt(nchan))


def spectra_of(frame_block, basis):
    feed_here, batch_frames, length = frame_block.shape
    flat = frame_block.reshape(feed_here * batch_frames, length)
    spectral = jnp.dot(
        flat, basis, precision=lax.Precision.HIGHEST, preferred_element_type=jnp.float32
    )
    spectral = spectral.reshape(feed_here, batch_frames, 2, length // 2)
    return jnp.transpose(spectral, (3, 2, 1, 0)).astype(jnp.bfloat16)


def beamform(turned, steer, feed_delay, first_channel):
    chan_here, _, batch_frames, feeds = turned.shape
    beam_scale = 1.0 / math.sqrt(feeds)

    def one_channel(inputs):
        local, offset = inputs
        channel = first_channel + offset
        turns = (channel + 1) * feed_delay % PHASES
        phase = turns[:, None] * steer % PHASES
        angle = phase.astype(jnp.float32) * (2.0 * math.pi / PHASES)
        w_real = jnp.cos(angle).astype(jnp.bfloat16)
        w_imag = jnp.sin(angle).astype(jnp.bfloat16)
        stacked = local.reshape(2 * batch_frames, feeds)
        with_real = jnp.dot(stacked, w_real, preferred_element_type=jnp.float32)
        with_imag = jnp.dot(stacked, w_imag, preferred_element_type=jnp.float32)
        beam_real = with_real[:batch_frames] - with_imag[batch_frames:]
        beam_imag = with_imag[:batch_frames] + with_real[batch_frames:]
        return (jnp.stack([beam_real, beam_imag]) * beam_scale).astype(jnp.bfloat16)

    offsets = jnp.arange(chan_here, dtype=jnp.int32)
    return lax.map(one_channel, (turned, offsets))


def synthesize(returned, chirp_cos, chirp_sin, basis):
    nchan, _, batch_frames, beams_here = returned.shape
    values = returned.astype(jnp.float32)
    beam_real = values[:, 0]
    beam_imag = values[:, 1]
    chirped_real = beam_real * chirp_cos - beam_imag * chirp_sin
    chirped_imag = beam_real * chirp_sin + beam_imag * chirp_cos
    stacked = jnp.stack([chirped_real, chirped_imag])
    ordered = jnp.transpose(stacked, (3, 2, 0, 1)).reshape(beams_here * batch_frames, 2 * nchan)
    result = jnp.dot(
        ordered, basis, precision=lax.Precision.HIGHEST, preferred_element_type=jnp.float32
    )
    return result.reshape(beams_here, batch_frames, 2 * nchan)


def plain_body(samples, filter_taps, feed_cylinder, feed_delay, pointing, chirp_rate):
    length = 2 * NCHAN
    feed_here = samples.shape[0]
    frames_here = samples.shape[1] // length
    frames = samples.reshape(feed_here, frames_here, length)
    tail = from_behind(frames[:, frames_here - (TAPS - 1) :, :], "tm", 1)
    padded = jnp.concatenate([tail, frames], axis=1).astype(jnp.float32)
    filtered = jnp.zeros((feed_here, frames_here, length), jnp.float32)
    for tap_index in range(TAPS):
        filtered = (
            filtered + filter_taps[tap_index] * padded[:, tap_index : tap_index + frames_here, :]
        )
    basis = forward_basis(length, NCHAN)
    steer = jnp.zeros((FEEDS, BEAMS), jnp.int32)
    for cylinder in range(CYL):
        steer = steer + jnp.where(
            feed_cylinder[:, None] == cylinder, pointing[None, :, cylinder], 0
        )
    chan_here = NCHAN // lax.axis_size("feed")
    first_channel = lax.axis_index("feed") * chan_here
    position = jnp.arange(NCHAN).astype(jnp.float32) / NCHAN
    chirp = (jnp.pi * chirp_rate)[None, :] * (position * position)[:, None]
    chirp_cos = jnp.cos(chirp)[:, None, :]
    chirp_sin = jnp.sin(chirp)[:, None, :]
    back_basis = inverse_basis(NCHAN)
    turned = lax.all_to_all(
        spectra_of(filtered, basis), "feed", split_axis=0, concat_axis=3, tiled=True
    )
    formed = beamform(turned, steer, feed_delay, first_channel)
    returned = lax.all_to_all(formed, "feed", split_axis=3, concat_axis=0, tiled=True)
    series = synthesize(returned, chirp_cos, chirp_sin, back_basis)
    return series


LANES = 128
PHASE_BITS = PHASES.bit_length() - 1
HALVES = 2
GROUP = ("near", "tm")
VMEM = pltpu.CompilerParams(vmem_limit_bytes=56 * 1024 * 1024)


def split_bf16(table):
    high = table.astype(ml_dtypes.bfloat16)
    low = (table - high.astype(np.float64)).astype(ml_dtypes.bfloat16)
    return np.stack([high, low])


def folded_forward_basis(length):
    half = length // 2
    tables = []
    for parity in range(2):
        channel = 2 * np.arange(half // 2)[:, None] + parity
        angle = (channel * np.arange(half)[None, :] % length) * (2.0 * np.pi / length)
        rows = np.concatenate([np.cos(angle), -np.sin(angle)], axis=0) / math.sqrt(length)
        tables.append(split_bf16(rows))
    return np.stack(tables)


def folded_inverse_basis(nchan, lane_channels):
    kappas = nchan // 2 // lane_channels
    times = np.arange(nchan // 2)[None, :]
    tables = []
    for parity in range(2):
        rows = []
        for sub in range(lane_channels):
            channel = 2 * (lane_channels * np.arange(kappas)[:, None] + sub) + parity
            angle = (channel * times % nchan) * (2.0 * np.pi / nchan)
            rows.append(np.concatenate([np.cos(angle), np.sin(angle)], axis=1))
            rows.append(np.concatenate([-np.sin(angle), np.cos(angle)], axis=1))
        tables.append(split_bf16(np.concatenate(rows, axis=0) / math.sqrt(nchan)))
    return np.stack(tables)


def dot_nt(left, right):
    return lax.dot_general(
        left, right, (((1,), (1,)), ((), ())), preferred_element_type=jnp.float32
    )


def spectra_kernel(
    frames_here, half_ref, samples_ref, tail_ref, taps_in_ref, basis_ref, out_ref,
    samples, tail, taps_ref, basis, folded, rows, packed, in_sems, out_sems,
):
    feed_here = samples_ref.shape[0]
    length = taps_ref.shape[1]
    half = length // 2
    before = TAPS - 1
    side = half_ref[0]
    sign = (1 - 2 * side).astype(jnp.float32)
    fetch_samples = pltpu.make_async_copy(samples_ref, samples, in_sems.at[0])
    fetch_tail = pltpu.make_async_copy(tail_ref, tail, in_sems.at[1])
    fetch_taps = pltpu.make_async_copy(taps_in_ref, taps_ref, in_sems.at[4])
    fetch_basis = [
        pltpu.make_async_copy(
            basis_ref.at[parity + side * (1 - 2 * parity)], basis.at[parity], in_sems.at[2 + parity]
        )
        for parity in range(2)
    ]
    fetches = [fetch_taps, fetch_samples, fetch_tail] + fetch_basis
    for fetch in fetches:
        fetch.start()
    fetch_taps.wait()
    fetch_samples.wait()

    def frame(index, start):
        if index < 0:
            lanes = pl.ds((index + before) * length + start, LANES)
            return tail[:, lanes].astype(jnp.float32)
        return samples[:, pl.ds(index * length + start, LANES)].astype(jnp.float32)

    def filtered(index, start):
        total = None
        for tap in range(TAPS):
            term = taps_ref[tap : tap + 1, start : start + LANES] * frame(
                index + tap - before, start
            )
            total = term if total is None else total + term
        return total

    for index in list(range(before, frames_here)) + list(range(before)):
        if index == 0:
            fetch_tail.wait()
        where = pl.ds(index * feed_here, feed_here)
        for start in range(0, half, LANES):
            near = filtered(index, start)
            far = filtered(index, start + half) * sign
            for parity, value in enumerate((near + far, near - far)):
                high = value.astype(jnp.bfloat16)
                folded[parity, 0, where, start : start + LANES] = high
                folded[parity, 1, where, start : start + LANES] = (
                    value - high.astype(jnp.float32)
                ).astype(jnp.bfloat16)

    per_channel = 2 * frames_here
    together = 2
    count = half // 2
    stores = []
    for parity in range(2):
        fetch_basis[parity].wait()
        for first in range(0, frames_here, together):
            where = pl.ds(first * feed_here, together * feed_here)
            high = folded[parity, 0, where, :]
            low = folded[parity, 1, where, :]
            result = (
                dot_nt(basis[parity, 0], high)
                + dot_nt(basis[parity, 1], high)
                + dot_nt(basis[parity, 0], low)
            )
            for part in range(2):
                for ahead in range(together):
                    start = parity * count * per_channel + part * frames_here + first + ahead
                    rows[pl.ds(start, count, stride=per_channel), :] = result[
                        part * count : (part + 1) * count,
                        ahead * feed_here : (ahead + 1) * feed_here,
                    ]
        block = pl.ds(parity * count * per_channel, count * per_channel)
        packed[block, :] = rows[block, :].astype(jnp.bfloat16)
        store = pltpu.make_async_copy(packed.at[block], out_ref.at[block], out_sems.at[parity])
        store.start()
        stores.append(store)
    for store in stores:
        store.wait()


def spectra_rows(half_index, samples, tail, taps, basis):
    feed_here = samples.shape[0]
    length = taps.shape[1]
    frames_here = samples.shape[1] // length
    total_rows = length * frames_here
    anywhere = pl.BlockSpec(memory_space=pl.ANY)
    in_hbm = pl.BlockSpec(memory_space=pltpu.HBM)
    return pl.pallas_call(
        functools.partial(spectra_kernel, frames_here),
        in_specs=[pl.BlockSpec(memory_space=pltpu.SMEM), in_hbm, anywhere, in_hbm, in_hbm],
        out_specs=anywhere,
        out_shape=jax.ShapeDtypeStruct((total_rows, feed_here), jnp.bfloat16),
        scratch_shapes=[
            pltpu.VMEM(samples.shape, samples.dtype),
            pltpu.VMEM(tail.shape, tail.dtype),
            pltpu.VMEM(taps.shape, taps.dtype),
            pltpu.VMEM(basis.shape, basis.dtype),
            pltpu.VMEM((2, 2, frames_here * feed_here, length // 2), jnp.bfloat16),
            pltpu.VMEM((total_rows, feed_here), jnp.float32),
            pltpu.VMEM((total_rows, feed_here), jnp.bfloat16),
            pltpu.SemaphoreType.DMA((5,)),
            pltpu.SemaphoreType.DMA((2,)),
        ],
        compiler_params=pltpu.CompilerParams(vmem_limit_bytes=24 * 1024 * 1024),
        name="spectra",
    )(half_index, samples, tail, taps, basis)


def tail_kernel(samples_ref, out_ref, sem):
    count = out_ref.shape[1]
    where = pl.ds(samples_ref.shape[1] - count, count)
    copy = pltpu.make_async_copy(samples_ref.at[:, where], out_ref, sem)
    copy.start()
    copy.wait()


def last_samples(samples, count):
    return pl.pallas_call(
        tail_kernel,
        in_specs=[pl.BlockSpec(memory_space=pltpu.HBM)],
        out_specs=pl.BlockSpec(memory_space=pl.ANY),
        out_shape=jax.ShapeDtypeStruct((samples.shape[0], count), samples.dtype),
        scratch_shapes=[pltpu.SemaphoreType.DMA],
        compiler_params=pltpu.CompilerParams(vmem_limit_bytes=4 * 1024 * 1024),
        name="tail",
    )(samples)


def sine_turns(turns):
    square = turns * turns
    total = None
    for power in range(11, 0, -2):
        factor = (2.0 * math.pi) ** power / math.factorial(power) * (-1) ** (power // 2)
        total = factor if total is None else total * square + factor
    return total * turns


def unit_vector(turns):
    cosine = sine_turns(0.25 - jnp.abs(turns))
    sine = sine_turns(jnp.maximum(jnp.minimum(turns, 0.5 - turns), -0.5 - turns))
    return cosine, sine


def centred(turns):
    return turns - jnp.floor(turns + 0.5)


def chain_start(first, channels, step):
    return (first + step * (channels // 2 - 1)).astype(jnp.float32)


def chain_of_weights(first, step, code, pointing_ref, out_ref, where):
    channels, _, width = out_ref.shape
    beams = width // 2
    repeat = beams // LANES
    middle = channels // 2
    cylinder = jnp.concatenate([lax.shift_right_logical(code, PHASE_BITS)] * repeat, axis=1)
    delay = jnp.concatenate([(code & (PHASES - 1)).astype(jnp.float32)] * repeat, axis=1)
    steer = jnp.broadcast_to(pointing_ref[0:1, :], delay.shape)
    for other in range(1, CYL):
        steer = jnp.where(cylinder == other, pointing_ref[other : other + 1, :], steer)
    turns = centred(delay * steer * (1.0 / PHASES))
    low_cos, low_sin = unit_vector(centred(first * turns))
    step_cos, step_sin = unit_vector(centred(float(step) * turns))
    high_cos = low_cos * step_cos - low_sin * step_sin
    high_sin = low_cos * step_sin + low_sin * step_cos
    twice = step_cos + step_cos

    def put(channel, cosine, sine):
        out_ref[channel, where, :beams] = cosine.astype(jnp.bfloat16)
        out_ref[channel, where, beams:] = sine.astype(jnp.bfloat16)

    put(middle - 1, low_cos, low_sin)
    put(middle, high_cos, high_sin)
    up = (low_cos, low_sin, high_cos, high_sin)
    down = (high_cos, high_sin, low_cos, low_sin)
    for away in range(1, middle):
        up = (up[2], up[3], twice * up[2] - up[0], twice * up[3] - up[1])
        down = (down[2], down[3], twice * down[2] - down[0], twice * down[3] - down[1])
        put(middle + away, up[2], up[3])
        put(middle - 1 - away, down[2], down[3])


def weights_kernel(block_rows, step, first_ref, code_ref, pointing_ref, out_ref):
    channels, rows, _ = out_ref.shape
    first = chain_start(first_ref[0], channels, step)

    def one_block(index, carry):
        where = pl.ds(pl.multiple_of(index * block_rows, block_rows), block_rows)
        chain_of_weights(first, step, code_ref[where], pointing_ref.at[0], out_ref, where)
        return carry

    lax.fori_loop(0, rows // block_rows, one_block, 0)


def make_weights(first, code, pointing, channels, step, feeds):
    sets, cylinders, beams = pointing.shape
    rows = 128
    tiles = feeds // rows
    return pl.pallas_call(
        functools.partial(weights_kernel, 32, step),
        grid=(sets * tiles,),
        in_specs=[
            pl.BlockSpec(memory_space=pltpu.SMEM),
            pl.BlockSpec((rows, LANES), lambda i: (i % tiles, 0)),
            pl.BlockSpec((1, cylinders, beams), lambda i: (i // tiles, 0, 0)),
        ],
        out_specs=pl.BlockSpec((channels, rows, 2 * beams), lambda i: (0, i, 0)),
        out_shape=jax.ShapeDtypeStruct((channels, sets * feeds, 2 * beams), jnp.bfloat16),
        compiler_params=VMEM,
        cost_estimate=pl.CostEstimate(
            flops=channels * sets * feeds * beams * 8,
            bytes_accessed=channels * sets * feeds * beams * 4,
            transcendentals=0,
        ),
        name="weights",
    )(first, code, pointing)


def padded_rows(rows):
    return -(-rows // 16) * 16


def turn_products(both):
    beams = both.shape[1] // 2
    half = both.shape[0] // 2
    by_imag = both[:, beams:]
    return both[:, :beams] + jnp.concatenate([-by_imag[half:], by_imag[:half]], axis=0)


def line_up(layout, arrived, wide, lined, spectra):
    near, cores, channels, frames_here = layout
    per_source = 2 * frames_here
    per_channel = per_source * cores
    spare = spectra.shape[1] - per_channel
    wide[...] = arrived[...].astype(jnp.float32)
    for place in range(near):
        for core in range(cores):
            base = (place * cores + core) * channels * per_source
            for part in range(2):
                for index in range(frames_here):
                    source = base + part * frames_here + index
                    target = (part * cores + core) * frames_here + index
                    lined[place, pl.ds(target, channels, stride=per_channel), :] = wide[
                        pl.ds(source, channels, stride=per_source), :
                    ]
    blank = jnp.zeros((spare, arrived.shape[1]), jnp.float32)
    for channel in range(channels):
        rows = slice(channel * per_channel, (channel + 1) * per_channel)
        blocks = [
            jnp.concatenate([lined[place, rows, :], blank], axis=0) for place in range(near)
        ]
        spectra[channel] = jnp.concatenate(blocks, axis=1).astype(jnp.bfloat16)


def beams_kernel(
    layout, which, step, pieces, first_ref, code_ref, pointing_ref, weights_ref, spectra_ref,
    *rest,
):
    near, cores, channels, frames_here = layout
    per_channel = 2 * frames_here * cores
    raw = which == 0
    if raw:
        out_ref, spectra, stored, own, total, spectra_sem, sems, arrived, wide, lined = rest
        fetch = pltpu.make_async_copy(spectra_ref, arrived, spectra_sem)
    else:
        out_ref, stored, own, total, spectra_sem, sems, spectra = rest
        fetch = pltpu.make_async_copy(spectra_ref, spectra, spectra_sem)
    fetch.start()
    made_feeds = stored.shape[1]
    own_rows = own.shape[1]
    count = channels // pieces
    copies = []
    for piece in range(pieces):
        place = pl.ds(piece * count, count)
        source = weights_ref.at[place, pl.ds(which * made_feeds, made_feeds)]
        copies.append(pltpu.make_async_copy(source, stored.at[place], sems.at[piece]))
    ahead = 5
    for copy in copies[:ahead]:
        copy.start()

    block_rows = 32
    first = chain_start(first_ref[0], channels, step)

    def one_block(index, carry):
        target = pl.ds(pl.multiple_of(index * block_rows, block_rows), block_rows)
        source = pl.ds(pl.multiple_of(made_feeds + index * block_rows, block_rows), block_rows)
        chain_of_weights(first, step, code_ref[source], pointing_ref.at[which], own, target)
        return carry

    lax.fori_loop(0, own_rows // block_rows, one_block, 0)
    fetch.wait()
    if raw:
        line_up(layout, arrived, wide, lined, spectra)

    for channel in range(channels):
        rows = slice(channel * per_channel, (channel + 1) * per_channel)
        total[rows, :] = jnp.dot(
            spectra[channel, :, made_feeds:], own[channel], preferred_element_type=jnp.float32
        )[:per_channel]
    for piece in range(pieces):
        copies[piece].wait()
        if piece + ahead < pieces:
            copies[piece + ahead].start()
        for channel in range(piece * count, (piece + 1) * count):
            rows = slice(channel * per_channel, (channel + 1) * per_channel)
            both = jnp.dot(
                spectra[channel, :, :made_feeds],
                stored[channel],
                preferred_element_type=jnp.float32,
            )[:per_channel]
            out_ref[rows, :] = turn_products(total[rows, :] + both).astype(out_ref.dtype)


def partial_beams(first, code, pointing, weights, spectra, layout, which, step, dtype):
    near, cores, channels, frames_here = layout
    feeds = code.shape[0]
    made_feeds = weights.shape[1] // pointing.shape[0]
    width = weights.shape[2]
    per_channel = 2 * cores * frames_here
    pieces = 8
    in_vmem = pl.BlockSpec(memory_space=pltpu.VMEM)
    lined_shape = (channels, padded_rows(per_channel), feeds)
    out_shape = [jax.ShapeDtypeStruct((channels * per_channel, width // 2), dtype)]
    scratch = [
        pltpu.VMEM((channels, made_feeds, width), weights.dtype),
        pltpu.VMEM((channels, feeds - made_feeds, width), weights.dtype),
        pltpu.VMEM((channels * per_channel, width), jnp.float32),
        pltpu.SemaphoreType.DMA,
        pltpu.SemaphoreType.DMA((pieces,)),
    ]
    if which == 0:
        out_shape.append(jax.ShapeDtypeStruct(lined_shape, jnp.bfloat16))
        scratch += [
            pltpu.VMEM(spectra.shape, spectra.dtype),
            pltpu.VMEM(spectra.shape, jnp.float32),
            pltpu.VMEM((near, channels * per_channel, feeds // near), jnp.float32),
        ]
    else:
        scratch.append(pltpu.VMEM(lined_shape, jnp.bfloat16))
    return pl.pallas_call(
        functools.partial(beams_kernel, layout, which, step, pieces),
        in_specs=[
            pl.BlockSpec(memory_space=pltpu.SMEM),
            in_vmem,
            in_vmem,
            pl.BlockSpec(memory_space=pltpu.HBM),
            pl.BlockSpec(memory_space=pl.ANY if which == 0 else pltpu.HBM),
        ],
        out_specs=[in_vmem] * len(out_shape),
        out_shape=out_shape,
        scratch_shapes=scratch,
        compiler_params=pltpu.CompilerParams(vmem_limit_bytes=50 * 1024 * 1024),
        cost_estimate=pl.CostEstimate(
            flops=channels * feeds * width * 2 * 128,
            bytes_accessed=channels * feeds * width * 2,
            transcendentals=0,
        ),
        name="beams",
    )(first, code, pointing, weights, spectra)


def gather_kernel(
    layout, beams_here, scale, own_ref, other_ref, out_ref, own, other, total, rows, sems
):
    near, cores, channels, frames_here = layout
    lane_channels = LANES // beams_here
    per_core = 2 * frames_here
    per_channel = per_core * cores
    groups = channels // lane_channels
    fetches = [
        pltpu.make_async_copy(own_ref, own, sems.at[0]),
        pltpu.make_async_copy(other_ref, other, sems.at[1]),
    ]
    for fetch in fetches:
        fetch.start()
    for fetch in fetches:
        fetch.wait()
    total[...] = (own[...] + other[...].astype(jnp.float32)) * scale
    for group in range(groups):
        values = [
            total[pl.ds((group * lane_channels + sub) * per_channel, per_channel), :]
            for sub in range(lane_channels)
        ]
        for place in range(near):
            lanes = slice(place * beams_here, (place + 1) * beams_here)
            tile = jnp.concatenate([value[:, lanes] for value in values], axis=1)
            for core in range(cores):
                start = ((place * cores + core) * groups + group) * per_core
                for part in range(2):
                    source = (part * cores + core) * frames_here
                    rows[pl.ds(start + part * frames_here, frames_here), :] = tile[
                        source : source + frames_here
                    ]
    out_ref[...] = rows[...].astype(jnp.bfloat16)


def gather_beams(own, other, layout, beams_here, scale):
    near, cores, channels, frames_here = layout
    total_rows = near * cores * channels // (LANES // beams_here) * 2 * frames_here
    return pl.pallas_call(
        functools.partial(gather_kernel, layout, beams_here, scale),
        in_specs=[pl.BlockSpec(memory_space=pltpu.HBM), pl.BlockSpec(memory_space=pl.ANY)],
        out_shape=jax.ShapeDtypeStruct((total_rows, LANES), jnp.bfloat16),
        scratch_shapes=[
            pltpu.VMEM(own.shape, own.dtype),
            pltpu.VMEM(other.shape, other.dtype),
            pltpu.VMEM(own.shape, jnp.float32),
            pltpu.VMEM((total_rows, LANES), jnp.float32),
            pltpu.SemaphoreType.DMA((2,)),
        ],
        compiler_params=pltpu.CompilerParams(vmem_limit_bytes=16 * 1024 * 1024),
        name="gather",
    )(own, other)


def series_kernel(
    beams_here, half_ref, received_ref, cos_ref, sin_ref, basis_ref, out_ref,
    arrived, basis, wide, lined, sems,
):
    frames_here = out_ref.shape[0]
    kappas = cos_ref.shape[0]
    lane_channels = LANES // beams_here
    side = kappas // 2
    half = half_ref[0]
    sign = (1 - 2 * half).astype(jnp.float32)
    fetch = pltpu.make_async_copy(received_ref, arrived, sems.at[2])
    fetch.start()
    fetch_basis = [
        pltpu.make_async_copy(
            basis_ref.at[parity + half * (1 - 2 * parity)], basis.at[parity], sems.at[parity]
        )
        for parity in range(2)
    ]
    for copy in fetch_basis:
        copy.start()
    fetch.wait()
    wide[...] = arrived[...].astype(jnp.float32)
    for index in range(frames_here):
        real = wide[pl.ds(index, kappas, stride=2 * frames_here), :]
        imag = wide[pl.ds(frames_here + index, kappas, stride=2 * frames_here), :]
        chirped_real = real * cos_ref[...] - imag * sin_ref[...]
        chirped_imag = real * sin_ref[...] + imag * cos_ref[...]
        target = slice(index * beams_here, (index + 1) * beams_here)
        for parity in range(2):
            where = slice(parity * side, (parity + 1) * side)
            both = jnp.concatenate([chirped_real[where], chirped_imag[where]], axis=0)
            turned = both.T
            high = turned.astype(jnp.bfloat16)
            low = (turned - high.astype(jnp.float32)).astype(jnp.bfloat16)
            for sub in range(lane_channels):
                source = slice(sub * beams_here, (sub + 1) * beams_here)
                lanes = slice(sub * 2 * side, (sub + 1) * 2 * side)
                lined[parity, 0, target, lanes] = high[source]
                lined[parity, 1, target, lanes] = low[source]
    sides = []
    for parity in range(2):
        high = lined[parity, 0]
        low = lined[parity, 1]
        fetch_basis[parity].wait()
        sides.append(
            jnp.dot(high, basis[parity, 0], preferred_element_type=jnp.float32)
            + jnp.dot(low, basis[parity, 0], preferred_element_type=jnp.float32)
            + jnp.dot(high, basis[parity, 1], preferred_element_type=jnp.float32)
        )
    times = sides[0].shape[1] // 2
    for part in range(2):
        even = sides[0][:, part * times : (part + 1) * times]
        odd = sides[1][:, part * times : (part + 1) * times]
        for which, value in enumerate((even + odd, (even - odd) * sign)):
            start = (2 * part + which) * times
            out_ref[:, :, start : start + times] = value.reshape(frames_here, beams_here, times)


def make_series(half_index, received, chirp_cos, chirp_sin, basis, beams_here, frames_here):
    in_vmem = pl.BlockSpec(memory_space=pltpu.VMEM)
    anywhere = pl.BlockSpec(memory_space=pl.ANY)
    series = pl.pallas_call(
        functools.partial(series_kernel, beams_here),
        in_specs=[
            pl.BlockSpec(memory_space=pltpu.SMEM), anywhere, in_vmem, in_vmem, anywhere,
        ],
        out_shape=jax.ShapeDtypeStruct(
            (frames_here, beams_here, 2 * basis.shape[3]), jnp.float32
        ),
        scratch_shapes=[
            pltpu.VMEM(received.shape, received.dtype),
            pltpu.VMEM(basis.shape, basis.dtype),
            pltpu.VMEM(received.shape, jnp.float32),
            pltpu.VMEM((2, 2, frames_here * beams_here, basis.shape[2]), jnp.bfloat16),
            pltpu.SemaphoreType.DMA((3,)),
        ],
        compiler_params=pltpu.CompilerParams(vmem_limit_bytes=24 * 1024 * 1024),
        name="series",
    )(half_index, received, chirp_cos, chirp_sin, basis)
    return jnp.transpose(series, (1, 0, 2))


def halves_body(samples, filter_taps, feed_cylinder, feed_delay, pointing, chirp_rate):
    length = filter_taps.shape[1]
    nchan = length // 2
    feed_here = samples.shape[0]
    frames_here = samples.shape[1] // length
    feeds = feed_delay.shape[0]
    beams = pointing.shape[0]
    beams_here = chirp_rate.shape[0]
    near = lax.axis_size("near")
    cores = lax.axis_size("tm")
    group = near * cores
    channels = nchan // group
    half_feeds = feeds // HALVES
    half_beams = beams // HALVES
    layout = (near, cores, channels, frames_here)
    half_index = lax.axis_index("half")
    place = lax.axis_index(GROUP)

    tail = from_behind(last_samples(samples, (TAPS - 1) * length), "tm", 1)
    forward = jnp.asarray(folded_forward_basis(length))
    half_scalar = jnp.reshape(half_index, (1,)).astype(jnp.int32)
    spectra = spectra_rows(half_scalar, samples, tail, filter_taps, forward)
    spectra = spectra.reshape(group, channels * 2 * frames_here, feed_here)
    received = lax.all_to_all(spectra, GROUP, 0, 0, tiled=True)
    received = received.reshape(-1, feed_here)

    in_parity = group // 2
    first = 2 * (place % in_parity) * channels + (place // in_parity ^ half_index) + 1
    first = jnp.reshape(first, (1,)).astype(jnp.int32)
    code = feed_cylinder * PHASES + feed_delay
    code = lax.dynamic_slice_in_dim(code, half_index * half_feeds, half_feeds)
    code = jnp.broadcast_to(code[:, None], (half_feeds, LANES))
    aim = jnp.transpose(pointing).astype(jnp.float32)
    aims = jnp.stack(
        [
            lax.dynamic_slice_in_dim(aim, half * half_beams, half_beams, 1)
            for half in (1 - half_index, half_index)
        ]
    )
    step = 2
    weights = make_weights(first, code, aims, channels, step, half_feeds * 3 // 4)
    to_send, lined = partial_beams(
        first, code, aims, weights, received, layout, 0, step, jnp.bfloat16
    )
    swap = [
        (half * near + i, (1 - half) * near + (i + near // 2) % near)
        for half in range(HALVES)
        for i in range(near)
    ]
    arrived = lax.ppermute(to_send, ("half", "near"), swap)
    (own,) = partial_beams(first, code, aims, weights, lined, layout, 1, step, jnp.float32)
    gathered = gather_beams(own, arrived, layout, beams_here, 1.0 / math.sqrt(feeds))
    lane_channels = LANES // beams_here
    gathered = gathered.reshape(group, -1, LANES)
    returned = lax.all_to_all(gathered, GROUP, 0, 0, tiled=True).reshape(-1, LANES)

    kappa = jnp.arange(nchan // lane_channels, dtype=jnp.int32)[:, None]
    sub = jnp.arange(LANES, dtype=jnp.int32)[None, :] // beams_here
    side = nchan // lane_channels // 2
    channel = 2 * (lane_channels * (kappa % side) + sub) + (kappa // side ^ half_index)
    position = channel.astype(jnp.float32) / nchan
    rate = jnp.tile(jnp.pi * chirp_rate, lane_channels)[None, :]
    chirp = rate * (position * position)
    inverse = jnp.asarray(folded_inverse_basis(nchan, lane_channels))
    return make_series(
        half_scalar, returned, jnp.cos(chirp), jnp.sin(chirp), inverse, beams_here, frames_here
    )


def solution(mesh):
    feed_size = mesh.shape["feed"]
    wide_enough = FEEDS // feed_size % LANES == 0 and BEAMS // feed_size * 4 == LANES
    if not wide_enough:
        return jax.shard_map(
            plain_body,
            mesh=mesh,
            in_specs=(P("feed", "tm"), P(), P(), P(), P(), P("feed")),
            out_specs=P("feed", "tm", None),
            check_vma=False,
        )
    devices = mesh.devices.reshape(HALVES, feed_size // HALVES, mesh.shape["tm"])
    halved = jax.sharding.Mesh(devices, ("half", "near", "tm"))
    feed = ("half", "near")
    return jax.shard_map(
        halves_body,
        mesh=halved,
        in_specs=(P(feed, "tm"), P(), P(), P(), P(), P(feed)),
        out_specs=P(feed, "tm", None),
        check_vma=False,
    )
```

```python
import functools
import math

import jax
import jax.numpy as jnp
import ml_dtypes
import numpy as np
from jax import lax
from jax.experimental import pallas as pl
from jax.experimental.pallas import tpu as pltpu
from jax.sharding import PartitionSpec as P

FEEDS = 2048
NCHAN = 512
BEAMS = 512
TAPS = 4
CYL = 4
PHASES = 4096


def from_behind(x, axis, by):
    length = lax.axis_size(axis)
    pairs = [(i, i + by) for i in range(length) if 0 <= i + by < length]
    return lax.ppermute(x, axis, pairs)


def forward_basis(length, nchan):
    sample_ids = jnp.arange(length, dtype=jnp.int32)[:, None]
    chan_ids = jnp.arange(nchan, dtype=jnp.int32)[None, :]
    angle = (sample_ids * chan_ids % length).astype(jnp.float32) * (2.0 * math.pi / length)
    scaled = 1.0 / math.sqrt(length)
    return jnp.concatenate([jnp.cos(angle), -jnp.sin(angle)], axis=1) * scaled


def inverse_basis(nchan):
    chan_ids = jnp.arange(nchan, dtype=jnp.int32)[:, None]
    time_ids = jnp.arange(nchan, dtype=jnp.int32)[None, :]
    angle = (chan_ids * time_ids % nchan).astype(jnp.float32) * (2.0 * math.pi / nchan)
    cosine = jnp.cos(angle)
    sine = jnp.sin(angle)
    upper = jnp.concatenate([cosine, sine], axis=1)
    lower = jnp.concatenate([-sine, cosine], axis=1)
    return jnp.concatenate([upper, lower], axis=0) * (1.0 / math.sqrt(nchan))


def spectra_of(frame_block, basis):
    feed_here, batch_frames, length = frame_block.shape
    flat = frame_block.reshape(feed_here * batch_frames, length)
    spectral = jnp.dot(
        flat, basis, precision=lax.Precision.HIGHEST, preferred_element_type=jnp.float32
    )
    spectral = spectral.reshape(feed_here, batch_frames, 2, length // 2)
    return jnp.transpose(spectral, (3, 2, 1, 0)).astype(jnp.bfloat16)


def beamform(turned, steer, feed_delay, first_channel):
    chan_here, _, batch_frames, feeds = turned.shape
    beam_scale = 1.0 / math.sqrt(feeds)

    def one_channel(inputs):
        local, offset = inputs
        channel = first_channel + offset
        turns = (channel + 1) * feed_delay % PHASES
        phase = turns[:, None] * steer % PHASES
        angle = phase.astype(jnp.float32) * (2.0 * math.pi / PHASES)
        w_real = jnp.cos(angle).astype(jnp.bfloat16)
        w_imag = jnp.sin(angle).astype(jnp.bfloat16)
        stacked = local.reshape(2 * batch_frames, feeds)
        with_real = jnp.dot(stacked, w_real, preferred_element_type=jnp.float32)
        with_imag = jnp.dot(stacked, w_imag, preferred_element_type=jnp.float32)
        beam_real = with_real[:batch_frames] - with_imag[batch_frames:]
        beam_imag = with_imag[:batch_frames] + with_real[batch_frames:]
        return (jnp.stack([beam_real, beam_imag]) * beam_scale).astype(jnp.bfloat16)

    offsets = jnp.arange(chan_here, dtype=jnp.int32)
    return lax.map(one_channel, (turned, offsets))


def synthesize(returned, chirp_cos, chirp_sin, basis):
    nchan, _, batch_frames, beams_here = returned.shape
    values = returned.astype(jnp.float32)
    beam_real = values[:, 0]
    beam_imag = values[:, 1]
    chirped_real = beam_real * chirp_cos - beam_imag * chirp_sin
    chirped_imag = beam_real * chirp_sin + beam_imag * chirp_cos
    stacked = jnp.stack([chirped_real, chirped_imag])
    ordered = jnp.transpose(stacked, (3, 2, 0, 1)).reshape(beams_here * batch_frames, 2 * nchan)
    result = jnp.dot(
        ordered, basis, precision=lax.Precision.HIGHEST, preferred_element_type=jnp.float32
    )
    return result.reshape(beams_here, batch_frames, 2 * nchan)


def plain_body(samples, filter_taps, feed_cylinder, feed_delay, pointing, chirp_rate):
    length = 2 * NCHAN
    feed_here = samples.shape[0]
    frames_here = samples.shape[1] // length
    frames = samples.reshape(feed_here, frames_here, length)
    tail = from_behind(frames[:, frames_here - (TAPS - 1) :, :], "tm", 1)
    padded = jnp.concatenate([tail, frames], axis=1).astype(jnp.float32)
    filtered = jnp.zeros((feed_here, frames_here, length), jnp.float32)
    for tap_index in range(TAPS):
        filtered = (
            filtered + filter_taps[tap_index] * padded[:, tap_index : tap_index + frames_here, :]
        )
    basis = forward_basis(length, NCHAN)
    steer = jnp.zeros((FEEDS, BEAMS), jnp.int32)
    for cylinder in range(CYL):
        steer = steer + jnp.where(
            feed_cylinder[:, None] == cylinder, pointing[None, :, cylinder], 0
        )
    chan_here = NCHAN // lax.axis_size("feed")
    first_channel = lax.axis_index("feed") * chan_here
    position = jnp.arange(NCHAN).astype(jnp.float32) / NCHAN
    chirp = (jnp.pi * chirp_rate)[None, :] * (position * position)[:, None]
    chirp_cos = jnp.cos(chirp)[:, None, :]
    chirp_sin = jnp.sin(chirp)[:, None, :]
    back_basis = inverse_basis(NCHAN)
    turned = lax.all_to_all(
        spectra_of(filtered, basis), "feed", split_axis=0, concat_axis=3, tiled=True
    )
    formed = beamform(turned, steer, feed_delay, first_channel)
    returned = lax.all_to_all(formed, "feed", split_axis=3, concat_axis=0, tiled=True)
    series = synthesize(returned, chirp_cos, chirp_sin, back_basis)
    return series


LANES = 128
PHASE_BITS = PHASES.bit_length() - 1
HALVES = 2
GROUP = ("near", "tm")
VMEM = pltpu.CompilerParams(vmem_limit_bytes=56 * 1024 * 1024)


def split_bf16(table):
    high = table.astype(ml_dtypes.bfloat16)
    low = (table - high.astype(np.float64)).astype(ml_dtypes.bfloat16)
    return np.stack([high, low])


def folded_forward_basis(length):
    half = length // 2
    tables = []
    for parity in range(2):
        channel = 2 * np.arange(half // 2)[:, None] + parity
        angle = (channel * np.arange(half)[None, :] % length) * (2.0 * np.pi / length)
        rows = np.concatenate([np.cos(angle), -np.sin(angle)], axis=0) / math.sqrt(length)
        tables.append(split_bf16(rows))
    return np.stack(tables)


def folded_inverse_basis(nchan, lane_channels):
    kappas = nchan // 2 // lane_channels
    times = np.arange(nchan // 2)[None, :]
    tables = []
    for parity in range(2):
        rows = []
        for sub in range(lane_channels):
            channel = 2 * (lane_channels * np.arange(kappas)[:, None] + sub) + parity
            angle = (channel * times % nchan) * (2.0 * np.pi / nchan)
            rows.append(np.concatenate([np.cos(angle), np.sin(angle)], axis=1))
            rows.append(np.concatenate([-np.sin(angle), np.cos(angle)], axis=1))
        tables.append(split_bf16(np.concatenate(rows, axis=0) / math.sqrt(nchan)))
    return np.stack(tables)


def dot_nt(left, right):
    return lax.dot_general(
        left, right, (((1,), (1,)), ((), ())), preferred_element_type=jnp.float32
    )


def spectra_kernel(
    frames_here, group, half_ref, samples_ref, tail_ref, taps_in_ref, basis_ref, out_ref,
    samples, tail, taps_ref, basis, folded, packed, in_sems, out_sems,
):
    feed_here = samples_ref.shape[0]
    length = taps_ref.shape[1]
    half = length // 2
    before = TAPS - 1
    side = half_ref[0]
    sign = (1 - 2 * side).astype(jnp.float32)
    fetch_samples = pltpu.make_async_copy(samples_ref, samples, in_sems.at[0])
    fetch_tail = pltpu.make_async_copy(tail_ref, tail, in_sems.at[1])
    fetch_taps = pltpu.make_async_copy(taps_in_ref, taps_ref, in_sems.at[4])
    fetch_basis = [
        pltpu.make_async_copy(
            basis_ref.at[parity + side * (1 - 2 * parity)], basis.at[parity], in_sems.at[2 + parity]
        )
        for parity in range(2)
    ]
    fetches = [fetch_taps, fetch_samples, fetch_tail] + fetch_basis
    for fetch in fetches:
        fetch.start()
    fetch_taps.wait()
    fetch_samples.wait()

    def frame(index, start):
        if index < 0:
            lanes = pl.ds((index + before) * length + start, LANES)
            return tail[:, lanes].astype(jnp.float32)
        return samples[:, pl.ds(index * length + start, LANES)].astype(jnp.float32)

    def filtered(index, start):
        total = None
        for tap in range(TAPS):
            term = taps_ref[tap : tap + 1, start : start + LANES] * frame(
                index + tap - before, start
            )
            total = term if total is None else total + term
        return total

    for index in list(range(before, frames_here)) + list(range(before)):
        if index == 0:
            fetch_tail.wait()
        where = pl.ds(index * feed_here, feed_here)
        for start in range(0, half, LANES):
            near = filtered(index, start)
            far = filtered(index, start + half) * sign
            for parity, value in enumerate((near + far, near - far)):
                high = value.astype(jnp.bfloat16)
                folded[parity, 0, where, start : start + LANES] = high
                folded[parity, 1, where, start : start + LANES] = (
                    value - high.astype(jnp.float32)
                ).astype(jnp.bfloat16)

    parts = 2 * frames_here
    together = 2
    count = half // 2
    channels = length // 2 // group
    stores = []
    for parity in range(2):
        fetch_basis[parity].wait()
        for first in range(0, frames_here, together):
            where = pl.ds(first * feed_here, together * feed_here)
            high = folded[parity, 0, where, :]
            low = folded[parity, 1, where, :]
            result = (
                dot_nt(basis[parity, 0], high)
                + dot_nt(basis[parity, 1], high)
                + dot_nt(basis[parity, 0], low)
            ).astype(jnp.bfloat16)
            for part in range(2):
                for ahead in range(together):
                    row = part * frames_here + first + ahead
                    for place in range(count // channels):
                        target = (parity * (count // channels) + place) * parts + row
                        source = part * count + place * channels
                        packed[pl.ds(target * channels, channels), :] = result[
                            source : source + channels,
                            ahead * feed_here : (ahead + 1) * feed_here,
                        ]
        block = pl.ds(parity * count * parts, count * parts)
        store = pltpu.make_async_copy(packed.at[block], out_ref.at[block], out_sems.at[parity])
        store.start()
        stores.append(store)
    for store in stores:
        store.wait()


def spectra_rows(half_index, samples, tail, taps, basis, group):
    feed_here = samples.shape[0]
    length = taps.shape[1]
    frames_here = samples.shape[1] // length
    total_rows = length * frames_here
    anywhere = pl.BlockSpec(memory_space=pl.ANY)
    in_hbm = pl.BlockSpec(memory_space=pltpu.HBM)
    return pl.pallas_call(
        functools.partial(spectra_kernel, frames_here, group),
        in_specs=[pl.BlockSpec(memory_space=pltpu.SMEM), in_hbm, anywhere, in_hbm, in_hbm],
        out_specs=anywhere,
        out_shape=jax.ShapeDtypeStruct((total_rows, feed_here), jnp.bfloat16),
        scratch_shapes=[
            pltpu.VMEM(samples.shape, samples.dtype),
            pltpu.VMEM(tail.shape, tail.dtype),
            pltpu.VMEM(taps.shape, taps.dtype),
            pltpu.VMEM(basis.shape, basis.dtype),
            pltpu.VMEM((2, 2, frames_here * feed_here, length // 2), jnp.bfloat16),
            pltpu.VMEM((total_rows, feed_here), jnp.bfloat16),
            pltpu.SemaphoreType.DMA((5,)),
            pltpu.SemaphoreType.DMA((2,)),
        ],
        compiler_params=pltpu.CompilerParams(vmem_limit_bytes=50 * 1024 * 1024),
        name="spectra",
    )(half_index, samples, tail, taps, basis)


def sine_turns(turns):
    square = turns * turns
    total = None
    for power in range(11, 0, -2):
        factor = (2.0 * math.pi) ** power / math.factorial(power) * (-1) ** (power // 2)
        total = factor if total is None else total * square + factor
    return total * turns


def unit_vector(turns):
    cosine = sine_turns(0.25 - jnp.abs(turns))
    sine = sine_turns(jnp.maximum(jnp.minimum(turns, 0.5 - turns), -0.5 - turns))
    return cosine, sine


def centred(turns):
    return turns - jnp.floor(turns + 0.5)


def chain_start(first, channels, step):
    return (first + step * (channels // 2 - 1)).astype(jnp.float32)


def chain_of_weights(first, step, code, pointing_ref, out_ref, where):
    channels, _, width = out_ref.shape
    beams = width // 2
    repeat = beams // LANES
    middle = channels // 2
    cylinder = jnp.concatenate([lax.shift_right_logical(code, PHASE_BITS)] * repeat, axis=1)
    delay = jnp.concatenate([(code & (PHASES - 1)).astype(jnp.float32)] * repeat, axis=1)
    steer = jnp.broadcast_to(pointing_ref[0:1, :], delay.shape)
    for other in range(1, CYL):
        steer = jnp.where(cylinder == other, pointing_ref[other : other + 1, :], steer)
    turns = centred(delay * steer * (1.0 / PHASES))
    low_cos, low_sin = unit_vector(centred(first * turns))
    step_cos, step_sin = unit_vector(centred(float(step) * turns))
    high_cos = low_cos * step_cos - low_sin * step_sin
    high_sin = low_cos * step_sin + low_sin * step_cos
    twice = step_cos + step_cos

    def put(channel, cosine, sine):
        out_ref[channel, where, :beams] = cosine.astype(jnp.bfloat16)
        out_ref[channel, where, beams:] = sine.astype(jnp.bfloat16)

    put(middle - 1, low_cos, low_sin)
    put(middle, high_cos, high_sin)
    up = (low_cos, low_sin, high_cos, high_sin)
    down = (high_cos, high_sin, low_cos, low_sin)
    for away in range(1, middle):
        up = (up[2], up[3], twice * up[2] - up[0], twice * up[3] - up[1])
        down = (down[2], down[3], twice * down[2] - down[0], twice * down[3] - down[1])
        put(middle + away, up[2], up[3])
        put(middle - 1 - away, down[2], down[3])


def weights_kernel(block_rows, step, first_ref, code_ref, pointing_ref, out_ref):
    channels, rows, _ = out_ref.shape
    first = chain_start(first_ref[0], channels, step)

    def one_block(index, carry):
        where = pl.ds(pl.multiple_of(index * block_rows, block_rows), block_rows)
        chain_of_weights(first, step, code_ref[where], pointing_ref.at[0], out_ref, where)
        return carry

    lax.fori_loop(0, rows // block_rows, one_block, 0)


def make_weights(first, code, pointing, channels, step, feeds):
    _, cylinders, beams = pointing.shape
    rows = 128
    tiles = [count // rows for count in feeds]
    return pl.pallas_call(
        functools.partial(weights_kernel, 32, step),
        grid=(sum(tiles),),
        in_specs=[
            pl.BlockSpec(memory_space=pltpu.SMEM),
            pl.BlockSpec((rows, LANES), lambda i: (jnp.where(i < tiles[0], i, i - tiles[0]), 0)),
            pl.BlockSpec((1, cylinders, beams), lambda i: (jnp.where(i < tiles[0], 0, 1), 0, 0)),
        ],
        out_specs=pl.BlockSpec((channels, rows, 2 * beams), lambda i: (0, i, 0)),
        out_shape=jax.ShapeDtypeStruct((channels, sum(feeds), 2 * beams), jnp.bfloat16),
        compiler_params=VMEM,
        cost_estimate=pl.CostEstimate(
            flops=channels * sum(feeds) * beams * 8,
            bytes_accessed=channels * sum(feeds) * beams * 4,
            transcendentals=0,
        ),
        name="weights",
    )(first, code, pointing)


def padded_rows(rows):
    return -(-rows // 16) * 16


def turn_products(both):
    beams = both.shape[1] // 2
    half = both.shape[0] // 2
    by_imag = both[:, beams:]
    return both[:, :beams] + jnp.concatenate([-by_imag[half:], by_imag[:half]], axis=0)


def line_up(layout, arrived, lined, spectra):
    near, cores, channels, frames_here = layout
    per_source = 2 * frames_here
    per_channel = per_source * cores
    spare = spectra.shape[1] - per_channel
    for place in range(near):
        for core in range(cores):
            base = (place * cores + core) * per_source
            for part in range(2):
                for index in range(frames_here):
                    source = (base + part * frames_here + index) * channels
                    target = (part * cores + core) * frames_here + index
                    lined[place, pl.ds(target, channels, stride=per_channel), :] = arrived[
                        pl.ds(source, channels), :
                    ].astype(jnp.float32)
    blank = jnp.zeros((spare, arrived.shape[1]), jnp.float32)
    for channel in range(channels):
        rows = slice(channel * per_channel, (channel + 1) * per_channel)
        blocks = [
            jnp.concatenate([lined[place, rows, :], blank], axis=0) for place in range(near)
        ]
        spectra[channel] = jnp.concatenate(blocks, axis=1).astype(jnp.bfloat16)


def beams_kernel(
    layout, which, step, pieces, skipped, first_ref, code_ref, pointing_ref, weights_ref, spectra_ref,
    *rest,
):
    near, cores, channels, frames_here = layout
    per_channel = 2 * frames_here * cores
    raw = which == 0
    if raw:
        out_ref, spectra, stored, own, total, spectra_sem, sems, arrived, lined = rest
        fetch = pltpu.make_async_copy(spectra_ref, arrived, spectra_sem)
    else:
        out_ref, stored, own, total, spectra_sem, sems, spectra = rest
        fetch = pltpu.make_async_copy(spectra_ref, spectra, spectra_sem)
    fetch.start()
    made_feeds = stored.shape[1]
    own_rows = own.shape[1]
    count = channels // pieces
    copies = []
    for piece in range(pieces):
        place = pl.ds(piece * count, count)
        source = weights_ref.at[place, pl.ds(skipped, made_feeds)]
        copies.append(pltpu.make_async_copy(source, stored.at[place], sems.at[piece]))
    ahead = 5
    for copy in copies[:ahead]:
        copy.start()

    block_rows = 32
    first = chain_start(first_ref[0], channels, step)

    def one_block(index, carry):
        target = pl.ds(pl.multiple_of(index * block_rows, block_rows), block_rows)
        source = pl.ds(pl.multiple_of(made_feeds + index * block_rows, block_rows), block_rows)
        chain_of_weights(first, step, code_ref[source], pointing_ref.at[which], own, target)
        return carry

    lax.fori_loop(0, own_rows // block_rows, one_block, 0)
    fetch.wait()
    if raw:
        line_up(layout, arrived, lined, spectra)

    for channel in range(channels):
        rows = slice(channel * per_channel, (channel + 1) * per_channel)
        total[rows, :] = jnp.dot(
            spectra[channel, :, made_feeds:], own[channel], preferred_element_type=jnp.float32
        )[:per_channel]
    for piece in range(pieces):
        copies[piece].wait()
        if piece + ahead < pieces:
            copies[piece + ahead].start()
        for channel in range(piece * count, (piece + 1) * count):
            rows = slice(channel * per_channel, (channel + 1) * per_channel)
            both = jnp.dot(
                spectra[channel, :, :made_feeds],
                stored[channel],
                preferred_element_type=jnp.float32,
            )[:per_channel]
            out_ref[rows, :] = turn_products(total[rows, :] + both).astype(out_ref.dtype)


def partial_beams(first, code, pointing, weights, made, spectra, layout, which, step, dtype):
    near, cores, channels, frames_here = layout
    feeds = code.shape[0]
    made_feeds = made[which]
    width = weights.shape[2]
    per_channel = 2 * cores * frames_here
    pieces = 8
    in_vmem = pl.BlockSpec(memory_space=pltpu.VMEM)
    lined_shape = (channels, padded_rows(per_channel), feeds)
    out_shape = [jax.ShapeDtypeStruct((channels * per_channel, width // 2), dtype)]
    scratch = [
        pltpu.VMEM((channels, made_feeds, width), weights.dtype),
        pltpu.VMEM((channels, feeds - made_feeds, width), weights.dtype),
        pltpu.VMEM((channels * per_channel, width), jnp.float32),
        pltpu.SemaphoreType.DMA,
        pltpu.SemaphoreType.DMA((pieces,)),
    ]
    if which == 0:
        out_shape.append(jax.ShapeDtypeStruct(lined_shape, jnp.bfloat16))
        scratch += [
            pltpu.VMEM(spectra.shape, spectra.dtype),
            pltpu.VMEM((near, channels * per_channel, feeds // near), jnp.float32),
        ]
    else:
        scratch.append(pltpu.VMEM(lined_shape, jnp.bfloat16))
    return pl.pallas_call(
        functools.partial(beams_kernel, layout, which, step, pieces, sum(made[:which])),
        in_specs=[
            pl.BlockSpec(memory_space=pltpu.SMEM),
            in_vmem,
            in_vmem,
            pl.BlockSpec(memory_space=pltpu.HBM),
            pl.BlockSpec(memory_space=pl.ANY if which == 0 else pltpu.HBM),
        ],
        out_specs=[in_vmem] * len(out_shape),
        out_shape=out_shape,
        scratch_shapes=scratch,
        compiler_params=pltpu.CompilerParams(vmem_limit_bytes=50 * 1024 * 1024),
        cost_estimate=pl.CostEstimate(
            flops=channels * feeds * width * 2 * 128,
            bytes_accessed=channels * feeds * width * 2,
            transcendentals=0,
        ),
        name="beams",
    )(first, code, pointing, weights, spectra)


def gather_kernel(
    layout, beams_here, scale, own_ref, other_ref, out_ref, own, other, total, rows, sems
):
    near, cores, channels, frames_here = layout
    lane_channels = LANES // beams_here
    per_core = 2 * frames_here
    per_channel = per_core * cores
    groups = channels // lane_channels
    fetches = [
        pltpu.make_async_copy(own_ref, own, sems.at[0]),
        pltpu.make_async_copy(other_ref, other, sems.at[1]),
    ]
    for fetch in fetches:
        fetch.start()
    for fetch in fetches:
        fetch.wait()
    total[...] = (own[...] + other[...].astype(jnp.float32)) * scale
    for group in range(groups):
        values = [
            total[pl.ds((group * lane_channels + sub) * per_channel, per_channel), :]
            for sub in range(lane_channels)
        ]
        for place in range(near):
            lanes = slice(place * beams_here, (place + 1) * beams_here)
            tile = jnp.concatenate([value[:, lanes] for value in values], axis=1)
            for core in range(cores):
                start = ((place * cores + core) * groups + group) * per_core
                for part in range(2):
                    source = (part * cores + core) * frames_here
                    rows[pl.ds(start + part * frames_here, frames_here), :] = tile[
                        source : source + frames_here
                    ]
    out_ref[...] = rows[...].astype(jnp.bfloat16)


def gather_beams(own, other, layout, beams_here, scale):
    near, cores, channels, frames_here = layout
    total_rows = near * cores * channels // (LANES // beams_here) * 2 * frames_here
    return pl.pallas_call(
        functools.partial(gather_kernel, layout, beams_here, scale),
        in_specs=[pl.BlockSpec(memory_space=pltpu.HBM), pl.BlockSpec(memory_space=pl.ANY)],
        out_shape=jax.ShapeDtypeStruct((total_rows, LANES), jnp.bfloat16),
        scratch_shapes=[
            pltpu.VMEM(own.shape, own.dtype),
            pltpu.VMEM(other.shape, other.dtype),
            pltpu.VMEM(own.shape, jnp.float32),
            pltpu.VMEM((total_rows, LANES), jnp.float32),
            pltpu.SemaphoreType.DMA((2,)),
        ],
        compiler_params=pltpu.CompilerParams(vmem_limit_bytes=16 * 1024 * 1024),
        name="gather",
    )(own, other)


def series_kernel(
    beams_here, half_ref, received_ref, cos_ref, sin_ref, basis_ref, out_ref,
    arrived, basis, wide, lined, sems,
):
    frames_here = out_ref.shape[0]
    kappas = cos_ref.shape[0]
    lane_channels = LANES // beams_here
    side = kappas // 2
    half = half_ref[0]
    sign = (1 - 2 * half).astype(jnp.float32)
    fetch = pltpu.make_async_copy(received_ref, arrived, sems.at[2])
    fetch.start()
    fetch_basis = [
        pltpu.make_async_copy(
            basis_ref.at[parity + half * (1 - 2 * parity)], basis.at[parity], sems.at[parity]
        )
        for parity in range(2)
    ]
    for copy in fetch_basis:
        copy.start()
    fetch.wait()
    wide[...] = arrived[...].astype(jnp.float32)
    for index in range(frames_here):
        real = wide[pl.ds(index, kappas, stride=2 * frames_here), :]
        imag = wide[pl.ds(frames_here + index, kappas, stride=2 * frames_here), :]
        chirped_real = real * cos_ref[...] - imag * sin_ref[...]
        chirped_imag = real * sin_ref[...] + imag * cos_ref[...]
        target = slice(index * beams_here, (index + 1) * beams_here)
        for parity in range(2):
            where = slice(parity * side, (parity + 1) * side)
            both = jnp.concatenate([chirped_real[where], chirped_imag[where]], axis=0)
            turned = both.T
            high = turned.astype(jnp.bfloat16)
            low = (turned - high.astype(jnp.float32)).astype(jnp.bfloat16)
            for sub in range(lane_channels):
                source = slice(sub * beams_here, (sub + 1) * beams_here)
                lanes = slice(sub * 2 * side, (sub + 1) * 2 * side)
                lined[parity, 0, target, lanes] = high[source]
                lined[parity, 1, target, lanes] = low[source]
    sides = []
    for parity in range(2):
        high = lined[parity, 0]
        low = lined[parity, 1]
        fetch_basis[parity].wait()
        sides.append(
            jnp.dot(high, basis[parity, 0], preferred_element_type=jnp.float32)
            + jnp.dot(low, basis[parity, 0], preferred_element_type=jnp.float32)
            + jnp.dot(high, basis[parity, 1], preferred_element_type=jnp.float32)
        )
    times = sides[0].shape[1] // 2
    for part in range(2):
        even = sides[0][:, part * times : (part + 1) * times]
        odd = sides[1][:, part * times : (part + 1) * times]
        for which, value in enumerate((even + odd, (even - odd) * sign)):
            start = (2 * part + which) * times
            out_ref[:, :, start : start + times] = value.reshape(frames_here, beams_here, times)


def make_series(half_index, received, chirp_cos, chirp_sin, basis, beams_here, frames_here):
    in_vmem = pl.BlockSpec(memory_space=pltpu.VMEM)
    anywhere = pl.BlockSpec(memory_space=pl.ANY)
    series = pl.pallas_call(
        functools.partial(series_kernel, beams_here),
        in_specs=[
            pl.BlockSpec(memory_space=pltpu.SMEM), anywhere, in_vmem, in_vmem, anywhere,
        ],
        out_shape=jax.ShapeDtypeStruct(
            (frames_here, beams_here, 2 * basis.shape[3]), jnp.float32
        ),
        scratch_shapes=[
            pltpu.VMEM(received.shape, received.dtype),
            pltpu.VMEM(basis.shape, basis.dtype),
            pltpu.VMEM(received.shape, jnp.float32),
            pltpu.VMEM((2, 2, frames_here * beams_here, basis.shape[2]), jnp.bfloat16),
            pltpu.SemaphoreType.DMA((3,)),
        ],
        compiler_params=pltpu.CompilerParams(vmem_limit_bytes=24 * 1024 * 1024),
        name="series",
    )(half_index, received, chirp_cos, chirp_sin, basis)
    return jnp.transpose(series, (1, 0, 2))


def halves_body(samples, filter_taps, feed_cylinder, feed_delay, pointing, chirp_rate):
    length = filter_taps.shape[1]
    nchan = length // 2
    feed_here = samples.shape[0]
    frames_here = samples.shape[1] // length
    feeds = feed_delay.shape[0]
    beams = pointing.shape[0]
    beams_here = chirp_rate.shape[0]
    near = lax.axis_size("near")
    cores = lax.axis_size("tm")
    group = near * cores
    channels = nchan // group
    half_feeds = feeds // HALVES
    half_beams = beams // HALVES
    layout = (near, cores, channels, frames_here)
    half_index = lax.axis_index("half")
    place = lax.axis_index(GROUP)

    tail = from_behind(samples[:, (frames_here - (TAPS - 1)) * length :], "tm", 1)
    forward = jnp.asarray(folded_forward_basis(length))
    half_scalar = jnp.reshape(half_index, (1,)).astype(jnp.int32)
    spectra = spectra_rows(half_scalar, samples, tail, filter_taps, forward, group)
    spectra = spectra.reshape(group, channels * 2 * frames_here, feed_here)
    received = lax.all_to_all(spectra, GROUP, 0, 0, tiled=True)
    received = received.reshape(-1, feed_here)

    in_parity = group // 2
    first = 2 * (place % in_parity) * channels + (place // in_parity ^ half_index) + 1
    first = jnp.reshape(first, (1,)).astype(jnp.int32)
    code = feed_cylinder * PHASES + feed_delay
    code = lax.dynamic_slice_in_dim(code, half_index * half_feeds, half_feeds)
    code = jnp.broadcast_to(code[:, None], (half_feeds, LANES))
    aim = jnp.transpose(pointing).astype(jnp.float32)
    aims = jnp.stack(
        [
            lax.dynamic_slice_in_dim(aim, half * half_beams, half_beams, 1)
            for half in (1 - half_index, half_index)
        ]
    )
    step = 2
    made = (half_feeds * 3 // 4, half_feeds // 2)
    weights = make_weights(first, code, aims, channels, step, made)
    to_send, lined = partial_beams(
        first, code, aims, weights, made, received, layout, 0, step, jnp.bfloat16
    )
    swap = [
        (half * near + i, (1 - half) * near + (i + near // 2) % near)
        for half in range(HALVES)
        for i in range(near)
    ]
    arrived = lax.ppermute(to_send, ("half", "near"), swap)
    (own,) = partial_beams(
        first, code, aims, weights, made, lined, layout, 1, step, jnp.float32
    )
    gathered = gather_beams(own, arrived, layout, beams_here, 1.0 / math.sqrt(feeds))
    lane_channels = LANES // beams_here
    gathered = gathered.reshape(group, -1, LANES)
    returned = lax.all_to_all(gathered, GROUP, 0, 0, tiled=True).reshape(-1, LANES)

    kappa = jnp.arange(nchan // lane_channels, dtype=jnp.int32)[:, None]
    sub = jnp.arange(LANES, dtype=jnp.int32)[None, :] // beams_here
    side = nchan // lane_channels // 2
    channel = 2 * (lane_channels * (kappa % side) + sub) + (kappa // side ^ half_index)
    position = channel.astype(jnp.float32) / nchan
    rate = jnp.tile(jnp.pi * chirp_rate, lane_channels)[None, :]
    chirp = rate * (position * position)
    inverse = jnp.asarray(folded_inverse_basis(nchan, lane_channels))
    return make_series(
        half_scalar, returned, jnp.cos(chirp), jnp.sin(chirp), inverse, beams_here, frames_here
    )


def solution(mesh):
    feed_size = mesh.shape["feed"]
    wide_enough = FEEDS // feed_size % LANES == 0 and BEAMS // feed_size * 4 == LANES
    if not wide_enough:
        return jax.shard_map(
            plain_body,
            mesh=mesh,
            in_specs=(P("feed", "tm"), P(), P(), P(), P(), P("feed")),
            out_specs=P("feed", "tm", None),
            check_vma=False,
        )
    devices = mesh.devices.reshape(HALVES, feed_size // HALVES, mesh.shape["tm"])
    halved = jax.sharding.Mesh(devices, ("half", "near", "tm"))
    feed = ("half", "near")
    return jax.shard_map(
        halves_body,
        mesh=halved,
        in_specs=(P(feed, "tm"), P(), P(), P(), P(), P(feed)),
        out_specs=P(feed, "tm", None),
        check_vma=False,
    )
```

```python
import functools
import math

import jax
import jax.numpy as jnp
import ml_dtypes
import numpy as np
from jax import lax
from jax.experimental import pallas as pl
from jax.experimental.pallas import tpu as pltpu
from jax.sharding import PartitionSpec as P

FEEDS = 2048
NCHAN = 512
BEAMS = 512
TAPS = 4
CYL = 4
PHASES = 4096


def from_behind(x, axis, by):
    length = lax.axis_size(axis)
    pairs = [(i, i + by) for i in range(length) if 0 <= i + by < length]
    return lax.ppermute(x, axis, pairs)


def forward_basis(length, nchan):
    sample_ids = jnp.arange(length, dtype=jnp.int32)[:, None]
    chan_ids = jnp.arange(nchan, dtype=jnp.int32)[None, :]
    angle = (sample_ids * chan_ids % length).astype(jnp.float32) * (2.0 * math.pi / length)
    scaled = 1.0 / math.sqrt(length)
    return jnp.concatenate([jnp.cos(angle), -jnp.sin(angle)], axis=1) * scaled


def inverse_basis(nchan):
    chan_ids = jnp.arange(nchan, dtype=jnp.int32)[:, None]
    time_ids = jnp.arange(nchan, dtype=jnp.int32)[None, :]
    angle = (chan_ids * time_ids % nchan).astype(jnp.float32) * (2.0 * math.pi / nchan)
    cosine = jnp.cos(angle)
    sine = jnp.sin(angle)
    upper = jnp.concatenate([cosine, sine], axis=1)
    lower = jnp.concatenate([-sine, cosine], axis=1)
    return jnp.concatenate([upper, lower], axis=0) * (1.0 / math.sqrt(nchan))


def spectra_of(frame_block, basis):
    feed_here, batch_frames, length = frame_block.shape
    flat = frame_block.reshape(feed_here * batch_frames, length)
    spectral = jnp.dot(
        flat, basis, precision=lax.Precision.HIGHEST, preferred_element_type=jnp.float32
    )
    spectral = spectral.reshape(feed_here, batch_frames, 2, length // 2)
    return jnp.transpose(spectral, (3, 2, 1, 0)).astype(jnp.bfloat16)


def beamform(turned, steer, feed_delay, first_channel):
    chan_here, _, batch_frames, feeds = turned.shape
    beam_scale = 1.0 / math.sqrt(feeds)

    def one_channel(inputs):
        local, offset = inputs
        channel = first_channel + offset
        turns = (channel + 1) * feed_delay % PHASES
        phase = turns[:, None] * steer % PHASES
        angle = phase.astype(jnp.float32) * (2.0 * math.pi / PHASES)
        w_real = jnp.cos(angle).astype(jnp.bfloat16)
        w_imag = jnp.sin(angle).astype(jnp.bfloat16)
        stacked = local.reshape(2 * batch_frames, feeds)
        with_real = jnp.dot(stacked, w_real, preferred_element_type=jnp.float32)
        with_imag = jnp.dot(stacked, w_imag, preferred_element_type=jnp.float32)
        beam_real = with_real[:batch_frames] - with_imag[batch_frames:]
        beam_imag = with_imag[:batch_frames] + with_real[batch_frames:]
        return (jnp.stack([beam_real, beam_imag]) * beam_scale).astype(jnp.bfloat16)

    offsets = jnp.arange(chan_here, dtype=jnp.int32)
    return lax.map(one_channel, (turned, offsets))


def synthesize(returned, chirp_cos, chirp_sin, basis):
    nchan, _, batch_frames, beams_here = returned.shape
    values = returned.astype(jnp.float32)
    beam_real = values[:, 0]
    beam_imag = values[:, 1]
    chirped_real = beam_real * chirp_cos - beam_imag * chirp_sin
    chirped_imag = beam_real * chirp_sin + beam_imag * chirp_cos
    stacked = jnp.stack([chirped_real, chirped_imag])
    ordered = jnp.transpose(stacked, (3, 2, 0, 1)).reshape(beams_here * batch_frames, 2 * nchan)
    result = jnp.dot(
        ordered, basis, precision=lax.Precision.HIGHEST, preferred_element_type=jnp.float32
    )
    return result.reshape(beams_here, batch_frames, 2 * nchan)


def plain_body(samples, filter_taps, feed_cylinder, feed_delay, pointing, chirp_rate):
    length = 2 * NCHAN
    feed_here = samples.shape[0]
    frames_here = samples.shape[1] // length
    frames = samples.reshape(feed_here, frames_here, length)
    tail = from_behind(frames[:, frames_here - (TAPS - 1) :, :], "tm", 1)
    padded = jnp.concatenate([tail, frames], axis=1).astype(jnp.float32)
    filtered = jnp.zeros((feed_here, frames_here, length), jnp.float32)
    for tap_index in range(TAPS):
        filtered = (
            filtered + filter_taps[tap_index] * padded[:, tap_index : tap_index + frames_here, :]
        )
    basis = forward_basis(length, NCHAN)
    steer = jnp.zeros((FEEDS, BEAMS), jnp.int32)
    for cylinder in range(CYL):
        steer = steer + jnp.where(
            feed_cylinder[:, None] == cylinder, pointing[None, :, cylinder], 0
        )
    chan_here = NCHAN // lax.axis_size("feed")
    first_channel = lax.axis_index("feed") * chan_here
    position = jnp.arange(NCHAN).astype(jnp.float32) / NCHAN
    chirp = (jnp.pi * chirp_rate)[None, :] * (position * position)[:, None]
    chirp_cos = jnp.cos(chirp)[:, None, :]
    chirp_sin = jnp.sin(chirp)[:, None, :]
    back_basis = inverse_basis(NCHAN)
    turned = lax.all_to_all(
        spectra_of(filtered, basis), "feed", split_axis=0, concat_axis=3, tiled=True
    )
    formed = beamform(turned, steer, feed_delay, first_channel)
    returned = lax.all_to_all(formed, "feed", split_axis=3, concat_axis=0, tiled=True)
    series = synthesize(returned, chirp_cos, chirp_sin, back_basis)
    return series


LANES = 128
PHASE_BITS = PHASES.bit_length() - 1
HALVES = 2
GROUP = ("near", "tm")
VMEM = pltpu.CompilerParams(vmem_limit_bytes=56 * 1024 * 1024)


def split_bf16(table):
    high = table.astype(ml_dtypes.bfloat16)
    low = (table - high.astype(np.float64)).astype(ml_dtypes.bfloat16)
    return np.stack([high, low])


def folded_forward_basis(length):
    half = length // 2
    tables = []
    for parity in range(2):
        channel = 2 * np.arange(half // 2)[:, None] + parity
        angle = (channel * np.arange(half)[None, :] % length) * (2.0 * np.pi / length)
        rows = np.concatenate([np.cos(angle), -np.sin(angle)], axis=0) / math.sqrt(length)
        tables.append(split_bf16(rows))
    return np.stack(tables)


def folded_inverse_basis(nchan, lane_channels):
    kappas = nchan // 2 // lane_channels
    times = np.arange(nchan // 2)[None, :]
    tables = []
    for parity in range(2):
        rows = []
        for sub in range(lane_channels):
            channel = 2 * (lane_channels * np.arange(kappas)[:, None] + sub) + parity
            angle = (channel * times % nchan) * (2.0 * np.pi / nchan)
            rows.append(np.concatenate([np.cos(angle), np.sin(angle)], axis=1))
            rows.append(np.concatenate([-np.sin(angle), np.cos(angle)], axis=1))
        tables.append(split_bf16(np.concatenate(rows, axis=0) / math.sqrt(nchan)))
    return np.stack(tables)


def dot_nt(left, right):
    return lax.dot_general(
        left, right, (((1,), (1,)), ((), ())), preferred_element_type=jnp.float32
    )


def spectra_kernel(
    frames_here, group, half_ref, samples_ref, tail_ref, taps_in_ref, basis_ref, out_ref,
    samples, tail, taps_ref, basis, folded, packed, in_sems, out_sems,
):
    feed_here = samples_ref.shape[0]
    length = taps_ref.shape[1]
    half = length // 2
    before = TAPS - 1
    side = half_ref[0]
    sign = (1 - 2 * side).astype(jnp.float32)
    fetch_samples = pltpu.make_async_copy(samples_ref, samples, in_sems.at[0])
    fetch_tail = pltpu.make_async_copy(tail_ref, tail, in_sems.at[1])
    fetch_taps = pltpu.make_async_copy(taps_in_ref, taps_ref, in_sems.at[4])
    fetch_basis = [
        pltpu.make_async_copy(
            basis_ref.at[parity + side * (1 - 2 * parity)], basis.at[parity], in_sems.at[2 + parity]
        )
        for parity in range(2)
    ]
    fetches = [fetch_taps, fetch_samples, fetch_tail] + fetch_basis
    for fetch in fetches:
        fetch.start()
    fetch_taps.wait()
    fetch_samples.wait()

    def frame(index, start):
        if index < 0:
            lanes = pl.ds((index + before) * length + start, LANES)
            return tail[:, lanes].astype(jnp.float32)
        return samples[:, pl.ds(index * length + start, LANES)].astype(jnp.float32)

    def filtered(index, start):
        total = None
        for tap in range(TAPS):
            term = taps_ref[tap : tap + 1, start : start + LANES] * frame(
                index + tap - before, start
            )
            total = term if total is None else total + term
        return total

    for index in list(range(before, frames_here)) + list(range(before)):
        if index == 0:
            fetch_tail.wait()
        where = pl.ds(index * feed_here, feed_here)
        for start in range(0, half, LANES):
            near = filtered(index, start)
            far = filtered(index, start + half) * sign
            for parity, value in enumerate((near + far, near - far)):
                high = value.astype(jnp.bfloat16)
                folded[parity, 0, where, start : start + LANES] = high
                folded[parity, 1, where, start : start + LANES] = (
                    value - high.astype(jnp.float32)
                ).astype(jnp.bfloat16)

    parts = 2 * frames_here
    together = 2
    count = half // 2
    channels = length // 2 // group
    stores = []
    for parity in range(2):
        fetch_basis[parity].wait()
        for first in range(0, frames_here, together):
            where = pl.ds(first * feed_here, together * feed_here)
            high = folded[parity, 0, where, :]
            low = folded[parity, 1, where, :]
            result = (
                dot_nt(basis[parity, 0], high)
                + dot_nt(basis[parity, 1], high)
                + dot_nt(basis[parity, 0], low)
            ).astype(jnp.bfloat16)
            for part in range(2):
                for ahead in range(together):
                    row = part * frames_here + first + ahead
                    for place in range(count // channels):
                        target = (parity * (count // channels) + place) * parts + row
                        source = part * count + place * channels
                        packed[pl.ds(target * channels, channels), :] = result[
                            source : source + channels,
                            ahead * feed_here : (ahead + 1) * feed_here,
                        ]
        block = pl.ds(parity * count * parts, count * parts)
        store = pltpu.make_async_copy(packed.at[block], out_ref.at[block], out_sems.at[parity])
        store.start()
        stores.append(store)
    for store in stores:
        store.wait()


def spectra_rows(half_index, samples, tail, taps, basis, group):
    feed_here = samples.shape[0]
    length = taps.shape[1]
    frames_here = samples.shape[1] // length
    total_rows = length * frames_here
    anywhere = pl.BlockSpec(memory_space=pl.ANY)
    in_hbm = pl.BlockSpec(memory_space=pltpu.HBM)
    return pl.pallas_call(
        functools.partial(spectra_kernel, frames_here, group),
        in_specs=[pl.BlockSpec(memory_space=pltpu.SMEM), in_hbm, anywhere, in_hbm, in_hbm],
        out_specs=anywhere,
        out_shape=jax.ShapeDtypeStruct((total_rows, feed_here), jnp.bfloat16),
        scratch_shapes=[
            pltpu.VMEM(samples.shape, samples.dtype),
            pltpu.VMEM(tail.shape, tail.dtype),
            pltpu.VMEM(taps.shape, taps.dtype),
            pltpu.VMEM(basis.shape, basis.dtype),
            pltpu.VMEM((2, 2, frames_here * feed_here, length // 2), jnp.bfloat16),
            pltpu.VMEM((total_rows, feed_here), jnp.bfloat16),
            pltpu.SemaphoreType.DMA((5,)),
            pltpu.SemaphoreType.DMA((2,)),
        ],
        compiler_params=pltpu.CompilerParams(vmem_limit_bytes=50 * 1024 * 1024),
        name="spectra",
    )(half_index, samples, tail, taps, basis)


def sine_turns(turns):
    square = turns * turns
    total = None
    for power in range(11, 0, -2):
        factor = (2.0 * math.pi) ** power / math.factorial(power) * (-1) ** (power // 2)
        total = factor if total is None else total * square + factor
    return total * turns


def unit_vector(turns):
    cosine = sine_turns(0.25 - jnp.abs(turns))
    sine = sine_turns(jnp.maximum(jnp.minimum(turns, 0.5 - turns), -0.5 - turns))
    return cosine, sine


def centred(turns):
    return turns - jnp.floor(turns + 0.5)


def chain_start(first, channels, step):
    return (first + step * (channels // 2 - 1)).astype(jnp.float32)


def chain_of_weights(first, step, code, pointing_ref, out_ref, where):
    channels, _, width = out_ref.shape
    beams = width // 2
    repeat = beams // LANES
    middle = channels // 2
    cylinder = jnp.concatenate([lax.shift_right_logical(code, PHASE_BITS)] * repeat, axis=1)
    delay = jnp.concatenate([(code & (PHASES - 1)).astype(jnp.float32)] * repeat, axis=1)
    steer = jnp.broadcast_to(pointing_ref[0:1, :], delay.shape)
    for other in range(1, CYL):
        steer = jnp.where(cylinder == other, pointing_ref[other : other + 1, :], steer)
    turns = centred(delay * steer * (1.0 / PHASES))
    low_cos, low_sin = unit_vector(centred(first * turns))
    step_cos, step_sin = unit_vector(centred(float(step) * turns))
    high_cos = low_cos * step_cos - low_sin * step_sin
    high_sin = low_cos * step_sin + low_sin * step_cos
    twice = step_cos + step_cos

    def put(channel, cosine, sine):
        out_ref[channel, where, :beams] = cosine.astype(jnp.bfloat16)
        out_ref[channel, where, beams:] = sine.astype(jnp.bfloat16)

    put(middle - 1, low_cos, low_sin)
    put(middle, high_cos, high_sin)
    up = (low_cos, low_sin, high_cos, high_sin)
    down = (high_cos, high_sin, low_cos, low_sin)
    for away in range(1, middle):
        up = (up[2], up[3], twice * up[2] - up[0], twice * up[3] - up[1])
        down = (down[2], down[3], twice * down[2] - down[0], twice * down[3] - down[1])
        put(middle + away, up[2], up[3])
        put(middle - 1 - away, down[2], down[3])


def weights_kernel(block_rows, step, first_ref, code_ref, pointing_ref, out_ref):
    channels, rows, _ = out_ref.shape
    first = chain_start(first_ref[0], channels, step)

    def one_block(index, carry):
        where = pl.ds(pl.multiple_of(index * block_rows, block_rows), block_rows)
        chain_of_weights(first, step, code_ref[where], pointing_ref.at[0], out_ref, where)
        return carry

    lax.fori_loop(0, rows // block_rows, one_block, 0)


def make_weights(first, code, pointing, channels, step, feeds):
    _, cylinders, beams = pointing.shape
    rows = 256
    tiles = [count // rows for count in feeds]
    return pl.pallas_call(
        functools.partial(weights_kernel, 32, step),
        grid=(sum(tiles),),
        in_specs=[
            pl.BlockSpec(memory_space=pltpu.SMEM),
            pl.BlockSpec((rows, LANES), lambda i: (jnp.where(i < tiles[0], i, i - tiles[0]), 0)),
            pl.BlockSpec((1, cylinders, beams), lambda i: (jnp.where(i < tiles[0], 0, 1), 0, 0)),
        ],
        out_specs=pl.BlockSpec((channels, rows, 2 * beams), lambda i: (0, i, 0)),
        out_shape=jax.ShapeDtypeStruct((channels, sum(feeds), 2 * beams), jnp.bfloat16),
        compiler_params=VMEM,
        cost_estimate=pl.CostEstimate(
            flops=channels * sum(feeds) * beams * 8,
            bytes_accessed=channels * sum(feeds) * beams * 4,
            transcendentals=0,
        ),
        name="weights",
    )(first, code, pointing)


def padded_rows(rows):
    return -(-rows // 16) * 16


def turn_products(both):
    beams = both.shape[1] // 2
    half = both.shape[0] // 2
    by_imag = both[:, beams:]
    return both[:, :beams] + jnp.concatenate([-by_imag[half:], by_imag[:half]], axis=0)


def line_up(layout, arrived, lined, spectra):
    near, cores, channels, frames_here = layout
    per_source = 2 * frames_here
    per_channel = per_source * cores
    spare = spectra.shape[1] - per_channel
    for place in range(near):
        for core in range(cores):
            base = (place * cores + core) * per_source
            for part in range(2):
                for index in range(frames_here):
                    source = (base + part * frames_here + index) * channels
                    target = (part * cores + core) * frames_here + index
                    lined[place, pl.ds(target, channels, stride=per_channel), :] = arrived[
                        pl.ds(source, channels), :
                    ].astype(jnp.float32)
    blank = jnp.zeros((spare, arrived.shape[1]), jnp.float32)
    for channel in range(channels):
        rows = slice(channel * per_channel, (channel + 1) * per_channel)
        blocks = [
            jnp.concatenate([lined[place, rows, :], blank], axis=0) for place in range(near)
        ]
        spectra[channel] = jnp.concatenate(blocks, axis=1).astype(jnp.bfloat16)


def beams_kernel(
    layout, which, step, pieces, skipped, base, first_ref, code_ref, pointing_ref, weights_ref, spectra_ref,
    *rest,
):
    _, cores, _, frames_here = layout
    per_channel = 2 * frames_here * cores
    raw = base is None
    if raw:
        out_ref, spectra_out_ref, *rest = rest
    else:
        out_ref, *rest = rest
    stored, own, total, code, spectra, extra_sems, sems, *rest = rest
    if raw:
        arrived, lined = rest
    channels, made_feeds, _ = stored.shape
    here = pl.ds(base or 0, channels)
    if raw:
        fetch = pltpu.make_async_copy(spectra_ref, arrived, extra_sems.at[0])
    else:
        fetch = pltpu.make_async_copy(spectra_ref.at[here], spectra, extra_sems.at[0])
    own_rows = own.shape[1]
    fetch_code = pltpu.make_async_copy(
        code_ref.at[pl.ds(made_feeds, own_rows)], code, extra_sems.at[1]
    )
    fetch_code.start()
    fetch.start()
    count = channels // pieces
    copies = []
    for piece in range(pieces):
        place = pl.ds(piece * count, count)
        there = pl.ds((base or 0) + piece * count, count)
        source = weights_ref.at[there, pl.ds(skipped, made_feeds)]
        copies.append(pltpu.make_async_copy(source, stored.at[place], sems.at[piece]))
    ahead = min(5, pieces)
    soon = ahead if raw else 2
    for copy in copies[:soon]:
        copy.start()

    block_rows = 32
    first = chain_start(first_ref[0] + step * (base or 0), channels, step)

    def one_block(index, carry):
        target = pl.ds(pl.multiple_of(index * block_rows, block_rows), block_rows)
        chain_of_weights(first, step, code[target], pointing_ref.at[which], own, target)
        return carry

    fetch_code.wait()
    lax.fori_loop(0, own_rows // block_rows, one_block, 0)
    fetch.wait()
    for copy in copies[soon:ahead]:
        copy.start()
    if raw:
        line_up(layout, arrived, lined, spectra)
        keep = pltpu.make_async_copy(spectra, spectra_out_ref, extra_sems.at[2])
        keep.start()

    for channel in range(channels):
        rows = slice(channel * per_channel, (channel + 1) * per_channel)
        total[rows, :] = jnp.dot(
            spectra[channel, :, made_feeds:], own[channel], preferred_element_type=jnp.float32
        )[:per_channel]
    for piece in range(pieces):
        copies[piece].wait()
        if piece + ahead < pieces:
            copies[piece + ahead].start()
        for channel in range(piece * count, (piece + 1) * count):
            rows = slice(channel * per_channel, (channel + 1) * per_channel)
            both = jnp.dot(
                spectra[channel, :, :made_feeds],
                stored[channel],
                preferred_element_type=jnp.float32,
            )[:per_channel]
            out_ref[rows, :] = turn_products(total[rows, :] + both).astype(out_ref.dtype)
    if raw:
        keep.wait()


def partial_beams(
    first, code, pointing, weights, made, spectra, layout, which, channels, base, step, dtype
):
    near, cores, all_channels, frames_here = layout
    feeds = code.shape[0]
    made_feeds = made[which]
    width = weights.shape[2]
    per_channel = 2 * cores * frames_here
    pieces = channels // 4
    raw = base is None
    lined_channels = all_channels if raw else channels
    in_vmem = pl.BlockSpec(memory_space=pltpu.VMEM)
    lined_shape = (lined_channels, padded_rows(per_channel), feeds)
    out_shape = [jax.ShapeDtypeStruct((channels * per_channel, width // 2), dtype)]
    scratch = [
        pltpu.VMEM((channels, made_feeds, width), weights.dtype),
        pltpu.VMEM((channels, feeds - made_feeds, width), weights.dtype),
        pltpu.VMEM((channels * per_channel, width), jnp.float32),
        pltpu.VMEM((feeds - made_feeds, LANES), code.dtype),
        pltpu.VMEM(lined_shape, jnp.bfloat16),
        pltpu.SemaphoreType.DMA((3,)),
        pltpu.SemaphoreType.DMA((pieces,)),
    ]
    if raw:
        out_shape.append(jax.ShapeDtypeStruct(lined_shape, jnp.bfloat16))
        scratch += [
            pltpu.VMEM(spectra.shape, spectra.dtype),
            pltpu.VMEM((near, all_channels * per_channel, feeds // near), jnp.float32),
        ]
    return pl.pallas_call(
        functools.partial(beams_kernel, layout, which, step, pieces, sum(made[:which]), base),
        in_specs=[
            pl.BlockSpec(memory_space=pltpu.SMEM),
            pl.BlockSpec(memory_space=pltpu.HBM),
            in_vmem,
            pl.BlockSpec(memory_space=pltpu.HBM),
            pl.BlockSpec(memory_space=pl.ANY if raw else pltpu.HBM),
        ],
        out_specs=[in_vmem, pl.BlockSpec(memory_space=pltpu.HBM)][: len(out_shape)],
        out_shape=out_shape,
        scratch_shapes=scratch,
        compiler_params=pltpu.CompilerParams(vmem_limit_bytes=50 * 1024 * 1024),
        cost_estimate=pl.CostEstimate(
            flops=(1 - which) * channels * feeds * width * 2 * 128 + 1,
            bytes_accessed=(1 - which) * channels * feeds * width * 2 + 1,
            transcendentals=0,
        ),
        name="beams",
    )(first, code, pointing, weights, spectra)


def gather_kernel(
    layout, beams_here, scale, own_ref, early_ref, late_ref, out_ref, own, other, total, rows, sems
):
    near, cores, channels, frames_here = layout
    lane_channels = LANES // beams_here
    per_core = 2 * frames_here
    per_channel = per_core * cores
    groups = channels // lane_channels
    fetches = [
        pltpu.make_async_copy(own_ref, own, sems.at[0]),
        pltpu.make_async_copy(early_ref, other.at[pl.ds(0, early_ref.shape[0])], sems.at[1]),
        pltpu.make_async_copy(
            late_ref, other.at[pl.ds(early_ref.shape[0], late_ref.shape[0])], sems.at[2]
        ),
    ]
    for fetch in fetches:
        fetch.start()
    for fetch in fetches:
        fetch.wait()
    total[...] = (own[...] + other[...].astype(jnp.float32)) * scale
    for group in range(groups):
        values = [
            total[pl.ds((group * lane_channels + sub) * per_channel, per_channel), :]
            for sub in range(lane_channels)
        ]
        for place in range(near):
            lanes = slice(place * beams_here, (place + 1) * beams_here)
            tile = jnp.concatenate([value[:, lanes] for value in values], axis=1)
            for core in range(cores):
                start = ((place * cores + core) * groups + group) * per_core
                for part in range(2):
                    source = (part * cores + core) * frames_here
                    rows[pl.ds(start + part * frames_here, frames_here), :] = tile[
                        source : source + frames_here
                    ]
    out_ref[...] = rows[...].astype(jnp.bfloat16)


def gather_beams(own, early, late, layout, beams_here, scale):
    near, cores, channels, frames_here = layout
    total_rows = near * cores * channels // (LANES // beams_here) * 2 * frames_here
    return pl.pallas_call(
        functools.partial(gather_kernel, layout, beams_here, scale),
        in_specs=[pl.BlockSpec(memory_space=pltpu.HBM)] + [pl.BlockSpec(memory_space=pl.ANY)] * 2,
        out_shape=jax.ShapeDtypeStruct((total_rows, LANES), jnp.bfloat16),
        scratch_shapes=[
            pltpu.VMEM(own.shape, own.dtype),
            pltpu.VMEM(own.shape, early.dtype),
            pltpu.VMEM(own.shape, jnp.float32),
            pltpu.VMEM((total_rows, LANES), jnp.float32),
            pltpu.SemaphoreType.DMA((3,)),
        ],
        compiler_params=pltpu.CompilerParams(vmem_limit_bytes=16 * 1024 * 1024),
        name="gather",
    )(own, early, late)


def series_kernel(
    beams_here, half_ref, received_ref, cos_ref, sin_ref, basis_ref, out_ref,
    arrived, basis, wide, lined, sems,
):
    frames_here = out_ref.shape[0]
    kappas = cos_ref.shape[0]
    lane_channels = LANES // beams_here
    side = kappas // 2
    half = half_ref[0]
    sign = (1 - 2 * half).astype(jnp.float32)
    fetch = pltpu.make_async_copy(received_ref, arrived, sems.at[2])
    fetch.start()
    fetch_basis = [
        pltpu.make_async_copy(
            basis_ref.at[parity + half * (1 - 2 * parity)], basis.at[parity], sems.at[parity]
        )
        for parity in range(2)
    ]
    for copy in fetch_basis:
        copy.start()
    fetch.wait()
    wide[...] = arrived[...].astype(jnp.float32)
    for index in range(frames_here):
        real = wide[pl.ds(index, kappas, stride=2 * frames_here), :]
        imag = wide[pl.ds(frames_here + index, kappas, stride=2 * frames_here), :]
        chirped_real = real * cos_ref[...] - imag * sin_ref[...]
        chirped_imag = real * sin_ref[...] + imag * cos_ref[...]
        target = slice(index * beams_here, (index + 1) * beams_here)
        for parity in range(2):
            where = slice(parity * side, (parity + 1) * side)
            both = jnp.concatenate([chirped_real[where], chirped_imag[where]], axis=0)
            turned = both.T
            high = turned.astype(jnp.bfloat16)
            low = (turned - high.astype(jnp.float32)).astype(jnp.bfloat16)
            for sub in range(lane_channels):
                source = slice(sub * beams_here, (sub + 1) * beams_here)
                lanes = slice(sub * 2 * side, (sub + 1) * 2 * side)
                lined[parity, 0, target, lanes] = high[source]
                lined[parity, 1, target, lanes] = low[source]
    sides = []
    for parity in range(2):
        high = lined[parity, 0]
        low = lined[parity, 1]
        fetch_basis[parity].wait()
        sides.append(
            jnp.dot(high, basis[parity, 0], preferred_element_type=jnp.float32)
            + jnp.dot(low, basis[parity, 0], preferred_element_type=jnp.float32)
            + jnp.dot(high, basis[parity, 1], preferred_element_type=jnp.float32)
        )
    times = sides[0].shape[1] // 2
    for part in range(2):
        even = sides[0][:, part * times : (part + 1) * times]
        odd = sides[1][:, part * times : (part + 1) * times]
        for which, value in enumerate((even + odd, (even - odd) * sign)):
            start = (2 * part + which) * times
            out_ref[:, :, start : start + times] = value.reshape(frames_here, beams_here, times)


def make_series(half_index, received, chirp_cos, chirp_sin, basis, beams_here, frames_here):
    in_vmem = pl.BlockSpec(memory_space=pltpu.VMEM)
    anywhere = pl.BlockSpec(memory_space=pl.ANY)
    series = pl.pallas_call(
        functools.partial(series_kernel, beams_here),
        in_specs=[
            pl.BlockSpec(memory_space=pltpu.SMEM), anywhere, in_vmem, in_vmem, anywhere,
        ],
        out_shape=jax.ShapeDtypeStruct(
            (frames_here, beams_here, 2 * basis.shape[3]), jnp.float32
        ),
        scratch_shapes=[
            pltpu.VMEM(received.shape, received.dtype),
            pltpu.VMEM(basis.shape, basis.dtype),
            pltpu.VMEM(received.shape, jnp.float32),
            pltpu.VMEM((2, 2, frames_here * beams_here, basis.shape[2]), jnp.bfloat16),
            pltpu.SemaphoreType.DMA((3,)),
        ],
        compiler_params=pltpu.CompilerParams(vmem_limit_bytes=24 * 1024 * 1024),
        name="series",
    )(half_index, received, chirp_cos, chirp_sin, basis)
    return jnp.transpose(series, (1, 0, 2))


def halves_body(samples, filter_taps, feed_cylinder, feed_delay, pointing, chirp_rate):
    length = filter_taps.shape[1]
    nchan = length // 2
    feed_here = samples.shape[0]
    frames_here = samples.shape[1] // length
    feeds = feed_delay.shape[0]
    beams = pointing.shape[0]
    beams_here = chirp_rate.shape[0]
    near = lax.axis_size("near")
    cores = lax.axis_size("tm")
    group = near * cores
    channels = nchan // group
    half_feeds = feeds // HALVES
    half_beams = beams // HALVES
    layout = (near, cores, channels, frames_here)
    half_index = lax.axis_index("half")
    place = lax.axis_index(GROUP)

    tail = from_behind(samples[:, (frames_here - (TAPS - 1)) * length :], "tm", 1)
    forward = jnp.asarray(folded_forward_basis(length))
    half_scalar = jnp.reshape(half_index, (1,)).astype(jnp.int32)
    spectra = spectra_rows(half_scalar, samples, tail, filter_taps, forward, group)
    spectra = spectra.reshape(group, channels * 2 * frames_here, feed_here)
    received = lax.all_to_all(spectra, GROUP, 0, 0, tiled=True)
    received = received.reshape(-1, feed_here)

    in_parity = group // 2
    first = 2 * (place % in_parity) * channels + (place // in_parity ^ half_index) + 1
    first = jnp.reshape(first, (1,)).astype(jnp.int32)
    code = feed_cylinder * PHASES + feed_delay
    code = lax.dynamic_slice_in_dim(code, half_index * half_feeds, half_feeds)
    code = jnp.broadcast_to(code[:, None], (half_feeds, LANES))
    aim = jnp.transpose(pointing).astype(jnp.float32)
    aims = jnp.stack(
        [
            lax.dynamic_slice_in_dim(aim, half * half_beams, half_beams, 1)
            for half in (1 - half_index, half_index)
        ]
    )
    step = 2
    made = (half_feeds * 3 // 4, half_feeds * 3 // 4)
    weights = make_weights(first, code, aims, channels, step, made)
    swap = [
        (half * near + i, (1 - half) * near + (i + near // 2) % near)
        for half in range(HALVES)
        for i in range(near)
    ]
    common = (first, code, aims, weights, made)
    piece = channels * 5 // 8
    early, lined = partial_beams(
        *common, received, layout, 0, piece, None, step, jnp.bfloat16
    )
    early = lax.ppermute(early, ("half", "near"), swap)
    (late,) = partial_beams(
        *common, lined, layout, 0, channels - piece, piece, step, jnp.bfloat16
    )
    late = lax.ppermute(late, ("half", "near"), swap)
    (own,) = partial_beams(*common, lined, layout, 1, channels, 0, step, jnp.float32)
    gathered = gather_beams(own, early, late, layout, beams_here, 1.0 / math.sqrt(feeds))
    lane_channels = LANES // beams_here
    gathered = gathered.reshape(group, -1, LANES)
    returned = lax.all_to_all(gathered, GROUP, 0, 0, tiled=True).reshape(-1, LANES)

    kappa = jnp.arange(nchan // lane_channels, dtype=jnp.int32)[:, None]
    sub = jnp.arange(LANES, dtype=jnp.int32)[None, :] // beams_here
    side = nchan // lane_channels // 2
    channel = 2 * (lane_channels * (kappa % side) + sub) + (kappa // side ^ half_index)
    position = channel.astype(jnp.float32) / nchan
    rate = jnp.tile(jnp.pi * chirp_rate, lane_channels)[None, :]
    chirp = rate * (position * position)
    inverse = jnp.asarray(folded_inverse_basis(nchan, lane_channels))
    return make_series(
        half_scalar, returned, jnp.cos(chirp), jnp.sin(chirp), inverse, beams_here, frames_here
    )


def solution(mesh):
    feed_size = mesh.shape["feed"]
    wide_enough = FEEDS // feed_size % LANES == 0 and BEAMS // feed_size * 4 == LANES
    if not wide_enough:
        return jax.shard_map(
            plain_body,
            mesh=mesh,
            in_specs=(P("feed", "tm"), P(), P(), P(), P(), P("feed")),
            out_specs=P("feed", "tm", None),
            check_vma=False,
        )
    devices = mesh.devices.reshape(HALVES, feed_size // HALVES, mesh.shape["tm"])
    halved = jax.sharding.Mesh(devices, ("half", "near", "tm"))
    feed = ("half", "near")
    return jax.shard_map(
        halves_body,
        mesh=halved,
        in_specs=(P(feed, "tm"), P(), P(), P(), P(), P(feed)),
        out_specs=P(feed, "tm", None),
        check_vma=False,
    )
```

```python
import functools
import math

import jax
import jax.numpy as jnp
import ml_dtypes
import numpy as np
from jax import lax
from jax.experimental import pallas as pl
from jax.experimental.pallas import tpu as pltpu
from jax.sharding import PartitionSpec as P

FEEDS = 2048
NCHAN = 512
BEAMS = 512
TAPS = 4
CYL = 4
PHASES = 4096


def from_behind(x, axis, by):
    length = lax.axis_size(axis)
    pairs = [(i, i + by) for i in range(length) if 0 <= i + by < length]
    return lax.ppermute(x, axis, pairs)


def forward_basis(length, nchan):
    sample_ids = jnp.arange(length, dtype=jnp.int32)[:, None]
    chan_ids = jnp.arange(nchan, dtype=jnp.int32)[None, :]
    angle = (sample_ids * chan_ids % length).astype(jnp.float32) * (2.0 * math.pi / length)
    scaled = 1.0 / math.sqrt(length)
    return jnp.concatenate([jnp.cos(angle), -jnp.sin(angle)], axis=1) * scaled


def inverse_basis(nchan):
    chan_ids = jnp.arange(nchan, dtype=jnp.int32)[:, None]
    time_ids = jnp.arange(nchan, dtype=jnp.int32)[None, :]
    angle = (chan_ids * time_ids % nchan).astype(jnp.float32) * (2.0 * math.pi / nchan)
    cosine = jnp.cos(angle)
    sine = jnp.sin(angle)
    upper = jnp.concatenate([cosine, sine], axis=1)
    lower = jnp.concatenate([-sine, cosine], axis=1)
    return jnp.concatenate([upper, lower], axis=0) * (1.0 / math.sqrt(nchan))


def spectra_of(frame_block, basis):
    feed_here, batch_frames, length = frame_block.shape
    flat = frame_block.reshape(feed_here * batch_frames, length)
    spectral = jnp.dot(
        flat, basis, precision=lax.Precision.HIGHEST, preferred_element_type=jnp.float32
    )
    spectral = spectral.reshape(feed_here, batch_frames, 2, length // 2)
    return jnp.transpose(spectral, (3, 2, 1, 0)).astype(jnp.bfloat16)


def beamform(turned, steer, feed_delay, first_channel):
    chan_here, _, batch_frames, feeds = turned.shape
    beam_scale = 1.0 / math.sqrt(feeds)

    def one_channel(inputs):
        local, offset = inputs
        channel = first_channel + offset
        turns = (channel + 1) * feed_delay % PHASES
        phase = turns[:, None] * steer % PHASES
        angle = phase.astype(jnp.float32) * (2.0 * math.pi / PHASES)
        w_real = jnp.cos(angle).astype(jnp.bfloat16)
        w_imag = jnp.sin(angle).astype(jnp.bfloat16)
        stacked = local.reshape(2 * batch_frames, feeds)
        with_real = jnp.dot(stacked, w_real, preferred_element_type=jnp.float32)
        with_imag = jnp.dot(stacked, w_imag, preferred_element_type=jnp.float32)
        beam_real = with_real[:batch_frames] - with_imag[batch_frames:]
        beam_imag = with_imag[:batch_frames] + with_real[batch_frames:]
        return (jnp.stack([beam_real, beam_imag]) * beam_scale).astype(jnp.bfloat16)

    offsets = jnp.arange(chan_here, dtype=jnp.int32)
    return lax.map(one_channel, (turned, offsets))


def synthesize(returned, chirp_cos, chirp_sin, basis):
    nchan, _, batch_frames, beams_here = returned.shape
    values = returned.astype(jnp.float32)
    beam_real = values[:, 0]
    beam_imag = values[:, 1]
    chirped_real = beam_real * chirp_cos - beam_imag * chirp_sin
    chirped_imag = beam_real * chirp_sin + beam_imag * chirp_cos
    stacked = jnp.stack([chirped_real, chirped_imag])
    ordered = jnp.transpose(stacked, (3, 2, 0, 1)).reshape(beams_here * batch_frames, 2 * nchan)
    result = jnp.dot(
        ordered, basis, precision=lax.Precision.HIGHEST, preferred_element_type=jnp.float32
    )
    return result.reshape(beams_here, batch_frames, 2 * nchan)


def plain_body(samples, filter_taps, feed_cylinder, feed_delay, pointing, chirp_rate):
    length = 2 * NCHAN
    feed_here = samples.shape[0]
    frames_here = samples.shape[1] // length
    frames = samples.reshape(feed_here, frames_here, length)
    tail = from_behind(frames[:, frames_here - (TAPS - 1) :, :], "tm", 1)
    padded = jnp.concatenate([tail, frames], axis=1).astype(jnp.float32)
    filtered = jnp.zeros((feed_here, frames_here, length), jnp.float32)
    for tap_index in range(TAPS):
        filtered = (
            filtered + filter_taps[tap_index] * padded[:, tap_index : tap_index + frames_here, :]
        )
    basis = forward_basis(length, NCHAN)
    steer = jnp.zeros((FEEDS, BEAMS), jnp.int32)
    for cylinder in range(CYL):
        steer = steer + jnp.where(
            feed_cylinder[:, None] == cylinder, pointing[None, :, cylinder], 0
        )
    chan_here = NCHAN // lax.axis_size("feed")
    first_channel = lax.axis_index("feed") * chan_here
    position = jnp.arange(NCHAN).astype(jnp.float32) / NCHAN
    chirp = (jnp.pi * chirp_rate)[None, :] * (position * position)[:, None]
    chirp_cos = jnp.cos(chirp)[:, None, :]
    chirp_sin = jnp.sin(chirp)[:, None, :]
    back_basis = inverse_basis(NCHAN)
    turned = lax.all_to_all(
        spectra_of(filtered, basis), "feed", split_axis=0, concat_axis=3, tiled=True
    )
    formed = beamform(turned, steer, feed_delay, first_channel)
    returned = lax.all_to_all(formed, "feed", split_axis=3, concat_axis=0, tiled=True)
    series = synthesize(returned, chirp_cos, chirp_sin, back_basis)
    return series


LANES = 128
PHASE_BITS = PHASES.bit_length() - 1
HALVES = 2
GROUP = ("near", "tm")
VMEM = pltpu.CompilerParams(vmem_limit_bytes=56 * 1024 * 1024)


def split_bf16(table):
    high = table.astype(ml_dtypes.bfloat16)
    low = (table - high.astype(np.float64)).astype(ml_dtypes.bfloat16)
    return np.stack([high, low])


def folded_forward_basis(length):
    half = length // 2
    tables = []
    for parity in range(2):
        channel = 2 * np.arange(half // 2)[:, None] + parity
        angle = (channel * np.arange(half)[None, :] % length) * (2.0 * np.pi / length)
        rows = np.concatenate([np.cos(angle), -np.sin(angle)], axis=0) / math.sqrt(length)
        tables.append(split_bf16(rows))
    return np.stack(tables)


def folded_inverse_basis(nchan, lane_channels):
    kappas = nchan // 2 // lane_channels
    times = np.arange(nchan // 2)[None, :]
    tables = []
    for parity in range(2):
        rows = []
        for sub in range(lane_channels):
            channel = 2 * (lane_channels * np.arange(kappas)[:, None] + sub) + parity
            angle = (channel * times % nchan) * (2.0 * np.pi / nchan)
            rows.append(np.concatenate([np.cos(angle), np.sin(angle)], axis=1))
            rows.append(np.concatenate([-np.sin(angle), np.cos(angle)], axis=1))
        tables.append(split_bf16(np.concatenate(rows, axis=0) / math.sqrt(nchan)))
    return np.stack(tables)


def dot_nt(left, right):
    return lax.dot_general(
        left, right, (((1,), (1,)), ((), ())), preferred_element_type=jnp.float32
    )


def spectra_kernel(
    frames_here, group, half_ref, samples_ref, tail_ref, taps_in_ref, basis_ref, out_ref,
    samples, tail, taps_ref, basis, folded, packed, in_sems, out_sems,
):
    feed_here = samples_ref.shape[0]
    length = taps_ref.shape[1]
    half = length // 2
    before = TAPS - 1
    side = half_ref[0]
    sign = (1 - 2 * side).astype(jnp.float32)
    fetch_samples = pltpu.make_async_copy(samples_ref, samples, in_sems.at[0])
    fetch_tail = pltpu.make_async_copy(tail_ref, tail, in_sems.at[1])
    fetch_taps = pltpu.make_async_copy(taps_in_ref, taps_ref, in_sems.at[4])
    fetch_basis = [
        pltpu.make_async_copy(
            basis_ref.at[parity + side * (1 - 2 * parity)], basis.at[parity], in_sems.at[2 + parity]
        )
        for parity in range(2)
    ]
    fetches = [fetch_taps, fetch_samples, fetch_tail] + fetch_basis
    for fetch in fetches:
        fetch.start()
    fetch_taps.wait()
    fetch_samples.wait()

    def frame(index, start):
        if index < 0:
            lanes = pl.ds((index + before) * length + start, LANES)
            return tail[:, lanes].astype(jnp.float32)
        return samples[:, pl.ds(index * length + start, LANES)].astype(jnp.float32)

    def filtered(index, start):
        total = None
        for tap in range(TAPS):
            term = taps_ref[tap : tap + 1, start : start + LANES] * frame(
                index + tap - before, start
            )
            total = term if total is None else total + term
        return total

    for index in list(range(before, frames_here)) + list(range(before)):
        if index == 0:
            fetch_tail.wait()
        where = pl.ds(index * feed_here, feed_here)
        for start in range(0, half, LANES):
            near = filtered(index, start)
            far = filtered(index, start + half) * sign
            for parity, value in enumerate((near + far, near - far)):
                high = value.astype(jnp.bfloat16)
                folded[parity, 0, where, start : start + LANES] = high
                folded[parity, 1, where, start : start + LANES] = (
                    value - high.astype(jnp.float32)
                ).astype(jnp.bfloat16)

    parts = 2 * frames_here
    together = 2
    count = half // 2
    channels = length // 2 // group
    stores = []
    for parity in range(2):
        fetch_basis[parity].wait()
        for first in range(0, frames_here, together):
            where = pl.ds(first * feed_here, together * feed_here)
            high = folded[parity, 0, where, :]
            low = folded[parity, 1, where, :]
            result = (
                dot_nt(basis[parity, 0], high)
                + dot_nt(basis[parity, 1], high)
                + dot_nt(basis[parity, 0], low)
            ).astype(jnp.bfloat16)
            for part in range(2):
                for ahead in range(together):
                    row = part * frames_here + first + ahead
                    for place in range(count // channels):
                        target = (parity * (count // channels) + place) * parts + row
                        source = part * count + place * channels
                        packed[pl.ds(target * channels, channels), :] = result[
                            source : source + channels,
                            ahead * feed_here : (ahead + 1) * feed_here,
                        ]
        block = pl.ds(parity * count * parts, count * parts)
        store = pltpu.make_async_copy(packed.at[block], out_ref.at[block], out_sems.at[parity])
        store.start()
        stores.append(store)
    for store in stores:
        store.wait()


def spectra_rows(half_index, samples, tail, taps, basis, group):
    feed_here = samples.shape[0]
    length = taps.shape[1]
    frames_here = samples.shape[1] // length
    total_rows = length * frames_here
    anywhere = pl.BlockSpec(memory_space=pl.ANY)
    in_hbm = pl.BlockSpec(memory_space=pltpu.HBM)
    return pl.pallas_call(
        functools.partial(spectra_kernel, frames_here, group),
        in_specs=[pl.BlockSpec(memory_space=pltpu.SMEM), in_hbm, anywhere, in_hbm, in_hbm],
        out_specs=anywhere,
        out_shape=jax.ShapeDtypeStruct((total_rows, feed_here), jnp.bfloat16),
        scratch_shapes=[
            pltpu.VMEM(samples.shape, samples.dtype),
            pltpu.VMEM(tail.shape, tail.dtype),
            pltpu.VMEM(taps.shape, taps.dtype),
            pltpu.VMEM(basis.shape, basis.dtype),
            pltpu.VMEM((2, 2, frames_here * feed_here, length // 2), jnp.bfloat16),
            pltpu.VMEM((total_rows, feed_here), jnp.bfloat16),
            pltpu.SemaphoreType.DMA((5,)),
            pltpu.SemaphoreType.DMA((2,)),
        ],
        compiler_params=pltpu.CompilerParams(vmem_limit_bytes=50 * 1024 * 1024),
        name="spectra",
    )(half_index, samples, tail, taps, basis)


def sine_turns(turns):
    square = turns * turns
    total = None
    for power in range(11, 0, -2):
        factor = (2.0 * math.pi) ** power / math.factorial(power) * (-1) ** (power // 2)
        total = factor if total is None else total * square + factor
    return total * turns


def unit_vector(turns):
    cosine = sine_turns(0.25 - jnp.abs(turns))
    sine = sine_turns(jnp.maximum(jnp.minimum(turns, 0.5 - turns), -0.5 - turns))
    return cosine, sine


def centred(turns):
    return turns - jnp.floor(turns + 0.5)


def chain_start(first, channels, step):
    return (first + step * (channels // 2 - 1)).astype(jnp.float32)


def chain_of_weights(first, step, code, pointing_ref, out_ref, where):
    channels, _, width = out_ref.shape
    beams = width // 2
    repeat = beams // LANES
    middle = channels // 2
    cylinder = jnp.concatenate([lax.shift_right_logical(code, PHASE_BITS)] * repeat, axis=1)
    delay = jnp.concatenate([(code & (PHASES - 1)).astype(jnp.float32)] * repeat, axis=1)
    steer = jnp.broadcast_to(pointing_ref[0:1, :], delay.shape)
    for other in range(1, CYL):
        steer = jnp.where(cylinder == other, pointing_ref[other : other + 1, :], steer)
    turns = centred(delay * steer * (1.0 / PHASES))
    low_cos, low_sin = unit_vector(centred(first * turns))
    step_cos, step_sin = unit_vector(centred(float(step) * turns))
    high_cos = low_cos * step_cos - low_sin * step_sin
    high_sin = low_cos * step_sin + low_sin * step_cos
    twice = step_cos + step_cos

    def put(channel, cosine, sine):
        out_ref[channel, where, :beams] = cosine.astype(jnp.bfloat16)
        out_ref[channel, where, beams:] = sine.astype(jnp.bfloat16)

    put(middle - 1, low_cos, low_sin)
    put(middle, high_cos, high_sin)
    up = (low_cos, low_sin, high_cos, high_sin)
    down = (high_cos, high_sin, low_cos, low_sin)
    for away in range(1, middle):
        up = (up[2], up[3], twice * up[2] - up[0], twice * up[3] - up[1])
        down = (down[2], down[3], twice * down[2] - down[0], twice * down[3] - down[1])
        put(middle + away, up[2], up[3])
        put(middle - 1 - away, down[2], down[3])


def weights_kernel(block_rows, step, first_ref, code_ref, pointing_ref, out_ref):
    channels, rows, _ = out_ref.shape
    first = chain_start(first_ref[0], channels, step)

    def one_block(index, carry):
        where = pl.ds(pl.multiple_of(index * block_rows, block_rows), block_rows)
        chain_of_weights(first, step, code_ref[where], pointing_ref.at[0], out_ref, where)
        return carry

    lax.fori_loop(0, rows // block_rows, one_block, 0)


def make_weights(first, code, pointing, channels, step, feeds):
    _, cylinders, beams = pointing.shape
    rows = 256
    tiles = [count // rows for count in feeds]
    return pl.pallas_call(
        functools.partial(weights_kernel, 32, step),
        grid=(sum(tiles),),
        in_specs=[
            pl.BlockSpec(memory_space=pltpu.SMEM),
            pl.BlockSpec((rows, LANES), lambda i: (jnp.where(i < tiles[0], i, i - tiles[0]), 0)),
            pl.BlockSpec((1, cylinders, beams), lambda i: (jnp.where(i < tiles[0], 0, 1), 0, 0)),
        ],
        out_specs=pl.BlockSpec((channels, rows, 2 * beams), lambda i: (0, i, 0)),
        out_shape=jax.ShapeDtypeStruct((channels, sum(feeds), 2 * beams), jnp.bfloat16),
        compiler_params=VMEM,
        cost_estimate=pl.CostEstimate(
            flops=channels * sum(feeds) * beams * 8,
            bytes_accessed=channels * sum(feeds) * beams * 4,
            transcendentals=0,
        ),
        name="weights",
    )(first, code, pointing)


def padded_rows(rows):
    return -(-rows // 16) * 16


def turn_products(both):
    beams = both.shape[1] // 2
    half = both.shape[0] // 2
    by_imag = both[:, beams:]
    return both[:, :beams] + jnp.concatenate([-by_imag[half:], by_imag[:half]], axis=0)


def line_up(layout, arrived, lined, spectra):
    near, cores, channels, frames_here = layout
    per_source = 2 * frames_here
    per_channel = per_source * cores
    spare = spectra.shape[1] - per_channel
    for place in range(near):
        for core in range(cores):
            base = (place * cores + core) * per_source
            for part in range(2):
                for index in range(frames_here):
                    source = (base + part * frames_here + index) * channels
                    target = (part * cores + core) * frames_here + index
                    lined[place, pl.ds(target, channels, stride=per_channel), :] = arrived[
                        pl.ds(source, channels), :
                    ].astype(jnp.float32)
    blank = jnp.zeros((spare, arrived.shape[1]), jnp.float32)
    for channel in range(channels):
        rows = slice(channel * per_channel, (channel + 1) * per_channel)
        blocks = [
            jnp.concatenate([lined[place, rows, :], blank], axis=0) for place in range(near)
        ]
        spectra[channel] = jnp.concatenate(blocks, axis=1).astype(jnp.bfloat16)


def beams_kernel(
    layout, which, step, pieces, skipped, base, first_ref, code_ref, pointing_ref, weights_ref, spectra_ref,
    *rest,
):
    _, cores, _, frames_here = layout
    per_channel = 2 * frames_here * cores
    raw = base is None
    if raw:
        out_ref, spectra_out_ref, *rest = rest
    else:
        out_ref, *rest = rest
    stored, own, total, code, spectra, extra_sems, sems, *rest = rest
    if raw:
        arrived, lined = rest
    channels, made_feeds, _ = stored.shape
    here = pl.ds(base or 0, channels)
    if raw:
        fetch = pltpu.make_async_copy(spectra_ref, arrived, extra_sems.at[0])
    else:
        fetch = pltpu.make_async_copy(spectra_ref.at[here], spectra, extra_sems.at[0])
    own_rows = own.shape[1]
    fetch_code = pltpu.make_async_copy(
        code_ref.at[pl.ds(made_feeds, own_rows)], code, extra_sems.at[1]
    )
    fetch_code.start()
    fetch.start()
    count = channels // pieces
    copies = []
    for piece in range(pieces):
        place = pl.ds(piece * count, count)
        there = pl.ds((base or 0) + piece * count, count)
        source = weights_ref.at[there, pl.ds(skipped, made_feeds)]
        copies.append(pltpu.make_async_copy(source, stored.at[place], sems.at[piece]))
    ahead = min(5, pieces)
    soon = ahead if raw else 2
    for copy in copies[:soon]:
        copy.start()

    block_rows = 32
    first = chain_start(first_ref[0] + step * (base or 0), channels, step)

    def one_block(index, carry):
        target = pl.ds(pl.multiple_of(index * block_rows, block_rows), block_rows)
        chain_of_weights(first, step, code[target], pointing_ref.at[which], own, target)
        return carry

    fetch_code.wait()
    lax.fori_loop(0, own_rows // block_rows, one_block, 0)
    fetch.wait()
    for copy in copies[soon:ahead]:
        copy.start()
    if raw:
        line_up(layout, arrived, lined, spectra)
        keep = pltpu.make_async_copy(spectra, spectra_out_ref, extra_sems.at[2])
        keep.start()

    for channel in range(channels):
        rows = slice(channel * per_channel, (channel + 1) * per_channel)
        total[rows, :] = jnp.dot(
            spectra[channel, :, made_feeds:], own[channel], preferred_element_type=jnp.float32
        )[:per_channel]
    for piece in range(pieces):
        copies[piece].wait()
        if piece + ahead < pieces:
            copies[piece + ahead].start()
        for channel in range(piece * count, (piece + 1) * count):
            rows = slice(channel * per_channel, (channel + 1) * per_channel)
            both = jnp.dot(
                spectra[channel, :, :made_feeds],
                stored[channel],
                preferred_element_type=jnp.float32,
            )[:per_channel]
            out_ref[rows, :] = turn_products(total[rows, :] + both).astype(out_ref.dtype)
    if raw:
        keep.wait()


def partial_beams(
    first, code, pointing, weights, made, spectra, layout, which, channels, base, step, dtype
):
    near, cores, all_channels, frames_here = layout
    feeds = code.shape[0]
    made_feeds = made[which]
    width = weights.shape[2]
    per_channel = 2 * cores * frames_here
    pieces = channels // 4
    raw = base is None
    lined_channels = all_channels if raw else channels
    in_vmem = pl.BlockSpec(memory_space=pltpu.VMEM)
    lined_shape = (lined_channels, padded_rows(per_channel), feeds)
    out_shape = [jax.ShapeDtypeStruct((channels * per_channel, width // 2), dtype)]
    scratch = [
        pltpu.VMEM((channels, made_feeds, width), weights.dtype),
        pltpu.VMEM((channels, feeds - made_feeds, width), weights.dtype),
        pltpu.VMEM((channels * per_channel, width), jnp.float32),
        pltpu.VMEM((feeds - made_feeds, LANES), code.dtype),
        pltpu.VMEM(lined_shape, jnp.bfloat16),
        pltpu.SemaphoreType.DMA((3,)),
        pltpu.SemaphoreType.DMA((pieces,)),
    ]
    if raw:
        out_shape.append(jax.ShapeDtypeStruct(lined_shape, jnp.bfloat16))
        scratch += [
            pltpu.VMEM(spectra.shape, spectra.dtype),
            pltpu.VMEM((near, all_channels * per_channel, feeds // near), jnp.float32),
        ]
    return pl.pallas_call(
        functools.partial(beams_kernel, layout, which, step, pieces, sum(made[:which]), base),
        in_specs=[
            pl.BlockSpec(memory_space=pltpu.SMEM),
            pl.BlockSpec(memory_space=pltpu.HBM),
            in_vmem,
            pl.BlockSpec(memory_space=pltpu.HBM),
            pl.BlockSpec(memory_space=pl.ANY if raw else pltpu.HBM),
        ],
        out_specs=[in_vmem, pl.BlockSpec(memory_space=pltpu.HBM)][: len(out_shape)],
        out_shape=out_shape,
        scratch_shapes=scratch,
        compiler_params=pltpu.CompilerParams(vmem_limit_bytes=50 * 1024 * 1024),
        cost_estimate=pl.CostEstimate(
            flops=(1 - which) * channels * feeds * width * 2 * 128 + 1,
            bytes_accessed=(1 - which) * channels * feeds * width * 2 + 1,
            transcendentals=0,
        ),
        name="beams",
    )(first, code, pointing, weights, spectra)


def gather_kernel(
    layout, beams_here, scale, own_ref, early_ref, late_ref, out_ref, own, other, total, rows, sems
):
    near, cores, channels, frames_here = layout
    lane_channels = LANES // beams_here
    per_core = 2 * frames_here
    per_channel = per_core * cores
    groups = channels // lane_channels
    fetches = [
        pltpu.make_async_copy(own_ref, own, sems.at[0]),
        pltpu.make_async_copy(early_ref, other.at[pl.ds(0, early_ref.shape[0])], sems.at[1]),
        pltpu.make_async_copy(
            late_ref, other.at[pl.ds(early_ref.shape[0], late_ref.shape[0])], sems.at[2]
        ),
    ]
    for fetch in fetches:
        fetch.start()
    for fetch in fetches:
        fetch.wait()
    total[...] = (own[...] + other[...].astype(jnp.float32)) * scale
    for group in range(groups):
        values = [
            total[pl.ds((group * lane_channels + sub) * per_channel, per_channel), :]
            for sub in range(lane_channels)
        ]
        for place in range(near):
            lanes = slice(place * beams_here, (place + 1) * beams_here)
            tile = jnp.concatenate([value[:, lanes] for value in values], axis=1)
            for core in range(cores):
                start = ((place * cores + core) * groups + group) * per_core
                for part in range(2):
                    source = (part * cores + core) * frames_here
                    rows[pl.ds(start + part * frames_here, frames_here), :] = tile[
                        source : source + frames_here
                    ]
    out_ref[...] = rows[...].astype(jnp.bfloat16)


def gather_beams(own, early, late, layout, beams_here, scale):
    near, cores, channels, frames_here = layout
    total_rows = near * cores * channels // (LANES // beams_here) * 2 * frames_here
    return pl.pallas_call(
        functools.partial(gather_kernel, layout, beams_here, scale),
        in_specs=[pl.BlockSpec(memory_space=pltpu.HBM)] + [pl.BlockSpec(memory_space=pl.ANY)] * 2,
        out_shape=jax.ShapeDtypeStruct((total_rows, LANES), jnp.bfloat16),
        scratch_shapes=[
            pltpu.VMEM(own.shape, own.dtype),
            pltpu.VMEM(own.shape, early.dtype),
            pltpu.VMEM(own.shape, jnp.float32),
            pltpu.VMEM((total_rows, LANES), jnp.float32),
            pltpu.SemaphoreType.DMA((3,)),
        ],
        compiler_params=pltpu.CompilerParams(vmem_limit_bytes=16 * 1024 * 1024),
        name="gather",
    )(own, early, late)


def series_kernel(
    beams_here, half_ref, received_ref, cos_ref, sin_ref, basis_ref, out_ref,
    arrived, basis, wide, lined, sems,
):
    frames_here = out_ref.shape[0]
    kappas = cos_ref.shape[0]
    lane_channels = LANES // beams_here
    side = kappas // 2
    half = half_ref[0]
    sign = (1 - 2 * half).astype(jnp.float32)
    fetch = pltpu.make_async_copy(received_ref, arrived, sems.at[2])
    fetch.start()
    fetch_basis = [
        pltpu.make_async_copy(
            basis_ref.at[parity + half * (1 - 2 * parity)], basis.at[parity], sems.at[parity]
        )
        for parity in range(2)
    ]
    for copy in fetch_basis:
        copy.start()
    fetch.wait()
    wide[...] = arrived[...].astype(jnp.float32)
    for index in range(frames_here):
        real = wide[pl.ds(index, kappas, stride=2 * frames_here), :]
        imag = wide[pl.ds(frames_here + index, kappas, stride=2 * frames_here), :]
        chirped_real = real * cos_ref[...] - imag * sin_ref[...]
        chirped_imag = real * sin_ref[...] + imag * cos_ref[...]
        target = slice(index * beams_here, (index + 1) * beams_here)
        for parity in range(2):
            where = slice(parity * side, (parity + 1) * side)
            both = jnp.concatenate([chirped_real[where], chirped_imag[where]], axis=0)
            turned = both.T
            high = turned.astype(jnp.bfloat16)
            low = (turned - high.astype(jnp.float32)).astype(jnp.bfloat16)
            for sub in range(lane_channels):
                source = slice(sub * beams_here, (sub + 1) * beams_here)
                lanes = slice(sub * 2 * side, (sub + 1) * 2 * side)
                lined[parity, 0, target, lanes] = high[source]
                lined[parity, 1, target, lanes] = low[source]
    sides = []
    for parity in range(2):
        high = lined[parity, 0]
        low = lined[parity, 1]
        fetch_basis[parity].wait()
        sides.append(
            jnp.dot(high, basis[parity, 0], preferred_element_type=jnp.float32)
            + jnp.dot(low, basis[parity, 0], preferred_element_type=jnp.float32)
            + jnp.dot(high, basis[parity, 1], preferred_element_type=jnp.float32)
        )
    times = sides[0].shape[1] // 2
    for part in range(2):
        even = sides[0][:, part * times : (part + 1) * times]
        odd = sides[1][:, part * times : (part + 1) * times]
        for which, value in enumerate((even + odd, (even - odd) * sign)):
            start = (2 * part + which) * times
            out_ref[:, :, start : start + times] = value.reshape(frames_here, beams_here, times)


def make_series(half_index, received, chirp_cos, chirp_sin, basis, beams_here, frames_here):
    in_vmem = pl.BlockSpec(memory_space=pltpu.VMEM)
    anywhere = pl.BlockSpec(memory_space=pl.ANY)
    series = pl.pallas_call(
        functools.partial(series_kernel, beams_here),
        in_specs=[
            pl.BlockSpec(memory_space=pltpu.SMEM), anywhere, in_vmem, in_vmem, anywhere,
        ],
        out_shape=jax.ShapeDtypeStruct(
            (frames_here, beams_here, 2 * basis.shape[3]), jnp.float32
        ),
        scratch_shapes=[
            pltpu.VMEM(received.shape, received.dtype),
            pltpu.VMEM(basis.shape, basis.dtype),
            pltpu.VMEM(received.shape, jnp.float32),
            pltpu.VMEM((2, 2, frames_here * beams_here, basis.shape[2]), jnp.bfloat16),
            pltpu.SemaphoreType.DMA((3,)),
        ],
        compiler_params=pltpu.CompilerParams(vmem_limit_bytes=24 * 1024 * 1024),
        name="series",
    )(half_index, received, chirp_cos, chirp_sin, basis)
    return jnp.transpose(series, (1, 0, 2))


def halves_body(samples, filter_taps, feed_cylinder, feed_delay, pointing, chirp_rate):
    length = filter_taps.shape[1]
    nchan = length // 2
    feed_here = samples.shape[0]
    frames_here = samples.shape[1] // length
    feeds = feed_delay.shape[0]
    beams = pointing.shape[0]
    beams_here = chirp_rate.shape[0]
    near = lax.axis_size("near")
    cores = lax.axis_size("tm")
    group = near * cores
    channels = nchan // group
    half_feeds = feeds // HALVES
    half_beams = beams // HALVES
    layout = (near, cores, channels, frames_here)
    half_index = lax.axis_index("half")
    place = lax.axis_index(GROUP)

    tail = from_behind(samples[:, (frames_here - (TAPS - 1)) * length :], "tm", 1)
    forward = jnp.asarray(folded_forward_basis(length))
    half_scalar = jnp.reshape(half_index, (1,)).astype(jnp.int32)
    taps = jnp.concatenate([filter_taps, filter_taps])
    spectra = spectra_rows(half_scalar, samples, tail, taps, forward, group)
    spectra = spectra.reshape(group, channels * 2 * frames_here, feed_here)
    received = lax.all_to_all(spectra, GROUP, 0, 0, tiled=True)
    received = received.reshape(-1, feed_here)

    in_parity = group // 2
    first = 2 * (place % in_parity) * channels + (place // in_parity ^ half_index) + 1
    first = jnp.reshape(first, (1,)).astype(jnp.int32)
    code = feed_cylinder * PHASES + feed_delay
    code = lax.dynamic_slice_in_dim(code, half_index * half_feeds, half_feeds)
    code = jnp.broadcast_to(code[:, None], (half_feeds, LANES))
    aim = jnp.transpose(pointing).astype(jnp.float32)
    aims = jnp.stack(
        [
            lax.dynamic_slice_in_dim(aim, half * half_beams, half_beams, 1)
            for half in (1 - half_index, half_index)
        ]
    )
    step = 2
    made = (half_feeds * 3 // 4, half_feeds * 3 // 4)
    weights = make_weights(first, code, aims, channels, step, made)
    swap = [
        (half * near + i, (1 - half) * near + (i + near // 2) % near)
        for half in range(HALVES)
        for i in range(near)
    ]
    common = (first, code, aims, weights, made)
    piece = channels * 5 // 8
    early, lined = partial_beams(
        *common, received, layout, 0, piece, None, step, jnp.bfloat16
    )
    early = lax.ppermute(early, ("half", "near"), swap)
    (late,) = partial_beams(
        *common, lined, layout, 0, channels - piece, piece, step, jnp.bfloat16
    )
    late = lax.ppermute(late, ("half", "near"), swap)
    (own,) = partial_beams(*common, lined, layout, 1, channels, 0, step, jnp.float32)
    gathered = gather_beams(own, early, late, layout, beams_here, 1.0 / math.sqrt(feeds))
    lane_channels = LANES // beams_here
    gathered = gathered.reshape(group, -1, LANES)
    returned = lax.all_to_all(gathered, GROUP, 0, 0, tiled=True).reshape(-1, LANES)

    kappa = jnp.arange(nchan // lane_channels, dtype=jnp.int32)[:, None]
    sub = jnp.arange(LANES, dtype=jnp.int32)[None, :] // beams_here
    side = nchan // lane_channels // 2
    channel = 2 * (lane_channels * (kappa % side) + sub) + (kappa // side ^ half_index)
    position = channel.astype(jnp.float32) / nchan
    rate = jnp.tile(jnp.pi * chirp_rate, lane_channels)[None, :]
    chirp = rate * (position * position)
    inverse = jnp.asarray(folded_inverse_basis(nchan, lane_channels))
    return make_series(
        half_scalar, returned, jnp.cos(chirp), jnp.sin(chirp), inverse, beams_here, frames_here
    )


def solution(mesh):
    feed_size = mesh.shape["feed"]
    wide_enough = FEEDS // feed_size % LANES == 0 and BEAMS // feed_size * 4 == LANES
    if not wide_enough:
        return jax.shard_map(
            plain_body,
            mesh=mesh,
            in_specs=(P("feed", "tm"), P(), P(), P(), P(), P("feed")),
            out_specs=P("feed", "tm", None),
            check_vma=False,
        )
    devices = mesh.devices.reshape(HALVES, feed_size // HALVES, mesh.shape["tm"])
    halved = jax.sharding.Mesh(devices, ("half", "near", "tm"))
    feed = ("half", "near")
    return jax.shard_map(
        halves_body,
        mesh=halved,
        in_specs=(P(feed, "tm"), P(), P(), P(), P(), P(feed)),
        out_specs=P(feed, "tm", None),
        check_vma=False,
    )
```

```python
import functools
import math

import jax
import jax.numpy as jnp
import ml_dtypes
import numpy as np
from jax import lax
from jax.experimental import pallas as pl
from jax.experimental.pallas import tpu as pltpu
from jax.sharding import PartitionSpec as P

FEEDS = 2048
NCHAN = 512
BEAMS = 512
TAPS = 4
CYL = 4
PHASES = 4096


def from_behind(x, axis, by):
    length = lax.axis_size(axis)
    pairs = [(i, i + by) for i in range(length) if 0 <= i + by < length]
    return lax.ppermute(x, axis, pairs)


def forward_basis(length, nchan):
    sample_ids = jnp.arange(length, dtype=jnp.int32)[:, None]
    chan_ids = jnp.arange(nchan, dtype=jnp.int32)[None, :]
    angle = (sample_ids * chan_ids % length).astype(jnp.float32) * (2.0 * math.pi / length)
    scaled = 1.0 / math.sqrt(length)
    return jnp.concatenate([jnp.cos(angle), -jnp.sin(angle)], axis=1) * scaled


def inverse_basis(nchan):
    chan_ids = jnp.arange(nchan, dtype=jnp.int32)[:, None]
    time_ids = jnp.arange(nchan, dtype=jnp.int32)[None, :]
    angle = (chan_ids * time_ids % nchan).astype(jnp.float32) * (2.0 * math.pi / nchan)
    cosine = jnp.cos(angle)
    sine = jnp.sin(angle)
    upper = jnp.concatenate([cosine, sine], axis=1)
    lower = jnp.concatenate([-sine, cosine], axis=1)
    return jnp.concatenate([upper, lower], axis=0) * (1.0 / math.sqrt(nchan))


def spectra_of(frame_block, basis):
    feed_here, batch_frames, length = frame_block.shape
    flat = frame_block.reshape(feed_here * batch_frames, length)
    spectral = jnp.dot(
        flat, basis, precision=lax.Precision.HIGHEST, preferred_element_type=jnp.float32
    )
    spectral = spectral.reshape(feed_here, batch_frames, 2, length // 2)
    return jnp.transpose(spectral, (3, 2, 1, 0)).astype(jnp.bfloat16)


def beamform(turned, steer, feed_delay, first_channel):
    chan_here, _, batch_frames, feeds = turned.shape
    beam_scale = 1.0 / math.sqrt(feeds)

    def one_channel(inputs):
        local, offset = inputs
        channel = first_channel + offset
        turns = (channel + 1) * feed_delay % PHASES
        phase = turns[:, None] * steer % PHASES
        angle = phase.astype(jnp.float32) * (2.0 * math.pi / PHASES)
        w_real = jnp.cos(angle).astype(jnp.bfloat16)
        w_imag = jnp.sin(angle).astype(jnp.bfloat16)
        stacked = local.reshape(2 * batch_frames, feeds)
        with_real = jnp.dot(stacked, w_real, preferred_element_type=jnp.float32)
        with_imag = jnp.dot(stacked, w_imag, preferred_element_type=jnp.float32)
        beam_real = with_real[:batch_frames] - with_imag[batch_frames:]
        beam_imag = with_imag[:batch_frames] + with_real[batch_frames:]
        return (jnp.stack([beam_real, beam_imag]) * beam_scale).astype(jnp.bfloat16)

    offsets = jnp.arange(chan_here, dtype=jnp.int32)
    return lax.map(one_channel, (turned, offsets))


def synthesize(returned, chirp_cos, chirp_sin, basis):
    nchan, _, batch_frames, beams_here = returned.shape
    values = returned.astype(jnp.float32)
    beam_real = values[:, 0]
    beam_imag = values[:, 1]
    chirped_real = beam_real * chirp_cos - beam_imag * chirp_sin
    chirped_imag = beam_real * chirp_sin + beam_imag * chirp_cos
    stacked = jnp.stack([chirped_real, chirped_imag])
    ordered = jnp.transpose(stacked, (3, 2, 0, 1)).reshape(beams_here * batch_frames, 2 * nchan)
    result = jnp.dot(
        ordered, basis, precision=lax.Precision.HIGHEST, preferred_element_type=jnp.float32
    )
    return result.reshape(beams_here, batch_frames, 2 * nchan)


def plain_body(samples, filter_taps, feed_cylinder, feed_delay, pointing, chirp_rate):
    length = 2 * NCHAN
    feed_here = samples.shape[0]
    frames_here = samples.shape[1] // length
    frames = samples.reshape(feed_here, frames_here, length)
    tail = from_behind(frames[:, frames_here - (TAPS - 1) :, :], "tm", 1)
    padded = jnp.concatenate([tail, frames], axis=1).astype(jnp.float32)
    filtered = jnp.zeros((feed_here, frames_here, length), jnp.float32)
    for tap_index in range(TAPS):
        filtered = (
            filtered + filter_taps[tap_index] * padded[:, tap_index : tap_index + frames_here, :]
        )
    basis = forward_basis(length, NCHAN)
    steer = jnp.zeros((FEEDS, BEAMS), jnp.int32)
    for cylinder in range(CYL):
        steer = steer + jnp.where(
            feed_cylinder[:, None] == cylinder, pointing[None, :, cylinder], 0
        )
    chan_here = NCHAN // lax.axis_size("feed")
    first_channel = lax.axis_index("feed") * chan_here
    position = jnp.arange(NCHAN).astype(jnp.float32) / NCHAN
    chirp = (jnp.pi * chirp_rate)[None, :] * (position * position)[:, None]
    chirp_cos = jnp.cos(chirp)[:, None, :]
    chirp_sin = jnp.sin(chirp)[:, None, :]
    back_basis = inverse_basis(NCHAN)
    turned = lax.all_to_all(
        spectra_of(filtered, basis), "feed", split_axis=0, concat_axis=3, tiled=True
    )
    formed = beamform(turned, steer, feed_delay, first_channel)
    returned = lax.all_to_all(formed, "feed", split_axis=3, concat_axis=0, tiled=True)
    series = synthesize(returned, chirp_cos, chirp_sin, back_basis)
    return series


LANES = 128
PHASE_BITS = PHASES.bit_length() - 1
HALVES = 2
GROUP = ("near", "tm")
VMEM = pltpu.CompilerParams(vmem_limit_bytes=56 * 1024 * 1024)


def split_bf16(table):
    high = table.astype(ml_dtypes.bfloat16)
    low = (table - high.astype(np.float64)).astype(ml_dtypes.bfloat16)
    return np.stack([high, low])


def folded_forward_basis(length):
    half = length // 2
    tables = []
    for parity in range(2):
        channel = 2 * np.arange(half // 2)[:, None] + parity
        angle = (channel * np.arange(half)[None, :] % length) * (2.0 * np.pi / length)
        rows = np.concatenate([np.cos(angle), -np.sin(angle)], axis=0) / math.sqrt(length)
        tables.append(split_bf16(rows))
    return np.stack(tables)


def folded_inverse_basis(nchan, lane_channels):
    kappas = nchan // 2 // lane_channels
    times = np.arange(nchan // 2)[None, :]
    tables = []
    for parity in range(2):
        rows = []
        for sub in range(lane_channels):
            channel = 2 * (lane_channels * np.arange(kappas)[:, None] + sub) + parity
            angle = (channel * times % nchan) * (2.0 * np.pi / nchan)
            rows.append(np.concatenate([np.cos(angle), np.sin(angle)], axis=1))
            rows.append(np.concatenate([-np.sin(angle), np.cos(angle)], axis=1))
        tables.append(split_bf16(np.concatenate(rows, axis=0) / math.sqrt(nchan)))
    return np.stack(tables)


def dot_nt(left, right):
    return lax.dot_general(
        left, right, (((1,), (1,)), ((), ())), preferred_element_type=jnp.float32
    )


def spectra_kernel(
    frames_here, group, half_ref, samples_ref, tail_ref, taps_in_ref, basis_ref, out_ref,
    samples, tail, taps_ref, basis, folded, packed, in_sems, out_sems,
):
    feed_here = samples_ref.shape[0]
    length = taps_ref.shape[1]
    half = length // 2
    before = TAPS - 1
    side = half_ref[0]
    sign = (1 - 2 * side).astype(jnp.float32)
    fetch_samples = pltpu.make_async_copy(samples_ref, samples, in_sems.at[0])
    fetch_tail = pltpu.make_async_copy(tail_ref, tail, in_sems.at[1])
    fetch_taps = pltpu.make_async_copy(taps_in_ref, taps_ref, in_sems.at[4])
    fetch_basis = [
        pltpu.make_async_copy(
            basis_ref.at[parity + side * (1 - 2 * parity)], basis.at[parity], in_sems.at[2 + parity]
        )
        for parity in range(2)
    ]
    fetches = [fetch_taps, fetch_samples, fetch_tail] + fetch_basis
    for fetch in fetches:
        fetch.start()
    fetch_taps.wait()
    fetch_samples.wait()

    def frame(index, start):
        if index < 0:
            lanes = pl.ds((index + before) * length + start, LANES)
            return tail[:, lanes].astype(jnp.float32)
        return samples[:, pl.ds(index * length + start, LANES)].astype(jnp.float32)

    def filtered(index, start):
        total = None
        for tap in range(TAPS):
            term = taps_ref[tap : tap + 1, start : start + LANES] * frame(
                index + tap - before, start
            )
            total = term if total is None else total + term
        return total

    for index in list(range(before, frames_here)) + list(range(before)):
        if index == 0:
            fetch_tail.wait()
        where = pl.ds(index * feed_here, feed_here)
        for start in range(0, half, LANES):
            near = filtered(index, start)
            far = filtered(index, start + half) * sign
            for parity, value in enumerate((near + far, near - far)):
                high = value.astype(jnp.bfloat16)
                folded[parity, 0, where, start : start + LANES] = high
                folded[parity, 1, where, start : start + LANES] = (
                    value - high.astype(jnp.float32)
                ).astype(jnp.bfloat16)

    parts = 2 * frames_here
    together = 2
    count = half // 2
    channels = length // 2 // group
    stores = []
    for parity in range(2):
        fetch_basis[parity].wait()
        for first in range(0, frames_here, together):
            where = pl.ds(first * feed_here, together * feed_here)
            high = folded[parity, 0, where, :]
            low = folded[parity, 1, where, :]
            result = (
                dot_nt(basis[parity, 0], high)
                + dot_nt(basis[parity, 0], low)
            ).astype(jnp.bfloat16)
            for part in range(2):
                for ahead in range(together):
                    row = part * frames_here + first + ahead
                    for place in range(count // channels):
                        target = (parity * (count // channels) + place) * parts + row
                        source = part * count + place * channels
                        packed[pl.ds(target * channels, channels), :] = result[
                            source : source + channels,
                            ahead * feed_here : (ahead + 1) * feed_here,
                        ]
        block = pl.ds(parity * count * parts, count * parts)
        store = pltpu.make_async_copy(packed.at[block], out_ref.at[block], out_sems.at[parity])
        store.start()
        stores.append(store)
    for store in stores:
        store.wait()


def spectra_rows(half_index, samples, tail, taps, basis, group):
    feed_here = samples.shape[0]
    length = taps.shape[1]
    frames_here = samples.shape[1] // length
    total_rows = length * frames_here
    anywhere = pl.BlockSpec(memory_space=pl.ANY)
    in_hbm = pl.BlockSpec(memory_space=pltpu.HBM)
    return pl.pallas_call(
        functools.partial(spectra_kernel, frames_here, group),
        in_specs=[pl.BlockSpec(memory_space=pltpu.SMEM), in_hbm, anywhere, in_hbm, in_hbm],
        out_specs=anywhere,
        out_shape=jax.ShapeDtypeStruct((total_rows, feed_here), jnp.bfloat16),
        scratch_shapes=[
            pltpu.VMEM(samples.shape, samples.dtype),
            pltpu.VMEM(tail.shape, tail.dtype),
            pltpu.VMEM(taps.shape, taps.dtype),
            pltpu.VMEM(basis.shape, basis.dtype),
            pltpu.VMEM((2, 2, frames_here * feed_here, length // 2), jnp.bfloat16),
            pltpu.VMEM((total_rows, feed_here), jnp.bfloat16),
            pltpu.SemaphoreType.DMA((5,)),
            pltpu.SemaphoreType.DMA((2,)),
        ],
        compiler_params=pltpu.CompilerParams(vmem_limit_bytes=50 * 1024 * 1024),
        name="spectra",
    )(half_index, samples, tail, taps, basis)


def sine_turns(turns):
    square = turns * turns
    total = None
    for power in range(11, 0, -2):
        factor = (2.0 * math.pi) ** power / math.factorial(power) * (-1) ** (power // 2)
        total = factor if total is None else total * square + factor
    return total * turns


def unit_vector(turns):
    cosine = sine_turns(0.25 - jnp.abs(turns))
    sine = sine_turns(jnp.maximum(jnp.minimum(turns, 0.5 - turns), -0.5 - turns))
    return cosine, sine


def centred(turns):
    return turns - jnp.floor(turns + 0.5)


def chain_start(first, channels, step):
    return (first + step * (channels // 2 - 1)).astype(jnp.float32)


def chain_of_weights(first, step, code, pointing_ref, out_ref, where):
    channels, _, width = out_ref.shape
    beams = width // 2
    repeat = beams // LANES
    middle = channels // 2
    cylinder = jnp.concatenate([lax.shift_right_logical(code, PHASE_BITS)] * repeat, axis=1)
    delay = jnp.concatenate([(code & (PHASES - 1)).astype(jnp.float32)] * repeat, axis=1)
    steer = jnp.broadcast_to(pointing_ref[0:1, :], delay.shape)
    for other in range(1, CYL):
        steer = jnp.where(cylinder == other, pointing_ref[other : other + 1, :], steer)
    turns = centred(delay * steer * (1.0 / PHASES))
    low_cos, low_sin = unit_vector(centred(first * turns))
    step_cos, step_sin = unit_vector(centred(float(step) * turns))
    high_cos = low_cos * step_cos - low_sin * step_sin
    high_sin = low_cos * step_sin + low_sin * step_cos
    twice = step_cos + step_cos

    def put(channel, cosine, sine):
        out_ref[channel, where, :beams] = cosine.astype(jnp.bfloat16)
        out_ref[channel, where, beams:] = sine.astype(jnp.bfloat16)

    put(middle - 1, low_cos, low_sin)
    put(middle, high_cos, high_sin)
    up = (low_cos, low_sin, high_cos, high_sin)
    down = (high_cos, high_sin, low_cos, low_sin)
    for away in range(1, middle):
        up = (up[2], up[3], twice * up[2] - up[0], twice * up[3] - up[1])
        down = (down[2], down[3], twice * down[2] - down[0], twice * down[3] - down[1])
        put(middle + away, up[2], up[3])
        put(middle - 1 - away, down[2], down[3])


def weights_kernel(block_rows, step, first_ref, code_ref, pointing_ref, out_ref):
    channels, rows, _ = out_ref.shape
    first = chain_start(first_ref[0], channels, step)

    def one_block(index, carry):
        where = pl.ds(pl.multiple_of(index * block_rows, block_rows), block_rows)
        chain_of_weights(first, step, code_ref[where], pointing_ref.at[0], out_ref, where)
        return carry

    lax.fori_loop(0, rows // block_rows, one_block, 0)


def make_weights(first, code, pointing, channels, step, feeds):
    _, cylinders, beams = pointing.shape
    rows = 256
    tiles = [count // rows for count in feeds]
    return pl.pallas_call(
        functools.partial(weights_kernel, 32, step),
        grid=(sum(tiles),),
        in_specs=[
            pl.BlockSpec(memory_space=pltpu.SMEM),
            pl.BlockSpec((rows, LANES), lambda i: (jnp.where(i < tiles[0], i, i - tiles[0]), 0)),
            pl.BlockSpec((1, cylinders, beams), lambda i: (jnp.where(i < tiles[0], 0, 1), 0, 0)),
        ],
        out_specs=pl.BlockSpec((channels, rows, 2 * beams), lambda i: (0, i, 0)),
        out_shape=jax.ShapeDtypeStruct((channels, sum(feeds), 2 * beams), jnp.bfloat16),
        compiler_params=VMEM,
        cost_estimate=pl.CostEstimate(
            flops=channels * sum(feeds) * beams * 8,
            bytes_accessed=channels * sum(feeds) * beams * 4,
            transcendentals=0,
        ),
        name="weights",
    )(first, code, pointing)


def padded_rows(rows):
    return -(-rows // 16) * 16


def turn_products(both):
    beams = both.shape[1] // 2
    half = both.shape[0] // 2
    by_imag = both[:, beams:]
    return both[:, :beams] + jnp.concatenate([-by_imag[half:], by_imag[:half]], axis=0)


def line_up(layout, arrived, lined, spectra):
    near, cores, channels, frames_here = layout
    per_source = 2 * frames_here
    per_channel = per_source * cores
    spare = spectra.shape[1] - per_channel
    for place in range(near):
        for core in range(cores):
            base = (place * cores + core) * per_source
            for part in range(2):
                for index in range(frames_here):
                    source = (base + part * frames_here + index) * channels
                    target = (part * cores + core) * frames_here + index
                    lined[place, pl.ds(target, channels, stride=per_channel), :] = arrived[
                        pl.ds(source, channels), :
                    ].astype(jnp.float32)
    blank = jnp.zeros((spare, arrived.shape[1]), jnp.float32)
    for channel in range(channels):
        rows = slice(channel * per_channel, (channel + 1) * per_channel)
        blocks = [
            jnp.concatenate([lined[place, rows, :], blank], axis=0) for place in range(near)
        ]
        spectra[channel] = jnp.concatenate(blocks, axis=1).astype(jnp.bfloat16)


def beams_kernel(
    layout, which, step, pieces, skipped, base, first_ref, code_ref, pointing_ref, weights_ref, spectra_ref,
    *rest,
):
    _, cores, _, frames_here = layout
    per_channel = 2 * frames_here * cores
    raw = base is None
    if raw:
        out_ref, spectra_out_ref, *rest = rest
    else:
        out_ref, *rest = rest
    stored, own, total, code, spectra, extra_sems, sems, *rest = rest
    if raw:
        arrived, lined = rest
    channels, made_feeds, _ = stored.shape
    here = pl.ds(base or 0, channels)
    if raw:
        fetch = pltpu.make_async_copy(spectra_ref, arrived, extra_sems.at[0])
    else:
        fetch = pltpu.make_async_copy(spectra_ref.at[here], spectra, extra_sems.at[0])
    own_rows = own.shape[1]
    fetch_code = pltpu.make_async_copy(
        code_ref.at[pl.ds(made_feeds, own_rows)], code, extra_sems.at[1]
    )
    fetch_code.start()
    fetch.start()
    count = channels // pieces
    copies = []
    for piece in range(pieces):
        place = pl.ds(piece * count, count)
        there = pl.ds((base or 0) + piece * count, count)
        source = weights_ref.at[there, pl.ds(skipped, made_feeds)]
        copies.append(pltpu.make_async_copy(source, stored.at[place], sems.at[piece]))
    ahead = min(5, pieces)
    soon = ahead if raw else 2
    for copy in copies[:soon]:
        copy.start()

    block_rows = 32
    first = chain_start(first_ref[0] + step * (base or 0), channels, step)

    def one_block(index, carry):
        target = pl.ds(pl.multiple_of(index * block_rows, block_rows), block_rows)
        chain_of_weights(first, step, code[target], pointing_ref.at[which], own, target)
        return carry

    fetch_code.wait()
    lax.fori_loop(0, own_rows // block_rows, one_block, 0)
    fetch.wait()
    for copy in copies[soon:ahead]:
        copy.start()
    if raw:
        line_up(layout, arrived, lined, spectra)
        keep = pltpu.make_async_copy(spectra, spectra_out_ref, extra_sems.at[2])
        keep.start()

    for channel in range(channels):
        rows = slice(channel * per_channel, (channel + 1) * per_channel)
        total[rows, :] = jnp.dot(
            spectra[channel, :, made_feeds:], own[channel], preferred_element_type=jnp.float32
        )[:per_channel]
    for piece in range(pieces):
        copies[piece].wait()
        if piece + ahead < pieces:
            copies[piece + ahead].start()
        for channel in range(piece * count, (piece + 1) * count):
            rows = slice(channel * per_channel, (channel + 1) * per_channel)
            both = jnp.dot(
                spectra[channel, :, :made_feeds],
                stored[channel],
                preferred_element_type=jnp.float32,
            )[:per_channel]
            out_ref[rows, :] = turn_products(total[rows, :] + both).astype(out_ref.dtype)
    if raw:
        keep.wait()


def partial_beams(
    first, code, pointing, weights, made, spectra, layout, which, channels, base, step, dtype
):
    near, cores, all_channels, frames_here = layout
    feeds = code.shape[0]
    made_feeds = made[which]
    width = weights.shape[2]
    per_channel = 2 * cores * frames_here
    pieces = channels // 4
    raw = base is None
    lined_channels = all_channels if raw else channels
    in_vmem = pl.BlockSpec(memory_space=pltpu.VMEM)
    lined_shape = (lined_channels, padded_rows(per_channel), feeds)
    out_shape = [jax.ShapeDtypeStruct((channels * per_channel, width // 2), dtype)]
    scratch = [
        pltpu.VMEM((channels, made_feeds, width), weights.dtype),
        pltpu.VMEM((channels, feeds - made_feeds, width), weights.dtype),
        pltpu.VMEM((channels * per_channel, width), jnp.float32),
        pltpu.VMEM((feeds - made_feeds, LANES), code.dtype),
        pltpu.VMEM(lined_shape, jnp.bfloat16),
        pltpu.SemaphoreType.DMA((3,)),
        pltpu.SemaphoreType.DMA((pieces,)),
    ]
    if raw:
        out_shape.append(jax.ShapeDtypeStruct(lined_shape, jnp.bfloat16))
        scratch += [
            pltpu.VMEM(spectra.shape, spectra.dtype),
            pltpu.VMEM((near, all_channels * per_channel, feeds // near), jnp.float32),
        ]
    return pl.pallas_call(
        functools.partial(beams_kernel, layout, which, step, pieces, sum(made[:which]), base),
        in_specs=[
            pl.BlockSpec(memory_space=pltpu.SMEM),
            pl.BlockSpec(memory_space=pltpu.HBM),
            in_vmem,
            pl.BlockSpec(memory_space=pltpu.HBM),
            pl.BlockSpec(memory_space=pl.ANY if raw else pltpu.HBM),
        ],
        out_specs=[in_vmem, pl.BlockSpec(memory_space=pltpu.HBM)][: len(out_shape)],
        out_shape=out_shape,
        scratch_shapes=scratch,
        compiler_params=pltpu.CompilerParams(vmem_limit_bytes=50 * 1024 * 1024),
        cost_estimate=pl.CostEstimate(
            flops=(1 - which) * channels * feeds * width * 2 * 128 + 1,
            bytes_accessed=(1 - which) * channels * feeds * width * 2 + 1,
            transcendentals=0,
        ),
        name="beams",
    )(first, code, pointing, weights, spectra)


def gather_kernel(
    layout, beams_here, scale, own_ref, early_ref, late_ref, out_ref, own, other, total, rows, sems
):
    near, cores, channels, frames_here = layout
    lane_channels = LANES // beams_here
    per_core = 2 * frames_here
    per_channel = per_core * cores
    groups = channels // lane_channels
    fetches = [
        pltpu.make_async_copy(own_ref, own, sems.at[0]),
        pltpu.make_async_copy(early_ref, other.at[pl.ds(0, early_ref.shape[0])], sems.at[1]),
        pltpu.make_async_copy(
            late_ref, other.at[pl.ds(early_ref.shape[0], late_ref.shape[0])], sems.at[2]
        ),
    ]
    for fetch in fetches:
        fetch.start()
    for fetch in fetches:
        fetch.wait()
    total[...] = (own[...] + other[...].astype(jnp.float32)) * scale
    for group in range(groups):
        values = [
            total[pl.ds((group * lane_channels + sub) * per_channel, per_channel), :]
            for sub in range(lane_channels)
        ]
        for place in range(near):
            lanes = slice(place * beams_here, (place + 1) * beams_here)
            tile = jnp.concatenate([value[:, lanes] for value in values], axis=1)
            for core in range(cores):
                start = ((place * cores + core) * groups + group) * per_core
                for part in range(2):
                    source = (part * cores + core) * frames_here
                    rows[pl.ds(start + part * frames_here, frames_here), :] = tile[
                        source : source + frames_here
                    ]
    out_ref[...] = rows[...].astype(jnp.bfloat16)


def gather_beams(own, early, late, layout, beams_here, scale):
    near, cores, channels, frames_here = layout
    total_rows = near * cores * channels // (LANES // beams_here) * 2 * frames_here
    return pl.pallas_call(
        functools.partial(gather_kernel, layout, beams_here, scale),
        in_specs=[pl.BlockSpec(memory_space=pltpu.HBM)] + [pl.BlockSpec(memory_space=pl.ANY)] * 2,
        out_shape=jax.ShapeDtypeStruct((total_rows, LANES), jnp.bfloat16),
        scratch_shapes=[
            pltpu.VMEM(own.shape, own.dtype),
            pltpu.VMEM(own.shape, early.dtype),
            pltpu.VMEM(own.shape, jnp.float32),
            pltpu.VMEM((total_rows, LANES), jnp.float32),
            pltpu.SemaphoreType.DMA((3,)),
        ],
        compiler_params=pltpu.CompilerParams(vmem_limit_bytes=16 * 1024 * 1024),
        name="gather",
    )(own, early, late)


def series_kernel(
    beams_here, half_ref, received_ref, cos_ref, sin_ref, basis_ref, out_ref,
    arrived, basis, wide, lined, sems,
):
    frames_here = out_ref.shape[0]
    kappas = cos_ref.shape[0]
    lane_channels = LANES // beams_here
    side = kappas // 2
    half = half_ref[0]
    sign = (1 - 2 * half).astype(jnp.float32)
    fetch = pltpu.make_async_copy(received_ref, arrived, sems.at[2])
    fetch.start()
    fetch_basis = [
        pltpu.make_async_copy(
            basis_ref.at[parity + half * (1 - 2 * parity)], basis.at[parity], sems.at[parity]
        )
        for parity in range(2)
    ]
    for copy in fetch_basis:
        copy.start()
    fetch.wait()
    wide[...] = arrived[...].astype(jnp.float32)
    for index in range(frames_here):
        real = wide[pl.ds(index, kappas, stride=2 * frames_here), :]
        imag = wide[pl.ds(frames_here + index, kappas, stride=2 * frames_here), :]
        chirped_real = real * cos_ref[...] - imag * sin_ref[...]
        chirped_imag = real * sin_ref[...] + imag * cos_ref[...]
        target = slice(index * beams_here, (index + 1) * beams_here)
        for parity in range(2):
            where = slice(parity * side, (parity + 1) * side)
            both = jnp.concatenate([chirped_real[where], chirped_imag[where]], axis=0)
            turned = both.T
            high = turned.astype(jnp.bfloat16)
            low = (turned - high.astype(jnp.float32)).astype(jnp.bfloat16)
            for sub in range(lane_channels):
                source = slice(sub * beams_here, (sub + 1) * beams_here)
                lanes = slice(sub * 2 * side, (sub + 1) * 2 * side)
                lined[parity, 0, target, lanes] = high[source]
                lined[parity, 1, target, lanes] = low[source]
    sides = []
    for parity in range(2):
        high = lined[parity, 0]
        low = lined[parity, 1]
        fetch_basis[parity].wait()
        sides.append(
            jnp.dot(high, basis[parity, 0], preferred_element_type=jnp.float32)
            + jnp.dot(low, basis[parity, 0], preferred_element_type=jnp.float32)
            + jnp.dot(high, basis[parity, 1], preferred_element_type=jnp.float32)
        )
    times = sides[0].shape[1] // 2
    for part in range(2):
        even = sides[0][:, part * times : (part + 1) * times]
        odd = sides[1][:, part * times : (part + 1) * times]
        for which, value in enumerate((even + odd, (even - odd) * sign)):
            start = (2 * part + which) * times
            out_ref[:, :, start : start + times] = value.reshape(frames_here, beams_here, times)


def make_series(half_index, received, chirp_cos, chirp_sin, basis, beams_here, frames_here):
    in_vmem = pl.BlockSpec(memory_space=pltpu.VMEM)
    anywhere = pl.BlockSpec(memory_space=pl.ANY)
    series = pl.pallas_call(
        functools.partial(series_kernel, beams_here),
        in_specs=[
            pl.BlockSpec(memory_space=pltpu.SMEM), anywhere, in_vmem, in_vmem, anywhere,
        ],
        out_shape=jax.ShapeDtypeStruct(
            (frames_here, beams_here, 2 * basis.shape[3]), jnp.float32
        ),
        scratch_shapes=[
            pltpu.VMEM(received.shape, received.dtype),
            pltpu.VMEM(basis.shape, basis.dtype),
            pltpu.VMEM(received.shape, jnp.float32),
            pltpu.VMEM((2, 2, frames_here * beams_here, basis.shape[2]), jnp.bfloat16),
            pltpu.SemaphoreType.DMA((3,)),
        ],
        compiler_params=pltpu.CompilerParams(vmem_limit_bytes=24 * 1024 * 1024),
        name="series",
    )(half_index, received, chirp_cos, chirp_sin, basis)
    return jnp.transpose(series, (1, 0, 2))


def halves_body(samples, filter_taps, feed_cylinder, feed_delay, pointing, chirp_rate):
    length = filter_taps.shape[1]
    nchan = length // 2
    feed_here = samples.shape[0]
    frames_here = samples.shape[1] // length
    feeds = feed_delay.shape[0]
    beams = pointing.shape[0]
    beams_here = chirp_rate.shape[0]
    near = lax.axis_size("near")
    cores = lax.axis_size("tm")
    group = near * cores
    channels = nchan // group
    half_feeds = feeds // HALVES
    half_beams = beams // HALVES
    layout = (near, cores, channels, frames_here)
    half_index = lax.axis_index("half")
    place = lax.axis_index(GROUP)

    tail = from_behind(samples[:, (frames_here - (TAPS - 1)) * length :], "tm", 1)
    forward = jnp.asarray(folded_forward_basis(length))
    half_scalar = jnp.reshape(half_index, (1,)).astype(jnp.int32)
    taps = jnp.concatenate([filter_taps, filter_taps])
    spectra = spectra_rows(half_scalar, samples, tail, taps, forward, group)
    spectra = spectra.reshape(group, channels * 2 * frames_here, feed_here)
    received = lax.all_to_all(spectra, GROUP, 0, 0, tiled=True)
    received = received.reshape(-1, feed_here)

    in_parity = group // 2
    first = 2 * (place % in_parity) * channels + (place // in_parity ^ half_index) + 1
    first = jnp.reshape(first, (1,)).astype(jnp.int32)
    code = feed_cylinder * PHASES + feed_delay
    code = lax.dynamic_slice_in_dim(code, half_index * half_feeds, half_feeds)
    code = jnp.broadcast_to(code[:, None], (half_feeds, LANES))
    aim = jnp.transpose(pointing).astype(jnp.float32)
    aims = jnp.stack(
        [
            lax.dynamic_slice_in_dim(aim, half * half_beams, half_beams, 1)
            for half in (1 - half_index, half_index)
        ]
    )
    step = 2
    made = (half_feeds * 3 // 4, half_feeds * 3 // 4)
    weights = make_weights(first, code, aims, channels, step, made)
    swap = [
        (half * near + i, (1 - half) * near + (i + near // 2) % near)
        for half in range(HALVES)
        for i in range(near)
    ]
    common = (first, code, aims, weights, made)
    piece = channels * 5 // 8
    early, lined = partial_beams(
        *common, received, layout, 0, piece, None, step, jnp.bfloat16
    )
    early = lax.ppermute(early, ("half", "near"), swap)
    (late,) = partial_beams(
        *common, lined, layout, 0, channels - piece, piece, step, jnp.bfloat16
    )
    late = lax.ppermute(late, ("half", "near"), swap)
    (own,) = partial_beams(*common, lined, layout, 1, channels, 0, step, jnp.float32)
    gathered = gather_beams(own, early, late, layout, beams_here, 1.0 / math.sqrt(feeds))
    lane_channels = LANES // beams_here
    gathered = gathered.reshape(group, -1, LANES)
    returned = lax.all_to_all(gathered, GROUP, 0, 0, tiled=True).reshape(-1, LANES)

    kappa = jnp.arange(nchan // lane_channels, dtype=jnp.int32)[:, None]
    sub = jnp.arange(LANES, dtype=jnp.int32)[None, :] // beams_here
    side = nchan // lane_channels // 2
    channel = 2 * (lane_channels * (kappa % side) + sub) + (kappa // side ^ half_index)
    position = channel.astype(jnp.float32) / nchan
    rate = jnp.tile(jnp.pi * chirp_rate, lane_channels)[None, :]
    chirp = rate * (position * position)
    inverse = jnp.asarray(folded_inverse_basis(nchan, lane_channels))
    return make_series(
        half_scalar, returned, jnp.cos(chirp), jnp.sin(chirp), inverse, beams_here, frames_here
    )


def solution(mesh):
    feed_size = mesh.shape["feed"]
    wide_enough = FEEDS // feed_size % LANES == 0 and BEAMS // feed_size * 4 == LANES
    if not wide_enough:
        return jax.shard_map(
            plain_body,
            mesh=mesh,
            in_specs=(P("feed", "tm"), P(), P(), P(), P(), P("feed")),
            out_specs=P("feed", "tm", None),
            check_vma=False,
        )
    devices = mesh.devices.reshape(HALVES, feed_size // HALVES, mesh.shape["tm"])
    halved = jax.sharding.Mesh(devices, ("half", "near", "tm"))
    feed = ("half", "near")
    return jax.shard_map(
        halves_body,
        mesh=halved,
        in_specs=(P(feed, "tm"), P(), P(), P(), P(), P(feed)),
        out_specs=P(feed, "tm", None),
        check_vma=False,
    )
```

```python
import functools
import math

import jax
import jax.numpy as jnp
import ml_dtypes
import numpy as np
from jax import lax
from jax.experimental import pallas as pl
from jax.experimental.pallas import tpu as pltpu
from jax.sharding import PartitionSpec as P

FEEDS = 2048
NCHAN = 512
BEAMS = 512
TAPS = 4
CYL = 4
PHASES = 4096


def from_behind(x, axis, by):
    length = lax.axis_size(axis)
    pairs = [(i, i + by) for i in range(length) if 0 <= i + by < length]
    return lax.ppermute(x, axis, pairs)


def forward_basis(length, nchan):
    sample_ids = jnp.arange(length, dtype=jnp.int32)[:, None]
    chan_ids = jnp.arange(nchan, dtype=jnp.int32)[None, :]
    angle = (sample_ids * chan_ids % length).astype(jnp.float32) * (2.0 * math.pi / length)
    scaled = 1.0 / math.sqrt(length)
    return jnp.concatenate([jnp.cos(angle), -jnp.sin(angle)], axis=1) * scaled


def inverse_basis(nchan):
    chan_ids = jnp.arange(nchan, dtype=jnp.int32)[:, None]
    time_ids = jnp.arange(nchan, dtype=jnp.int32)[None, :]
    angle = (chan_ids * time_ids % nchan).astype(jnp.float32) * (2.0 * math.pi / nchan)
    cosine = jnp.cos(angle)
    sine = jnp.sin(angle)
    upper = jnp.concatenate([cosine, sine], axis=1)
    lower = jnp.concatenate([-sine, cosine], axis=1)
    return jnp.concatenate([upper, lower], axis=0) * (1.0 / math.sqrt(nchan))


def spectra_of(frame_block, basis):
    feed_here, batch_frames, length = frame_block.shape
    flat = frame_block.reshape(feed_here * batch_frames, length)
    spectral = jnp.dot(
        flat, basis, precision=lax.Precision.HIGHEST, preferred_element_type=jnp.float32
    )
    spectral = spectral.reshape(feed_here, batch_frames, 2, length // 2)
    return jnp.transpose(spectral, (3, 2, 1, 0)).astype(jnp.bfloat16)


def beamform(turned, steer, feed_delay, first_channel):
    chan_here, _, batch_frames, feeds = turned.shape
    beam_scale = 1.0 / math.sqrt(feeds)

    def one_channel(inputs):
        local, offset = inputs
        channel = first_channel + offset
        turns = (channel + 1) * feed_delay % PHASES
        phase = turns[:, None] * steer % PHASES
        angle = phase.astype(jnp.float32) * (2.0 * math.pi / PHASES)
        w_real = jnp.cos(angle).astype(jnp.bfloat16)
        w_imag = jnp.sin(angle).astype(jnp.bfloat16)
        stacked = local.reshape(2 * batch_frames, feeds)
        with_real = jnp.dot(stacked, w_real, preferred_element_type=jnp.float32)
        with_imag = jnp.dot(stacked, w_imag, preferred_element_type=jnp.float32)
        beam_real = with_real[:batch_frames] - with_imag[batch_frames:]
        beam_imag = with_imag[:batch_frames] + with_real[batch_frames:]
        return (jnp.stack([beam_real, beam_imag]) * beam_scale).astype(jnp.bfloat16)

    offsets = jnp.arange(chan_here, dtype=jnp.int32)
    return lax.map(one_channel, (turned, offsets))


def synthesize(returned, chirp_cos, chirp_sin, basis):
    nchan, _, batch_frames, beams_here = returned.shape
    values = returned.astype(jnp.float32)
    beam_real = values[:, 0]
    beam_imag = values[:, 1]
    chirped_real = beam_real * chirp_cos - beam_imag * chirp_sin
    chirped_imag = beam_real * chirp_sin + beam_imag * chirp_cos
    stacked = jnp.stack([chirped_real, chirped_imag])
    ordered = jnp.transpose(stacked, (3, 2, 0, 1)).reshape(beams_here * batch_frames, 2 * nchan)
    result = jnp.dot(
        ordered, basis, precision=lax.Precision.HIGHEST, preferred_element_type=jnp.float32
    )
    return result.reshape(beams_here, batch_frames, 2 * nchan)


def plain_body(samples, filter_taps, feed_cylinder, feed_delay, pointing, chirp_rate):
    length = 2 * NCHAN
    feed_here = samples.shape[0]
    frames_here = samples.shape[1] // length
    frames = samples.reshape(feed_here, frames_here, length)
    tail = from_behind(frames[:, frames_here - (TAPS - 1) :, :], "tm", 1)
    padded = jnp.concatenate([tail, frames], axis=1).astype(jnp.float32)
    filtered = jnp.zeros((feed_here, frames_here, length), jnp.float32)
    for tap_index in range(TAPS):
        filtered = (
            filtered + filter_taps[tap_index] * padded[:, tap_index : tap_index + frames_here, :]
        )
    basis = forward_basis(length, NCHAN)
    steer = jnp.zeros((FEEDS, BEAMS), jnp.int32)
    for cylinder in range(CYL):
        steer = steer + jnp.where(
            feed_cylinder[:, None] == cylinder, pointing[None, :, cylinder], 0
        )
    chan_here = NCHAN // lax.axis_size("feed")
    first_channel = lax.axis_index("feed") * chan_here
    position = jnp.arange(NCHAN).astype(jnp.float32) / NCHAN
    chirp = (jnp.pi * chirp_rate)[None, :] * (position * position)[:, None]
    chirp_cos = jnp.cos(chirp)[:, None, :]
    chirp_sin = jnp.sin(chirp)[:, None, :]
    back_basis = inverse_basis(NCHAN)
    turned = lax.all_to_all(
        spectra_of(filtered, basis), "feed", split_axis=0, concat_axis=3, tiled=True
    )
    formed = beamform(turned, steer, feed_delay, first_channel)
    returned = lax.all_to_all(formed, "feed", split_axis=3, concat_axis=0, tiled=True)
    series = synthesize(returned, chirp_cos, chirp_sin, back_basis)
    return series


LANES = 128
PHASE_BITS = PHASES.bit_length() - 1
HALVES = 2
GROUP = ("near", "tm")
VMEM = pltpu.CompilerParams(vmem_limit_bytes=56 * 1024 * 1024)


def split_bf16(table):
    high = table.astype(ml_dtypes.bfloat16)
    low = (table - high.astype(np.float64)).astype(ml_dtypes.bfloat16)
    return np.stack([high, low])


def folded_forward_basis(length):
    half = length // 2
    tables = []
    for parity in range(2):
        channel = 2 * np.arange(half // 2)[:, None] + parity
        angle = (channel * np.arange(half)[None, :] % length) * (2.0 * np.pi / length)
        rows = np.concatenate([np.cos(angle), -np.sin(angle)], axis=0) / math.sqrt(length)
        tables.append(split_bf16(rows))
    return np.stack(tables)


def folded_inverse_basis(nchan, lane_channels):
    kappas = nchan // 2 // lane_channels
    times = np.arange(nchan // 2)[None, :]
    tables = []
    for parity in range(2):
        rows = []
        for sub in range(lane_channels):
            channel = 2 * (lane_channels * np.arange(kappas)[:, None] + sub) + parity
            angle = (channel * times % nchan) * (2.0 * np.pi / nchan)
            rows.append(np.concatenate([np.cos(angle), np.sin(angle)], axis=1))
            rows.append(np.concatenate([-np.sin(angle), np.cos(angle)], axis=1))
        tables.append(split_bf16(np.concatenate(rows, axis=0) / math.sqrt(nchan)))
    return np.stack(tables)


def dot_nt(left, right):
    return lax.dot_general(
        left, right, (((1,), (1,)), ((), ())), preferred_element_type=jnp.float32
    )


def spectra_kernel(
    frames_here, group, half_ref, samples_ref, tail_ref, taps_in_ref, basis_ref, out_ref,
    samples, tail, taps_ref, basis, folded, packed, in_sems, out_sems,
):
    feed_here = samples_ref.shape[0]
    length = taps_ref.shape[1]
    half = length // 2
    before = TAPS - 1
    side = half_ref[0]
    sign = (1 - 2 * side).astype(jnp.float32)
    fetch_samples = pltpu.make_async_copy(samples_ref, samples, in_sems.at[0])
    fetch_tail = pltpu.make_async_copy(tail_ref, tail, in_sems.at[1])
    fetch_taps = pltpu.make_async_copy(taps_in_ref, taps_ref, in_sems.at[4])
    fetch_basis = [
        pltpu.make_async_copy(
            basis_ref.at[parity + side * (1 - 2 * parity)], basis.at[parity], in_sems.at[2 + parity]
        )
        for parity in range(2)
    ]
    fetches = [fetch_taps, fetch_samples, fetch_tail] + fetch_basis
    for fetch in fetches:
        fetch.start()
    fetch_taps.wait()
    fetch_samples.wait()

    def frame(index, start):
        if index < 0:
            lanes = pl.ds((index + before) * length + start, LANES)
            return tail[:, lanes].astype(jnp.float32)
        return samples[:, pl.ds(index * length + start, LANES)].astype(jnp.float32)

    def filtered(index, start):
        total = None
        for tap in range(TAPS):
            term = taps_ref[tap : tap + 1, start : start + LANES] * frame(
                index + tap - before, start
            )
            total = term if total is None else total + term
        return total

    for index in list(range(before, frames_here)) + list(range(before)):
        if index == 0:
            fetch_tail.wait()
        where = pl.ds(index * feed_here, feed_here)
        for start in range(0, half, LANES):
            near = filtered(index, start)
            far = filtered(index, start + half) * sign
            for parity, value in enumerate((near + far, near - far)):
                high = value.astype(jnp.bfloat16)
                folded[parity, 0, where, start : start + LANES] = high
                folded[parity, 1, where, start : start + LANES] = (
                    value - high.astype(jnp.float32)
                ).astype(jnp.bfloat16)

    parts = 2 * frames_here
    together = 2
    count = half // 2
    channels = length // 2 // group
    stores = []
    for parity in range(2):
        fetch_basis[parity].wait()
        for first in range(0, frames_here, together):
            where = pl.ds(first * feed_here, together * feed_here)
            high = folded[parity, 0, where, :]
            low = folded[parity, 1, where, :]
            result = (
                dot_nt(basis[parity, 0], high)
                + dot_nt(basis[parity, 0], low)
            ).astype(jnp.bfloat16)
            for part in range(2):
                for ahead in range(together):
                    row = part * frames_here + first + ahead
                    for place in range(count // channels):
                        target = (parity * (count // channels) + place) * parts + row
                        source = part * count + place * channels
                        packed[pl.ds(target * channels, channels), :] = result[
                            source : source + channels,
                            ahead * feed_here : (ahead + 1) * feed_here,
                        ]
        block = pl.ds(parity * count * parts, count * parts)
        store = pltpu.make_async_copy(packed.at[block], out_ref.at[block], out_sems.at[parity])
        store.start()
        stores.append(store)
    for store in stores:
        store.wait()


def spectra_rows(half_index, samples, tail, taps, basis, group):
    feed_here = samples.shape[0]
    length = taps.shape[1]
    frames_here = samples.shape[1] // length
    total_rows = length * frames_here
    anywhere = pl.BlockSpec(memory_space=pl.ANY)
    in_hbm = pl.BlockSpec(memory_space=pltpu.HBM)
    return pl.pallas_call(
        functools.partial(spectra_kernel, frames_here, group),
        in_specs=[pl.BlockSpec(memory_space=pltpu.SMEM), in_hbm, anywhere, in_hbm, in_hbm],
        out_specs=anywhere,
        out_shape=jax.ShapeDtypeStruct((total_rows, feed_here), jnp.bfloat16),
        scratch_shapes=[
            pltpu.VMEM(samples.shape, samples.dtype),
            pltpu.VMEM(tail.shape, tail.dtype),
            pltpu.VMEM(taps.shape, taps.dtype),
            pltpu.VMEM(basis.shape, basis.dtype),
            pltpu.VMEM((2, 2, frames_here * feed_here, length // 2), jnp.bfloat16),
            pltpu.VMEM((total_rows, feed_here), jnp.bfloat16),
            pltpu.SemaphoreType.DMA((5,)),
            pltpu.SemaphoreType.DMA((2,)),
        ],
        compiler_params=pltpu.CompilerParams(vmem_limit_bytes=50 * 1024 * 1024),
        name="spectra",
    )(half_index, samples, tail, taps, basis)


def sine_turns(turns):
    square = turns * turns
    total = None
    for power in range(11, 0, -2):
        factor = (2.0 * math.pi) ** power / math.factorial(power) * (-1) ** (power // 2)
        total = factor if total is None else total * square + factor
    return total * turns


def unit_vector(turns):
    cosine = sine_turns(0.25 - jnp.abs(turns))
    sine = sine_turns(jnp.maximum(jnp.minimum(turns, 0.5 - turns), -0.5 - turns))
    return cosine, sine


def centred(turns):
    return turns - jnp.floor(turns + 0.5)


def chain_start(first, channels, step):
    return (first + step * (channels // 2 - 1)).astype(jnp.float32)


def chain_of_weights(first, step, code, pointing_ref, out_ref, where):
    channels, _, width = out_ref.shape
    beams = width // 2
    repeat = beams // LANES
    middle = channels // 2
    cylinder = jnp.concatenate([lax.shift_right_logical(code, PHASE_BITS)] * repeat, axis=1)
    delay = jnp.concatenate([(code & (PHASES - 1)).astype(jnp.float32)] * repeat, axis=1)
    steer = jnp.broadcast_to(pointing_ref[0:1, :], delay.shape)
    for other in range(1, CYL):
        steer = jnp.where(cylinder == other, pointing_ref[other : other + 1, :], steer)
    turns = centred(delay * steer * (1.0 / PHASES))
    low_cos, low_sin = unit_vector(centred(first * turns))
    step_cos, step_sin = unit_vector(centred(float(step) * turns))
    high_cos = low_cos * step_cos - low_sin * step_sin
    high_sin = low_cos * step_sin + low_sin * step_cos
    twice = step_cos + step_cos

    def put(channel, cosine, sine):
        out_ref[channel, where, :beams] = cosine.astype(jnp.bfloat16)
        out_ref[channel, where, beams:] = sine.astype(jnp.bfloat16)

    put(middle - 1, low_cos, low_sin)
    put(middle, high_cos, high_sin)
    up = (low_cos, low_sin, high_cos, high_sin)
    down = (high_cos, high_sin, low_cos, low_sin)
    for away in range(1, middle):
        up = (up[2], up[3], twice * up[2] - up[0], twice * up[3] - up[1])
        down = (down[2], down[3], twice * down[2] - down[0], twice * down[3] - down[1])
        put(middle + away, up[2], up[3])
        put(middle - 1 - away, down[2], down[3])


def weights_kernel(block_rows, step, first_ref, code_ref, pointing_ref, out_ref):
    channels, rows, _ = out_ref.shape
    first = chain_start(first_ref[0], channels, step)

    def one_block(index, carry):
        where = pl.ds(pl.multiple_of(index * block_rows, block_rows), block_rows)
        chain_of_weights(first, step, code_ref[where], pointing_ref.at[0], out_ref, where)
        return carry

    lax.fori_loop(0, rows // block_rows, one_block, 0)


def make_weights(first, code, pointing, channels, step, feeds):
    _, cylinders, beams = pointing.shape
    rows = 256
    tiles = [count // rows for count in feeds]
    return pl.pallas_call(
        functools.partial(weights_kernel, 32, step),
        grid=(sum(tiles),),
        in_specs=[
            pl.BlockSpec(memory_space=pltpu.SMEM),
            pl.BlockSpec((rows, LANES), lambda i: (jnp.where(i < tiles[0], i, i - tiles[0]), 0)),
            pl.BlockSpec((1, cylinders, beams), lambda i: (jnp.where(i < tiles[0], 0, 1), 0, 0)),
        ],
        out_specs=pl.BlockSpec((channels, rows, 2 * beams), lambda i: (0, i, 0)),
        out_shape=jax.ShapeDtypeStruct((channels, sum(feeds), 2 * beams), jnp.bfloat16),
        compiler_params=VMEM,
        cost_estimate=pl.CostEstimate(
            flops=channels * sum(feeds) * beams * 8,
            bytes_accessed=channels * sum(feeds) * beams * 4,
            transcendentals=0,
        ),
        name="weights",
    )(first, code, pointing)


def padded_rows(rows):
    return -(-rows // 16) * 16


def turn_products(both):
    beams = both.shape[1] // 2
    half = both.shape[0] // 2
    by_imag = both[:, beams:]
    return both[:, :beams] + jnp.concatenate([-by_imag[half:], by_imag[:half]], axis=0)


def line_up(layout, arrived, lined, spectra):
    near, cores, channels, frames_here = layout
    per_source = 2 * frames_here
    per_channel = per_source * cores
    spare = spectra.shape[1] - per_channel
    for place in range(near):
        for core in range(cores):
            base = (place * cores + core) * per_source
            for part in range(2):
                for index in range(frames_here):
                    source = (base + part * frames_here + index) * channels
                    target = (part * cores + core) * frames_here + index
                    lined[place, pl.ds(target, channels, stride=per_channel), :] = arrived[
                        pl.ds(source, channels), :
                    ].astype(jnp.float32)
    blank = jnp.zeros((spare, arrived.shape[1]), jnp.float32)
    for channel in range(channels):
        rows = slice(channel * per_channel, (channel + 1) * per_channel)
        blocks = [
            jnp.concatenate([lined[place, rows, :], blank], axis=0) for place in range(near)
        ]
        spectra[channel] = jnp.concatenate(blocks, axis=1).astype(jnp.bfloat16)


def beams_kernel(
    layout, which, step, pieces, skipped, base, first_ref, code_ref, pointing_ref, weights_ref, spectra_ref,
    *rest,
):
    _, cores, _, frames_here = layout
    per_channel = 2 * frames_here * cores
    raw = base is None
    if raw:
        out_ref, spectra_out_ref, *rest = rest
    else:
        out_ref, *rest = rest
    stored, own, total, code, spectra, extra_sems, sems, *rest = rest
    if raw:
        arrived, lined = rest
    channels, made_feeds, _ = stored.shape
    here = pl.ds(base or 0, channels)
    if raw:
        fetch = pltpu.make_async_copy(spectra_ref, arrived, extra_sems.at[0])
    else:
        fetch = pltpu.make_async_copy(spectra_ref.at[here], spectra, extra_sems.at[0])
    own_rows = own.shape[1]
    fetch_code = pltpu.make_async_copy(
        code_ref.at[pl.ds(made_feeds, own_rows)], code, extra_sems.at[1]
    )
    fetch_code.start()
    fetch.start()
    count = channels // pieces
    copies = []
    for piece in range(pieces):
        place = pl.ds(piece * count, count)
        there = pl.ds((base or 0) + piece * count, count)
        source = weights_ref.at[there, pl.ds(skipped, made_feeds)]
        copies.append(pltpu.make_async_copy(source, stored.at[place], sems.at[piece]))
    ahead = min(5, pieces)
    soon = ahead if raw else 3
    for copy in copies[:soon]:
        copy.start()

    block_rows = 32
    first = chain_start(first_ref[0] + step * (base or 0), channels, step)

    def one_block(index, carry):
        target = pl.ds(pl.multiple_of(index * block_rows, block_rows), block_rows)
        chain_of_weights(first, step, code[target], pointing_ref.at[which], own, target)
        return carry

    fetch_code.wait()
    lax.fori_loop(0, own_rows // block_rows, one_block, 0)
    fetch.wait()
    for copy in copies[soon:ahead]:
        copy.start()
    if raw:
        line_up(layout, arrived, lined, spectra)
        keep = pltpu.make_async_copy(spectra, spectra_out_ref, extra_sems.at[2])
        keep.start()

    for channel in range(channels):
        rows = slice(channel * per_channel, (channel + 1) * per_channel)
        total[rows, :] = jnp.dot(
            spectra[channel, :, made_feeds:], own[channel], preferred_element_type=jnp.float32
        )[:per_channel]
    for piece in range(pieces):
        copies[piece].wait()
        if piece + ahead < pieces:
            copies[piece + ahead].start()
        for channel in range(piece * count, (piece + 1) * count):
            rows = slice(channel * per_channel, (channel + 1) * per_channel)
            both = jnp.dot(
                spectra[channel, :, :made_feeds],
                stored[channel],
                preferred_element_type=jnp.float32,
            )[:per_channel]
            out_ref[rows, :] = turn_products(total[rows, :] + both).astype(out_ref.dtype)
    if raw:
        keep.wait()


def partial_beams(
    first, code, pointing, weights, made, spectra, layout, which, channels, base, step, dtype
):
    near, cores, all_channels, frames_here = layout
    feeds = code.shape[0]
    made_feeds = made[which]
    width = weights.shape[2]
    per_channel = 2 * cores * frames_here
    pieces = channels // 4
    raw = base is None
    lined_channels = all_channels if raw else channels
    in_vmem = pl.BlockSpec(memory_space=pltpu.VMEM)
    lined_shape = (lined_channels, padded_rows(per_channel), feeds)
    out_shape = [jax.ShapeDtypeStruct((channels * per_channel, width // 2), dtype)]
    scratch = [
        pltpu.VMEM((channels, made_feeds, width), weights.dtype),
        pltpu.VMEM((channels, feeds - made_feeds, width), weights.dtype),
        pltpu.VMEM((channels * per_channel, width), jnp.float32),
        pltpu.VMEM((feeds - made_feeds, LANES), code.dtype),
        pltpu.VMEM(lined_shape, jnp.bfloat16),
        pltpu.SemaphoreType.DMA((3,)),
        pltpu.SemaphoreType.DMA((pieces,)),
    ]
    if raw:
        out_shape.append(jax.ShapeDtypeStruct(lined_shape, jnp.bfloat16))
        scratch += [
            pltpu.VMEM(spectra.shape, spectra.dtype),
            pltpu.VMEM((near, all_channels * per_channel, feeds // near), jnp.float32),
        ]
    return pl.pallas_call(
        functools.partial(beams_kernel, layout, which, step, pieces, sum(made[:which]), base),
        in_specs=[
            pl.BlockSpec(memory_space=pltpu.SMEM),
            pl.BlockSpec(memory_space=pltpu.HBM),
            in_vmem,
            pl.BlockSpec(memory_space=pltpu.HBM),
            pl.BlockSpec(memory_space=pl.ANY if raw else pltpu.HBM),
        ],
        out_specs=[in_vmem, pl.BlockSpec(memory_space=pltpu.HBM)][: len(out_shape)],
        out_shape=out_shape,
        scratch_shapes=scratch,
        compiler_params=pltpu.CompilerParams(vmem_limit_bytes=50 * 1024 * 1024),
        cost_estimate=pl.CostEstimate(
            flops=(1 - which) * channels * feeds * width * 2 * 128 + 1,
            bytes_accessed=(1 - which) * channels * feeds * width * 2 + 1,
            transcendentals=0,
        ),
        name="beams",
    )(first, code, pointing, weights, spectra)


def gather_kernel(
    layout, beams_here, scale, own_ref, early_ref, late_ref, out_ref, own, other, total, rows, sems
):
    near, cores, channels, frames_here = layout
    lane_channels = LANES // beams_here
    per_core = 2 * frames_here
    per_channel = per_core * cores
    groups = channels // lane_channels
    fetches = [
        pltpu.make_async_copy(own_ref, own, sems.at[0]),
        pltpu.make_async_copy(early_ref, other.at[pl.ds(0, early_ref.shape[0])], sems.at[1]),
        pltpu.make_async_copy(
            late_ref, other.at[pl.ds(early_ref.shape[0], late_ref.shape[0])], sems.at[2]
        ),
    ]
    for fetch in fetches:
        fetch.start()
    for fetch in fetches:
        fetch.wait()
    total[...] = (own[...] + other[...].astype(jnp.float32)) * scale
    for group in range(groups):
        values = [
            total[pl.ds((group * lane_channels + sub) * per_channel, per_channel), :]
            for sub in range(lane_channels)
        ]
        for place in range(near):
            lanes = slice(place * beams_here, (place + 1) * beams_here)
            tile = jnp.concatenate([value[:, lanes] for value in values], axis=1)
            for core in range(cores):
                start = ((place * cores + core) * groups + group) * per_core
                for part in range(2):
                    source = (part * cores + core) * frames_here
                    rows[pl.ds(start + part * frames_here, frames_here), :] = tile[
                        source : source + frames_here
                    ]
    out_ref[...] = rows[...].astype(jnp.bfloat16)


def gather_beams(own, early, late, layout, beams_here, scale):
    near, cores, channels, frames_here = layout
    total_rows = near * cores * channels // (LANES // beams_here) * 2 * frames_here
    return pl.pallas_call(
        functools.partial(gather_kernel, layout, beams_here, scale),
        in_specs=[pl.BlockSpec(memory_space=pltpu.HBM)] + [pl.BlockSpec(memory_space=pl.ANY)] * 2,
        out_shape=jax.ShapeDtypeStruct((total_rows, LANES), jnp.bfloat16),
        scratch_shapes=[
            pltpu.VMEM(own.shape, own.dtype),
            pltpu.VMEM(own.shape, early.dtype),
            pltpu.VMEM(own.shape, jnp.float32),
            pltpu.VMEM((total_rows, LANES), jnp.float32),
            pltpu.SemaphoreType.DMA((3,)),
        ],
        compiler_params=pltpu.CompilerParams(vmem_limit_bytes=16 * 1024 * 1024),
        name="gather",
    )(own, early, late)


def series_kernel(
    beams_here, half_ref, received_ref, cos_ref, sin_ref, basis_ref, out_ref,
    arrived, basis, wide, lined, sems,
):
    frames_here = out_ref.shape[0]
    kappas = cos_ref.shape[0]
    lane_channels = LANES // beams_here
    side = kappas // 2
    half = half_ref[0]
    sign = (1 - 2 * half).astype(jnp.float32)
    fetch = pltpu.make_async_copy(received_ref, arrived, sems.at[2])
    fetch.start()
    fetch_basis = [
        pltpu.make_async_copy(
            basis_ref.at[parity + half * (1 - 2 * parity)], basis.at[parity], sems.at[parity]
        )
        for parity in range(2)
    ]
    for copy in fetch_basis:
        copy.start()
    fetch.wait()
    wide[...] = arrived[...].astype(jnp.float32)
    for index in range(frames_here):
        real = wide[pl.ds(index, kappas, stride=2 * frames_here), :]
        imag = wide[pl.ds(frames_here + index, kappas, stride=2 * frames_here), :]
        chirped_real = real * cos_ref[...] - imag * sin_ref[...]
        chirped_imag = real * sin_ref[...] + imag * cos_ref[...]
        target = slice(index * beams_here, (index + 1) * beams_here)
        for parity in range(2):
            where = slice(parity * side, (parity + 1) * side)
            both = jnp.concatenate([chirped_real[where], chirped_imag[where]], axis=0)
            turned = both.T
            high = turned.astype(jnp.bfloat16)
            low = (turned - high.astype(jnp.float32)).astype(jnp.bfloat16)
            for sub in range(lane_channels):
                source = slice(sub * beams_here, (sub + 1) * beams_here)
                lanes = slice(sub * 2 * side, (sub + 1) * 2 * side)
                lined[parity, 0, target, lanes] = high[source]
                lined[parity, 1, target, lanes] = low[source]
    sides = []
    for parity in range(2):
        high = lined[parity, 0]
        low = lined[parity, 1]
        fetch_basis[parity].wait()
        sides.append(
            jnp.dot(high, basis[parity, 0], preferred_element_type=jnp.float32)
            + jnp.dot(low, basis[parity, 0], preferred_element_type=jnp.float32)
            + jnp.dot(high, basis[parity, 1], preferred_element_type=jnp.float32)
        )
    times = sides[0].shape[1] // 2
    for part in range(2):
        even = sides[0][:, part * times : (part + 1) * times]
        odd = sides[1][:, part * times : (part + 1) * times]
        for which, value in enumerate((even + odd, (even - odd) * sign)):
            start = (2 * part + which) * times
            out_ref[:, :, start : start + times] = value.reshape(frames_here, beams_here, times)


def make_series(half_index, received, chirp_cos, chirp_sin, basis, beams_here, frames_here):
    in_vmem = pl.BlockSpec(memory_space=pltpu.VMEM)
    anywhere = pl.BlockSpec(memory_space=pl.ANY)
    series = pl.pallas_call(
        functools.partial(series_kernel, beams_here),
        in_specs=[
            pl.BlockSpec(memory_space=pltpu.SMEM), anywhere, in_vmem, in_vmem, anywhere,
        ],
        out_shape=jax.ShapeDtypeStruct(
            (frames_here, beams_here, 2 * basis.shape[3]), jnp.float32
        ),
        scratch_shapes=[
            pltpu.VMEM(received.shape, received.dtype),
            pltpu.VMEM(basis.shape, basis.dtype),
            pltpu.VMEM(received.shape, jnp.float32),
            pltpu.VMEM((2, 2, frames_here * beams_here, basis.shape[2]), jnp.bfloat16),
            pltpu.SemaphoreType.DMA((3,)),
        ],
        compiler_params=pltpu.CompilerParams(vmem_limit_bytes=24 * 1024 * 1024),
        name="series",
    )(half_index, received, chirp_cos, chirp_sin, basis)
    return jnp.transpose(series, (1, 0, 2))


def halves_body(samples, filter_taps, feed_cylinder, feed_delay, pointing, chirp_rate):
    length = filter_taps.shape[1]
    nchan = length // 2
    feed_here = samples.shape[0]
    frames_here = samples.shape[1] // length
    feeds = feed_delay.shape[0]
    beams = pointing.shape[0]
    beams_here = chirp_rate.shape[0]
    near = lax.axis_size("near")
    cores = lax.axis_size("tm")
    group = near * cores
    channels = nchan // group
    half_feeds = feeds // HALVES
    half_beams = beams // HALVES
    layout = (near, cores, channels, frames_here)
    half_index = lax.axis_index("half")
    place = lax.axis_index(GROUP)

    tail = from_behind(samples[:, (frames_here - (TAPS - 1)) * length :], "tm", 1)
    forward = jnp.asarray(folded_forward_basis(length))
    half_scalar = jnp.reshape(half_index, (1,)).astype(jnp.int32)
    taps = jnp.concatenate([filter_taps, filter_taps])
    spectra = spectra_rows(half_scalar, samples, tail, taps, forward, group)
    spectra = spectra.reshape(group, channels * 2 * frames_here, feed_here)
    received = lax.all_to_all(spectra, GROUP, 0, 0, tiled=True)
    received = received.reshape(-1, feed_here)

    in_parity = group // 2
    first = 2 * (place % in_parity) * channels + (place // in_parity ^ half_index) + 1
    first = jnp.reshape(first, (1,)).astype(jnp.int32)
    code = feed_cylinder * PHASES + feed_delay
    code = lax.dynamic_slice_in_dim(code, half_index * half_feeds, half_feeds)
    code = jnp.broadcast_to(code[:, None], (half_feeds, LANES))
    aim = jnp.transpose(pointing).astype(jnp.float32)
    aims = jnp.stack(
        [
            lax.dynamic_slice_in_dim(aim, half * half_beams, half_beams, 1)
            for half in (1 - half_index, half_index)
        ]
    )
    step = 2
    made = (half_feeds * 3 // 4, half_feeds * 3 // 4)
    weights = make_weights(first, code, aims, channels, step, made)
    swap = [
        (half * near + i, (1 - half) * near + (i + near // 2) % near)
        for half in range(HALVES)
        for i in range(near)
    ]
    common = (first, code, aims, weights, made)
    piece = channels * 5 // 8
    early, lined = partial_beams(
        *common, received, layout, 0, piece, None, step, jnp.bfloat16
    )
    early = lax.ppermute(early, ("half", "near"), swap)
    (late,) = partial_beams(
        *common, lined, layout, 0, channels - piece, piece, step, jnp.bfloat16
    )
    late = lax.ppermute(late, ("half", "near"), swap)
    (own,) = partial_beams(*common, lined, layout, 1, channels, 0, step, jnp.float32)
    gathered = gather_beams(own, early, late, layout, beams_here, 1.0 / math.sqrt(feeds))
    lane_channels = LANES // beams_here
    gathered = gathered.reshape(group, -1, LANES)
    returned = lax.all_to_all(gathered, GROUP, 0, 0, tiled=True).reshape(-1, LANES)

    kappa = jnp.arange(nchan // lane_channels, dtype=jnp.int32)[:, None]
    sub = jnp.arange(LANES, dtype=jnp.int32)[None, :] // beams_here
    side = nchan // lane_channels // 2
    channel = 2 * (lane_channels * (kappa % side) + sub) + (kappa // side ^ half_index)
    position = channel.astype(jnp.float32) / nchan
    rate = jnp.tile(jnp.pi * chirp_rate, lane_channels)[None, :]
    chirp = rate * (position * position)
    inverse = jnp.asarray(folded_inverse_basis(nchan, lane_channels))
    return make_series(
        half_scalar, returned, jnp.cos(chirp), jnp.sin(chirp), inverse, beams_here, frames_here
    )


def solution(mesh):
    feed_size = mesh.shape["feed"]
    wide_enough = FEEDS // feed_size % LANES == 0 and BEAMS // feed_size * 4 == LANES
    if not wide_enough:
        return jax.shard_map(
            plain_body,
            mesh=mesh,
            in_specs=(P("feed", "tm"), P(), P(), P(), P(), P("feed")),
            out_specs=P("feed", "tm", None),
            check_vma=False,
        )
    devices = mesh.devices.reshape(HALVES, feed_size // HALVES, mesh.shape["tm"])
    halved = jax.sharding.Mesh(devices, ("half", "near", "tm"))
    feed = ("half", "near")
    return jax.shard_map(
        halves_body,
        mesh=halved,
        in_specs=(P(feed, "tm"), P(), P(), P(), P(), P(feed)),
        out_specs=P(feed, "tm", None),
        check_vma=False,
    )
```
